32 devices in a mesh: ctx: 4 (over y, x), exp: 8 (over z, core).
Axes of the slice: x: 2, y: 2, z: 4, core: 2. Of those that a mesh axis runs over, the one named last changes fastest.
Arguments:
- queries: bfloat16 [4, 256, 6144], P(None, 'ctx', 'exp'), may hold values from -6 to 6
- keys: bfloat16 [4, 256, 6144], P(None, 'ctx', 'exp'), may hold values from -6 to 6
- values: bfloat16 [4, 256, 6144], P(None, 'ctx', 'exp'), may hold values from -6 to 6
- log_decay: float32 [4, 256, 48], P(None, 'ctx', 'exp'), may hold values from -1 to 0
- norm_gain: float32 [6144], P('exp'), may hold values from 0.1 to 1.9
- router: bfloat16 [6144, 16], replicated, may hold values from -0.078125 to 0.078125
- expert_up: bfloat16 [16, 6144, 6144], P('exp', None, 'ctx'), may hold values from -0.078125 to 0.078125
- expert_down: bfloat16 [16, 6144, 6144], P('exp', 'ctx'), may hold values from -0.078125 to 0.078125
- expert_ids: int32 [256, 4, 2], P('ctx'), may hold values from 0 to 15, all different within a row; in each aligned block of 256 rows (0 to 255, 256 to 511, ..., all dimensions but the last counted through in order) at most 40 rows name the same one
Outputs:
- layer_out: bfloat16 [4, 256, 6144], P(None, 'ctx', 'exp')
The draws below stay inside these ranges and needn't reach their ends.
Inputs may be any that keep to these rules, and one draw needn't show every extreme that they name: `expert_ids`: within each block of 256 rows (the positions of one group for all requests), no expert is named more than 40 times; the two ids of a row differ.
All inputs are finite; a program needn't handle non-finite values.
Results may differ from the reference program's by a relative error of at most 0.012.
Values may be sent and summed in bfloat16 or wider, within the bound.
No kernel may reach another device: no remote copies, remote signals or barrier semaphores. Data moves between devices by JAX's collectives and lax.ppermute only.
A program may use at most 128 MiB of HBM per device.

```python
import math
import jax
import jax.numpy as jnp
import numpy as np
from jax import lax

HEAD_TOTAL = 48
DH = 128
D = 6144
FF = 6144
EXPERTS = 16
REQUEST_TOTAL = 4
CH = 64
POSITION_TOTAL = 256
CAP = 40
N_CTX = 4


def draw_log_decay(key, part):
    random_subkeys = jax.random.split(key, 7)
    fast_share = 0.5
    fast_heads = jax.random.uniform(random_subkeys[0], (1, 1, HEAD_TOTAL)) < fast_share
    slow_rate = jnp.exp(jax.random.uniform(random_subkeys[1], (1, 1, HEAD_TOTAL), minval=math.log(0.2), maxval=math.log(1.0))) / POSITION_TOTAL
    fast_rate = jnp.exp(jax.random.uniform(random_subkeys[2], (1, 1, HEAD_TOTAL), minval=math.log(1.0 / 50.0), maxval=math.log(1.0 / 30.0)))
    decay_speed = jnp.where(fast_heads, fast_rate, slow_rate)
    jaggedness = jnp.exp(jax.random.uniform(random_subkeys[3], (REQUEST_TOTAL, POSITION_TOTAL, HEAD_TOTAL), minval=math.log(0.5), maxval=math.log(2.0)))
    dilation_factor = jnp.exp(jax.random.uniform(random_subkeys[4], (REQUEST_TOTAL, POSITION_TOTAL // CH, 1, HEAD_TOTAL), minval=math.log(0.6), maxval=math.log(1.6)))
    dilation_factor = jnp.broadcast_to(dilation_factor, (REQUEST_TOTAL, POSITION_TOTAL // CH, CH, HEAD_TOTAL)).reshape(REQUEST_TOTAL, POSITION_TOTAL, HEAD_TOTAL)
    spike_events = jax.random.uniform(random_subkeys[5], (REQUEST_TOTAL, POSITION_TOTAL, HEAD_TOTAL)) < 3.0 / POSITION_TOTAL
    loss_values = jnp.log(jax.random.uniform(random_subkeys[6], (REQUEST_TOTAL, POSITION_TOTAL, HEAD_TOTAL), minval=0.5, maxval=0.8))
    return (-decay_speed * jaggedness * dilation_factor + jnp.where(spike_events, loss_values, 0.0)).astype(jnp.float32)


def level_of(key, shape, shards, low, top_value):
    factor_of = 1.0
    for dim, shards_of in shards:
        steps = jax.random.uniform(jax.random.fold_in(jax.random.fold_in(key, 6), dim), (shards_of,), jnp.float32, low / len(shards), top_value / len(shards))
        factor_of = factor_of * jnp.repeat(jnp.exp(steps), shape[dim] // shards_of).reshape((-1,) + (1,) * (len(shape) - 1 - dim))
    return factor_of


def routed_block(stream_key, own, number, rows, count, top, bound, slope):
    order = jax.random.permutation(stream_key, count)
    crowded, ordinary = load_shares(count, rows * top, bound, slope, True), load_shares(count, rows * top, bound, slope, False)
    places = jnp.arange(count)

    def named(sizes, rotation):
        used = int((sizes > 0).sum())
        fixed = max(1, used // 4)
        moved = fixed + (places - fixed + rotation * (used - fixed)) % max(1, count - fixed)
        return jnp.zeros((count,), jnp.int32).at[order[jnp.where(places < fixed, places, moved)]].set(jnp.asarray(sizes, jnp.int32))

    sizes = jnp.where(number % 4 == 0, named(crowded, number // 4), named(ordinary, number - number // 4 - 1))
    mixed = jax.random.permutation(jax.random.fold_in(own, 3), count)
    source_of, taker = mixed[0:count // 2 * 2:2], mixed[1:count // 2 * 2:2]
    room = jnp.minimum(sizes[source_of] - 1, bound - sizes[taker]) // 2
    room = jnp.where((source_of == order[0]) | (taker == order[0]) | (sizes[taker] == 0), 0, jnp.maximum(room, 0))
    moved = jax.random.randint(jax.random.fold_in(own, 4), (count // 2,), 0, 1 << 20) % (room + 1)
    sizes = sizes.at[source_of].add(-moved).at[taker].add(moved)
    members = jnp.searchsorted(jnp.cumsum(sizes), jnp.arange(rows * top), side="right").astype(jnp.int32)
    grid = members.reshape(top, rows).T
    grid = grid[jax.random.permutation(jax.random.fold_in(own, 1), rows)]
    rotation = jax.random.randint(jax.random.fold_in(own, 2), (rows, 1), 0, top)
    return jnp.take_along_axis(grid, (jnp.arange(top)[None, :] + rotation) % top, axis=1)


def load_shares(count, total, limit, skew, full):
    portions = [(1 << 20) // math.isqrt(grade ** skew) + 1 for grade in range(1, count + 1)]
    largest = limit if full else min(limit, max(-(-total // count), total * portions[0] // sum(portions)))
    least = 1 if total - largest >= count - 1 else 0
    given, spare = [largest] + [least] * (count - 1), total - largest - least * (count - 1)
    while spare > 0:
        candidates = [i for i in range(1, count) if given[i] < largest] or [i for i in range(1, count) if given[i] < limit]
        mass, remaining = sum([portions[i] for i in candidates]), spare
        for i in candidates:
            extra = min(limit - given[i], max(1, remaining * portions[i] // mass), spare)
            given[i] = given[i] + extra
            spare = spare - extra
    return np.array(given)


def scatter_about(rng, shape, scale, reach, shards=(), kind=jnp.bfloat16):
    factor_of = level_of(rng, shape, shards, -0.22, 0.18) if shards else 1.0
    array = jax.random.normal(rng, shape, jnp.float32) * scale * factor_of
    return jnp.minimum(jnp.maximum(array, -reach), reach).astype(kind)


def setup_inputs(seed: int = 0) -> dict:
    splits = jax.random.split(jax.random.key(seed), 10)
    queries = scatter_about(splits[0], (REQUEST_TOTAL, POSITION_TOTAL, D), 1.0, 6.0, ((1, 4), (2, 8)))
    keys = scatter_about(splits[1], (REQUEST_TOTAL, POSITION_TOTAL, D), 1.0, 6.0, ((1, 4), (2, 8)))
    values = scatter_about(splits[2], (REQUEST_TOTAL, POSITION_TOTAL, D), 1.0, 6.0, ((1, 4), (2, 8)))
    log_decay = draw_log_decay(jax.random.fold_in(splits[9], 71), 0)
    norm_gain = jnp.clip(1.0 + 0.18 * jax.random.normal(splits[4], (D,), jnp.float32), 0.1, 1.9)
    router = scatter_about(splits[5], (D, EXPERTS), D ** -0.5, 0.078125)
    expert_up = scatter_about(splits[6], (EXPERTS, D, FF), D ** -0.5, 0.078125, ((0, 8), (2, 4)))
    expert_down = scatter_about(splits[7], (EXPERTS, FF, D), FF ** -0.5, 0.078125, ((0, 8), (1, 4)))
    expert_ids_keys = jax.random.split(jax.random.fold_in(splits[8], 1), POSITION_TOTAL * REQUEST_TOTAL // (CH * REQUEST_TOTAL))
    expert_ids_turns = jax.random.permutation(jax.random.fold_in(splits[8], 3), POSITION_TOTAL * REQUEST_TOTAL // (CH * REQUEST_TOTAL))
    expert_ids = jax.vmap(lambda own, number: routed_block(jax.random.fold_in(splits[8], 2), own, number, CH * REQUEST_TOTAL, EXPERTS, 2, CAP, 2))(expert_ids_keys, expert_ids_turns).reshape((POSITION_TOTAL, REQUEST_TOTAL, 2))
    return dict(queries=queries, keys=keys, values=values, log_decay=log_decay, norm_gain=norm_gain, router=router, expert_up=expert_up, expert_down=expert_down, expert_ids=expert_ids)


def attention_part(queries, keys, values, log_decay, norm_gain):
    shape5 = (REQUEST_TOTAL, N_CTX, CH, HEAD_TOTAL, DH)
    query5 = queries.astype(jnp.float32).reshape(shape5)
    key5 = keys.astype(jnp.float32).reshape(shape5)
    value5 = values.astype(jnp.float32).reshape(shape5)
    cumulative = jnp.cumsum(log_decay.reshape(REQUEST_TOTAL, N_CTX, CH, HEAD_TOTAL), axis=2)
    cum_first = jnp.moveaxis(cumulative, 3, 2)
    spread = cum_first[..., :, None] - cum_first[..., None, :]
    causal = jnp.tril(jnp.ones((CH, CH), dtype=bool))
    decay_mask = jnp.where(causal, jnp.exp(jnp.minimum(spread, 0.0)), 0.0)
    scores = jnp.einsum('rbthd,rbshd->rbhts', query5, key5)
    weights = (scores * decay_mask).astype(jnp.bfloat16)
    weights = lax.optimization_barrier(weights).astype(jnp.float32)
    inside = jnp.einsum('rbhts,rbshd->rbthd', weights, value5)
    last_cum = cumulative[:, :, -1, :]
    key_decay = key5 * jnp.exp(last_cum[:, :, None, :] - cumulative)[..., None]
    local_state = jnp.einsum('rbshd,rbshe->rbhde', key_decay, value5, precision=lax.Precision.HIGHEST)
    block_decay = jnp.exp(last_cum)

    def advance(running, step_input):
        decay_now, state_now = step_input
        return (decay_now[..., None, None] * running + state_now, running)
    start_state = jnp.zeros((REQUEST_TOTAL, HEAD_TOTAL, DH, DH), jnp.float32)
    _, incoming = lax.scan(advance, start_state, (jnp.moveaxis(block_decay, 1, 0), jnp.moveaxis(local_state, 1, 0)))
    incoming = jnp.moveaxis(incoming, 0, 1)
    carried = jnp.einsum('rbthd,rbhde->rbthe', query5, incoming, precision=lax.Precision.HIGHEST)
    output = inside + jnp.exp(cumulative)[..., None] * carried
    mean_square = lax.optimization_barrier(jnp.mean(output * output, axis=-1, keepdims=True)) + 1e-05
    normed = (output * lax.rsqrt(mean_square)).reshape(REQUEST_TOTAL, POSITION_TOTAL, D) * norm_gain
    return normed.astype(jnp.bfloat16)

def reference(queries, keys, values, log_decay, norm_gain, router, expert_up, expert_down, expert_ids):
    normed = attention_part(queries, keys, values, log_decay, norm_gain)
    block_rows = jnp.transpose(normed.reshape(REQUEST_TOTAL, N_CTX, CH, D), (1, 2, 0, 3)).reshape(N_CTX, CH * REQUEST_TOTAL, D)
    block_ids = expert_ids.reshape(N_CTX, CH * REQUEST_TOTAL, 2)
    own_hot = jnp.eye(EXPERTS, dtype=jnp.float32)

    def moe_block(step_input):
        token_rows, id_rows = step_input
        choice_hot = (id_rows[..., None] == jnp.arange(EXPERTS)).astype(jnp.int32)
        flat_hot = choice_hot.reshape(-1, EXPERTS)
        before = jnp.cumsum(flat_hot, axis=0) - flat_hot
        slot_index = lax.optimization_barrier(jnp.sum(before * flat_hot, axis=1)).reshape(-1, 2)
        slot_hot = (slot_index[..., None] == jnp.arange(CAP)).astype(jnp.float32)
        choice_float = choice_hot.astype(jnp.float32)
        placement = jnp.einsum('tje,tjc->cet', choice_float, slot_hot)
        partner = jnp.einsum('tje,tjc,tjx->cex', choice_float, slot_hot, choice_float[:, ::-1, :])
        routed = jnp.einsum('cet,td->ced', placement, token_rows.astype(jnp.float32)).astype(jnp.bfloat16)
        logits = jnp.einsum('ced,dx->cex', routed.astype(jnp.float32), router.astype(jnp.float32))
        self_logit = lax.optimization_barrier(jnp.sum(logits * own_hot[None], axis=-1))
        other_logit = lax.optimization_barrier(jnp.sum(logits * partner, axis=-1))
        gate_weight = jax.nn.sigmoid(self_logit - other_logit)

        def one_expert(expert_index):
            expert_rows = lax.dynamic_index_in_dim(routed, expert_index, 1, keepdims=False)
            hidden = jax.nn.silu(jnp.dot(expert_rows, expert_up[expert_index], preferred_element_type=jnp.float32)).astype(jnp.bfloat16)
            return jnp.dot(hidden, expert_down[expert_index], preferred_element_type=jnp.float32)
        outputs = jnp.moveaxis(lax.map(one_expert, jnp.arange(EXPERTS)), 0, 1)
        replies = (gate_weight[..., None] * outputs).astype(jnp.bfloat16)
        combined = jnp.einsum('cet,ced->td', placement, replies.astype(jnp.float32))
        return (token_rows.astype(jnp.float32) + combined).astype(jnp.bfloat16)
    mixed = lax.map(moe_block, (block_rows, block_ids))
    return jnp.transpose(mixed.reshape(N_CTX, CH, REQUEST_TOTAL, D), (2, 0, 1, 3)).reshape(REQUEST_TOTAL, POSITION_TOTAL, D)
```

```python
import functools

import jax
import jax.numpy as jnp
from jax import lax
from jax.experimental import pallas as pl
from jax.experimental.pallas import tpu as pltpu
from jax.sharding import PartitionSpec as P

CAP = 40
F32 = jnp.float32
BF16 = jnp.bfloat16
VMEM = pl.BlockSpec(memory_space=pltpu.VMEM)
SMEM = pl.BlockSpec(memory_space=pltpu.SMEM)


def params(mib, n=0):
    return pltpu.CompilerParams(
        vmem_limit_bytes=mib << 20, dimension_semantics=("arbitrary",) * n if n else None
    )


def bits_of(n):
    return [1 << b for b in range(n.bit_length() - 1)]


def swap(x, axis, n, k, keep=lambda i: True):
    return lax.ppermute(x, axis, [(i, i ^ k) for i in range(n) if keep(i)])


def dot(a, b, ca=1, cb=0, **kw):
    return lax.dot_general(a, b, (((ca,), (cb,)), ((), ())), preferred_element_type=F32, **kw)


def iota(shape, dim):
    return lax.broadcasted_iota(jnp.int32, shape, dim)


def running_sum(log_decay):
    length = log_decay.shape[0]
    tril = (iota((length, length), 0) >= iota((length, length), 1)).astype(F32)
    return dot(tril, log_decay, precision=lax.Precision.HIGHEST)


def running_sum_rows(log_decay):
    length = log_decay.shape[0]
    triu = (iota((length, length), 0) <= iota((length, length), 1)).astype(F32)
    return dot(log_decay, triu, 0, 0, precision=lax.Precision.HIGHEST)


def state_kernel(keys, values, log_decay, *states):
    requests, length, features = keys.shape
    heads = log_decay.shape[2]
    dim = features // heads
    per = requests // len(states)
    for r in range(requests):
        cum = running_sum(log_decay[r])
        fade = jnp.exp(cum[length - 1 : length, :] - cum)
        for h in range(heads):
            lanes = slice(h * dim, (h + 1) * dim)
            faded = (keys[r, :, lanes].astype(F32) * fade[:, h : h + 1]).astype(BF16)
            states[r // per][(r % per) * heads + h] = dot(faded, values[r, :, lanes], 0, 0).astype(BF16)


def inside_kernel(place, queries, keys, values, log_decay, ids, inside, placement, other):
    requests, length, features = keys.shape
    heads = log_decay.shape[2]
    dim = features // heads
    causal = iota((length, length), 0) >= iota((length, length), 1)
    for r in range(requests):
        cum = running_sum(log_decay[r])
        rows = running_sum_rows(log_decay[r])
        for h in range(heads):
            lanes = slice(h * dim, (h + 1) * dim)
            spread = cum[:, h : h + 1] - rows[h : h + 1, :]
            mask = jnp.where(causal, jnp.exp(jnp.minimum(spread, 0.0)), 0.0)
            scores = dot(queries[r, :, lanes], keys[r, :, lanes], 1, 1)
            inside[r, :, lanes] = dot((scores * mask).astype(BF16), values[r, :, lanes])
    slots, tokens = placement.shape
    experts = slots // CAP
    own = other.shape[0] // CAP
    owner = place[1]
    expert_row = iota((experts, tokens), 0)
    relative = sum((expert_row >= own * k).astype(jnp.int32) for k in range(1, experts // own))
    expert = (relative ^ owner) * own + (expert_row - relative * own)
    first, second = ids[0:1, :], ids[1:2, :]
    named = (first == expert) | (second == expert)
    row = iota((tokens, tokens), 0)
    col = iota((tokens, tokens), 1)

    def order(i):
        request = sum((i >= length * k).astype(jnp.int32) for k in range(1, requests))
        return (i - request * length) * requests + request

    earlier = (order(row) < order(col)).astype(BF16)
    before = dot(named.astype(BF16), earlier)
    code = jnp.where(named, before, -1.0).astype(BF16)
    slot_row = iota((slots, experts), 0)
    slot_expert = iota((slots, experts), 1)
    spread_rows = (slot_row >= slot_expert * CAP) & (slot_row < slot_expert * CAP + CAP)
    codes = dot(spread_rows.astype(BF16), code)
    row_of = iota((slots, tokens), 0)
    expert_of = ((row_of.astype(F32) + 0.5) * (1.0 / CAP)).astype(jnp.int32)
    taken = codes == (row_of - expert_of * CAP).astype(F32)
    placement[...] = taken.astype(BF16)
    both = (first + second).astype(F32)
    mine = jnp.sum(jnp.where(taken[: own * CAP], both, 0.0), axis=1, keepdims=True)
    me = owner * own + expert_of[: own * CAP, :1]
    other[...] = jnp.broadcast_to(mine.astype(jnp.int32) - me, other.shape)


def output_kernel(queries, inside, log_decay, gain, placement, *refs, halves):
    incoming, normed, blocks = refs[:halves], refs[halves], refs[halves + 1 : -1]
    rows = refs[-1]
    requests, length, features = queries.shape
    heads = log_decay.shape[2]
    dim = features // heads
    per = requests // halves
    for r in range(requests):
        grow = jnp.exp(running_sum(log_decay[r]))
        for h in range(heads):
            lanes = slice(h * dim, (h + 1) * dim)
            carried = dot(queries[r, :, lanes], incoming[r // per][(r % per) * heads + h])
            out = inside[r, :, lanes] + grow[:, h : h + 1] * carried
            square = jnp.mean(out * out, axis=1, keepdims=True) + 1e-05
            value = (out * lax.rsqrt(square) * gain[0:1, lanes]).astype(BF16)
            normed[r, :, lanes] = value
            rows[r * length : (r + 1) * length, lanes] = value
    routed = dot(placement[...], rows[...])
    own = blocks[0].shape[0]
    for k, block in enumerate(blocks):
        for j in range(own):
            at = (k * own + j) * CAP
            block[j] = routed[at : at + CAP].astype(BF16)


def stack_rows(refs, j):
    return jnp.concatenate([ref[j].astype(F32) for ref in refs], axis=0).astype(BF16)


def gate_kernel(place, other, router, *refs):
    blocks, weight = refs[:-1], refs[-1]
    own, cap, width = blocks[0].shape
    owner = place[1]
    experts = router.shape[1]
    for j in range(own):
        logits = jnp.zeros((cap, experts), F32)
        for k, block in enumerate(blocks):
            at = pl.multiple_of((owner ^ k) * width, width)
            logits = logits + dot(block[j], router[pl.ds(at, width), :])
        col = iota((cap, experts), 1)
        mine = jnp.sum(jnp.where(col == owner * own + j, logits, 0.0), axis=1, keepdims=True)
        theirs_at = other[j * cap : (j + 1) * cap, :1]
        theirs = jnp.sum(jnp.where(col == theirs_at, logits, 0.0), axis=1, keepdims=True)
        weight[j] = jnp.broadcast_to(1.0 / (1.0 + jnp.exp(theirs - mine)), (cap, 128))


def up_kernel(place, *refs, parts, first, last):
    blocks = refs[: 2 * parts]
    left, right = refs[2 * parts], refs[2 * parts + 1]
    out = refs[-1]
    j = pl.program_id(0)
    total = dot(stack_rows(blocks[:parts], j), left[0]) + dot(stack_rows(blocks[parts:], j), right[0])
    if not first:
        total = total + refs[-2][0]
    out[0] = (total / (1.0 + jnp.exp(-total))).astype(BF16) if last else total


def up_chunk(place, chunk, left, right, weights, total, last):
    own, depth, hidden = weights.shape
    cap, width = left[0].shape[1:]
    parts = len(left)
    rows = parts * cap
    tile = hidden // 2 if hidden % 256 == 0 else hidden
    first = total is None

    def weight_spec(k):
        return pl.BlockSpec((1, width, tile), lambda j, n, at: (j, at[1] ^ k, n))

    total_spec = pl.BlockSpec((1, rows, tile), lambda j, n, at: (j, 0, n))
    return pl.pallas_call(
        functools.partial(up_kernel, parts=parts, first=first, last=last),
        grid_spec=pltpu.PrefetchScalarGridSpec(
            num_scalar_prefetch=1,
            grid=(own, hidden // tile),
            in_specs=[VMEM] * (2 * parts)
            + [weight_spec(2 * chunk), weight_spec(2 * chunk + 1)]
            + ([] if first else [total_spec]),
            out_specs=total_spec,
        ),
        out_shape=jax.ShapeDtypeStruct((own, rows, hidden), BF16 if last else F32),
        compiler_params=params(32, 2),
        cost_estimate=pl.CostEstimate(
            flops=4 * own * rows * width * hidden,
            bytes_accessed=4 * own * width * hidden,
            transcendentals=0,
        ),
        name=f"up_{chunk}",
    )(place, *left, *right, weights, weights, *([] if first else [total]))


def down_kernel(place, hidden, left, right, *outs, routes):
    for weights, sides, route in zip((left, right), (outs[:2], outs[2:]), routes):
        result = dot(hidden[0], weights[0])
        for out, members in zip(sides, route):
            for i, member in enumerate(members):
                out[i, 0] = result[member * CAP : (member + 1) * CAP].astype(BF16)


def down_chunk(place, chunk, hidden, weights, width, routes):
    own, rows, depth = hidden.shape
    parts = rows // CAP
    tile = width // 2 if width % 256 == 0 else width
    steps = width // tile

    def weight_spec(k):
        return pl.BlockSpec((1, depth, tile), lambda j, n, at: (j, 0, (at[1] ^ k) * steps + n))

    out_spec = pl.BlockSpec((parts // 2, 1, CAP, tile), lambda j, n, at: (0, j, 0, n))
    return pl.pallas_call(
        functools.partial(down_kernel, routes=routes),
        grid_spec=pltpu.PrefetchScalarGridSpec(
            num_scalar_prefetch=1,
            grid=(own, steps),
            in_specs=[
                pl.BlockSpec((1, rows, depth), lambda j, n, at: (j, 0, 0)),
                weight_spec(2 * chunk),
                weight_spec(2 * chunk + 1),
            ],
            out_specs=[out_spec] * 4,
        ),
        out_shape=[jax.ShapeDtypeStruct((parts // 2, own, CAP, width), BF16)] * 4,
        compiler_params=params(32, 2),
        cost_estimate=pl.CostEstimate(
            flops=4 * own * rows * width * depth,
            bytes_accessed=4 * own * width * depth,
            transcendentals=0,
        ),
        name=f"down_{chunk}",
    )(place, hidden, weights, weights)


def combine_kernel(normed, placement, *refs):
    blocks, out = refs[:-1], refs[-1]
    requests, length, _ = normed.shape
    own = blocks[0].shape[0]
    replies = jnp.concatenate(
        [block[j].astype(F32) for block in blocks for j in range(own)], axis=0
    ).astype(BF16)
    combined = dot(placement[...], replies, 0, 0)
    for r in range(requests):
        rows = slice(r * length, (r + 1) * length)
        out[r] = (normed[r].astype(F32) + combined[rows]).astype(BF16)


def gather_ctx(block, bits, n):
    have = {0: block}
    for bit in bits:
        have.update({rel | bit: swap(a, "ctx", n, bit) for rel, a in list(have.items())})
    return [have[rel] for rel in range(n)]


def route_of(bits, n):
    keep = [0]
    for bit in reversed(bits[1:]):
        keep = keep + [m | bit for m in keep]
    return [m | bits[0] for m in keep], keep


def reduce_ctx(sent, kept, bits, n):
    kept = kept.astype(F32)
    for step, bit in enumerate(bits):
        total = kept + swap(sent, "ctx", n, bit).astype(F32)
        if step + 1 < len(bits):
            half = total.shape[0] // 2
            kept, sent = total[:half], total[half:].astype(BF16)
    return total[0]


def body(n_ctx, n_exp, queries, keys, values, log_decay, norm_gain, router, expert_up, expert_down, expert_ids):
    requests, length, features = queries.shape
    heads = log_decay.shape[2]
    dim = features // heads
    experts = router.shape[1]
    own = expert_up.shape[0]
    tokens = requests * length
    halves = 2 if requests % 2 == 0 else 1
    pairs = requests * heads // halves
    me = lax.axis_index("ctx")
    place = jnp.stack([me, lax.axis_index("exp")]).astype(jnp.int32)
    struct = jax.ShapeDtypeStruct

    states = pl.pallas_call(
        state_kernel,
        in_specs=[VMEM] * 3,
        out_specs=[VMEM] * halves,
        out_shape=[struct((pairs, dim, dim), BF16)] * halves,
        compiler_params=params(32),
        name="local_state",
    )(keys, values, log_decay)

    block_decay = jnp.exp(jnp.sum(log_decay, axis=1)).reshape(halves, pairs, 1, 1)
    bits = bits_of(n_ctx)
    decay_total = block_decay
    decay_before = jnp.ones_like(block_decay)
    steps = []
    for bit in bits:
        upper = (me & bit) != 0
        partner_decay = swap(decay_total, "ctx", n_ctx, bit)
        steps.append((upper, decay_before, decay_total, partner_decay))
        decay_before = jnp.where(upper, decay_before * partner_decay, decay_before)
        decay_total = decay_total * partner_decay
    incoming = []
    for half in range(halves):
        total, before = states[half], jnp.zeros((), F32)
        for bit, (upper, d_before, d_total, d_partner) in zip(bits, steps):
            last = bit == bits[-1]
            partner = swap(total, "ctx", n_ctx, bit, lambda i: not last or not i & bit).astype(F32)
            before = before + jnp.where(upper, d_before[half], 0.0) * partner
            if not last:
                mine = total.astype(F32)
                total = (
                    jnp.where(upper, 1.0, d_partner[half]) * mine
                    + jnp.where(upper, d_total[half], 1.0) * partner
                ).astype(BF16)
        incoming.append(before.astype(BF16))

    ids = jnp.transpose(expert_ids, (2, 1, 0)).reshape(2, tokens)
    inside, placement, other = pl.pallas_call(
        inside_kernel,
        in_specs=[SMEM] + [VMEM] * 5,
        out_specs=[VMEM] * 3,
        out_shape=[
            struct((requests, length, features), F32),
            struct((experts * CAP, tokens), BF16),
            struct((own * CAP, 128), jnp.int32),
        ],
        compiler_params=params(32),
        name="inside_and_placement",
    )(place, queries, keys, values, log_decay, ids)

    normed, *outgoing = pl.pallas_call(
        functools.partial(output_kernel, halves=halves),
        in_specs=[VMEM] * (5 + halves),
        out_specs=[VMEM] * (1 + n_exp),
        out_shape=[struct((requests, length, features), BF16)]
        + [struct((own, CAP, features), BF16)] * n_exp,
        scratch_shapes=[pltpu.VMEM((tokens, features), BF16)],
        compiler_params=params(32),
        name="output_and_dispatch",
    )(queries, inside, log_decay, norm_gain.reshape(1, features), placement, *incoming)

    arrived = [outgoing[0]] + [swap(outgoing[k], "exp", n_exp, k) for k in range(1, n_exp)]
    weight = pl.pallas_call(
        gate_kernel,
        in_specs=[SMEM] + [VMEM] * (2 + n_exp),
        out_specs=VMEM,
        out_shape=struct((own, CAP, 128), F32),
        compiler_params=params(32),
        name="gate",
    )(place, other, router, *arrived)

    there, back = bits, bits[::-1]
    chunks = n_exp // 2
    total = None
    for chunk in range(chunks):
        left = gather_ctx(arrived[2 * chunk], there, n_ctx)
        right = gather_ctx(arrived[2 * chunk + 1], back, n_ctx)
        total = up_chunk(place, chunk, left, right, expert_up, total, chunk == chunks - 1)

    routes = (route_of(there, n_ctx), route_of(back, n_ctx))
    returned = [None] * n_exp
    for chunk in reversed(range(chunks)):
        outs = down_chunk(place, chunk, total, expert_down, features, routes)
        for side, order in enumerate((there, back)):
            k = 2 * chunk + side
            summed = reduce_ctx(outs[2 * side], outs[2 * side + 1], order, n_ctx)
            reply = (summed * weight[:, :, :1]).astype(BF16)
            returned[k] = swap(reply, "exp", n_exp, k) if k else reply

    return pl.pallas_call(
        combine_kernel,
        in_specs=[VMEM] * (2 + n_exp),
        out_specs=VMEM,
        out_shape=struct((requests, length, features), BF16),
        compiler_params=params(32),
        name="combine",
    )(normed, placement, *returned)


def solution(mesh):
    in_specs = (
        P(None, "ctx", "exp"),
        P(None, "ctx", "exp"),
        P(None, "ctx", "exp"),
        P(None, "ctx", "exp"),
        P("exp"),
        P(),
        P("exp", None, "ctx"),
        P("exp", "ctx", None),
        P("ctx", None, None),
    )
    out_specs = P(None, "ctx", "exp")
    run = functools.partial(body, mesh.shape["ctx"], mesh.shape["exp"])
    return jax.shard_map(run, mesh=mesh, in_specs=in_specs, out_specs=out_specs, check_vma=False)
```

```python
import functools

import jax
import jax.numpy as jnp
from jax import lax
from jax.experimental import pallas as pl
from jax.experimental.pallas import tpu as pltpu
from jax.sharding import PartitionSpec as P

CAP = 40
F32 = jnp.float32
BF16 = jnp.bfloat16
VMEM = pl.BlockSpec(memory_space=pltpu.VMEM)
SMEM = pl.BlockSpec(memory_space=pltpu.SMEM)


def params(mib, n=0):
    return pltpu.CompilerParams(
        vmem_limit_bytes=mib << 20, dimension_semantics=("arbitrary",) * n if n else None
    )


def bits_of(n):
    return [1 << b for b in range(n.bit_length() - 1)]


def swap(x, axis, n, k, keep=lambda i: True):
    return lax.ppermute(x, axis, [(i, i ^ k) for i in range(n) if keep(i)])


def dot(a, b, ca=1, cb=0, **kw):
    return lax.dot_general(a, b, (((ca,), (cb,)), ((), ())), preferred_element_type=F32, **kw)


def iota(shape, dim):
    return lax.broadcasted_iota(jnp.int32, shape, dim)


def running_sum(log_decay):
    length = log_decay.shape[1]
    tril = (iota((length, length), 0) >= iota((length, length), 1)).astype(F32)
    return dot(tril, log_decay, 1, 1, precision=lax.Precision.HIGHEST)


def running_sum_rows(log_decay):
    length = log_decay.shape[1]
    triu = (iota((length, length), 0) <= iota((length, length), 1)).astype(F32)
    return dot(log_decay, triu, precision=lax.Precision.HIGHEST)


def state_kernel(keys, values, log_decay, *refs):
    states, (key_buf, value_buf, sems) = refs[:-3], refs[-3:]
    requests, length, features = keys.shape
    heads = log_decay.shape[0] // requests
    dim = features // heads
    per = requests // len(states)
    copies = []
    for r in range(requests):
        pair = (
            pltpu.make_async_copy(keys.at[r], key_buf.at[r], sems.at[0, r]),
            pltpu.make_async_copy(values.at[r], value_buf.at[r], sems.at[1, r]),
        )
        for copy in pair:
            copy.start()
        copies.append(pair)
    cum = running_sum(log_decay[...])
    fade = jnp.exp(cum[length - 1 : length, :] - cum)
    for r in range(requests):
        for copy in copies[r]:
            copy.wait()
        for h in range(heads):
            lanes = slice(h * dim, (h + 1) * dim)
            at = h * requests + r
            faded = (key_buf[r, :, lanes].astype(F32) * fade[:, at : at + 1]).astype(BF16)
            states[r // per][(r % per) * heads + h] = dot(
                faded, value_buf[r, :, lanes], 0, 0
            ).astype(BF16)


def inside_kernel(place, queries, keys, values, log_decay, ids, inside, placement, other):
    requests, length, features = keys.shape
    heads = log_decay.shape[0] // requests
    dim = features // heads
    causal = iota((length, length), 0) >= iota((length, length), 1)
    cum = running_sum(log_decay[...])
    rows = running_sum_rows(log_decay[...])
    for r in range(requests):
        for h in range(heads):
            lanes = slice(h * dim, (h + 1) * dim)
            at = h * requests + r
            spread = cum[:, at : at + 1] - rows[at : at + 1, :]
            mask = jnp.where(causal, jnp.exp(jnp.minimum(spread, 0.0)), 0.0)
            scores = dot(queries[r, :, lanes], keys[r, :, lanes], 1, 1)
            inside[r, :, lanes] = dot((scores * mask).astype(BF16), values[r, :, lanes])
    slots, tokens = placement.shape
    experts = slots // CAP
    own = other.shape[0] // CAP
    owner = place[1]
    expert_row = iota((experts, tokens), 0)
    relative = sum((expert_row >= own * k).astype(jnp.int32) for k in range(1, experts // own))
    expert = ((2 * relative) ^ owner) * own + (expert_row - relative * own)
    first = jnp.concatenate([ids[r, 0:1, :] for r in range(requests)], axis=1)
    second = jnp.concatenate([ids[r, 1:2, :] for r in range(requests)], axis=1)
    named = (first == expert) | (second == expert)
    row = iota((tokens, tokens), 0)
    col = iota((tokens, tokens), 1)

    def order(i):
        request = sum((i >= length * k).astype(jnp.int32) for k in range(1, requests))
        return (i - request * length) * requests + request

    earlier = (order(row) < order(col)).astype(BF16)
    before = dot(named.astype(BF16), earlier)
    code = jnp.where(named, before, -1.0).astype(BF16)
    slot_row = iota((slots, experts), 0)
    slot_expert = iota((slots, experts), 1)
    spread_rows = (slot_row >= slot_expert * CAP) & (slot_row < slot_expert * CAP + CAP)
    codes = dot(spread_rows.astype(BF16), code)
    row_of = iota((slots, tokens), 0)
    expert_of = ((row_of.astype(F32) + 0.5) * (1.0 / CAP)).astype(jnp.int32)
    taken = codes == (row_of - expert_of * CAP).astype(F32)
    placement[...] = taken.astype(BF16)
    both = (first + second).astype(F32)
    mine = jnp.sum(jnp.where(taken[: own * CAP], both, 0.0), axis=1, keepdims=True)
    me = owner * own + expert_of[: own * CAP, :1]
    other[...] = jnp.broadcast_to(mine.astype(jnp.int32) - me, other.shape)


def output_kernel(queries, inside, log_decay, gain, *refs):
    incoming, normed = refs[:-1], refs[-1]
    requests, length, features = queries.shape
    heads = log_decay.shape[0] // requests
    dim = features // heads
    per = requests // len(incoming)
    grow = jnp.exp(running_sum(log_decay[...]))
    for r in range(requests):
        for h in range(heads):
            lanes = slice(h * dim, (h + 1) * dim)
            at = h * requests + r
            carried = dot(queries[r, :, lanes], incoming[r // per][(r % per) * heads + h])
            out = inside[r, :, lanes] + grow[:, at : at + 1] * carried
            square = jnp.mean(out * out, axis=1, keepdims=True) + 1e-05
            normed[r * length : (r + 1) * length, lanes] = (
                out * lax.rsqrt(square) * gain[0:1, lanes]
            ).astype(BF16)


def dispatch_kernel(placement, *refs):
    sides, blocks = refs[:2], refs[2:]
    own, cap, width = blocks[0].shape
    for i, side in enumerate(sides):
        routed = dot(placement[...], side[...])
        lanes = slice(i * width // 2, (i + 1) * width // 2)
        for k, block in enumerate(blocks):
            for j in range(own):
                at = (k * own + j) * cap
                block[j, :, lanes] = routed[at : at + cap].astype(BF16)


def gate_kernel(place, other, router, *refs):
    blocks, weight = refs[:-1], refs[-1]
    own, cap, width = blocks[0].shape
    half = width // 2
    owner = place[1]
    experts = router.shape[0]
    for j in range(own):
        logits = jnp.zeros((cap, experts), F32)
        for k, block in enumerate(blocks):
            for side in range(2):
                at = pl.multiple_of((owner ^ (2 * k + side)) * half, half)
                logits = logits + dot(
                    block[j, :, side * half : (side + 1) * half], router[:, pl.ds(at, half)], 1, 1
                )
        col = iota((cap, experts), 1)
        mine = jnp.sum(jnp.where(col == owner * own + j, logits, 0.0), axis=1, keepdims=True)
        theirs_at = other[j * cap : (j + 1) * cap, :1]
        theirs = jnp.sum(jnp.where(col == theirs_at, logits, 0.0), axis=1, keepdims=True)
        weight[j] = jnp.broadcast_to(1.0 / (1.0 + jnp.exp(theirs - mine)), (cap, 128))


def tiles_of(width):
    return 2 if width % 512 == 0 else 1


def up_kernel(place, *refs, parts, first, last):
    blocks, weights = refs[:parts], refs[parts]
    out, acc = refs[-2:]
    j, k = pl.program_id(0), pl.program_id(1)
    depth = weights.shape[1]
    steps = blocks[0].shape[2] // depth
    for step in range(steps):

        @pl.when(k == step)
        def _():
            lanes = slice(step * depth, (step + 1) * depth)
            x = jnp.concatenate([b[j, :, lanes].astype(F32) for b in blocks], axis=0).astype(BF16)
            total = dot(x, weights[0])
            if step:
                total = total + acc[...]
            elif not first:
                total = total + refs[parts + 1][0]
            if step < steps - 1:
                acc[...] = total
            elif last:
                out[0] = (total / (1.0 + jnp.exp(-total))).astype(BF16)
            else:
                out[0] = total


def up_chunk(place, chunk, blocks, weights, total, last):
    own, depth, hidden = weights.shape
    cap, width = blocks[0].shape[1:]
    parts = len(blocks)
    rows = parts * cap
    tiles = tiles_of(width)
    tile = width // 2 // tiles
    first = total is None
    total_spec = pl.BlockSpec((1, rows, hidden), lambda j, k, at: (j, 0, 0))
    return pl.pallas_call(
        functools.partial(up_kernel, parts=parts, first=first, last=last),
        grid_spec=pltpu.PrefetchScalarGridSpec(
            num_scalar_prefetch=1,
            grid=(own, 2 * tiles),
            in_specs=[VMEM] * parts
            + [
                pl.BlockSpec(
                    (1, tile, hidden),
                    lambda j, k, at: (j, (at[1] ^ (2 * chunk + k // tiles)) * tiles + k % tiles, 0),
                )
            ]
            + ([] if first else [total_spec]),
            out_specs=total_spec,
            scratch_shapes=[pltpu.VMEM((rows, hidden), F32)],
        ),
        out_shape=jax.ShapeDtypeStruct((own, rows, hidden), BF16 if last else F32),
        compiler_params=params(32, 2),
        cost_estimate=pl.CostEstimate(
            flops=2 * own * rows * width * hidden,
            bytes_accessed=2 * own * width * hidden,
            transcendentals=0,
        ),
        name=f"up_{chunk}",
    )(place, *blocks, weights, *([] if first else [total]))


def down_kernel(place, hidden, weights, *outs, route):
    result = dot(hidden[0], weights[0])
    for out, members in zip(outs, route):
        for i, member in enumerate(members):
            out[i, 0] = result[member * CAP : (member + 1) * CAP].astype(BF16)


def down_chunk(place, chunk, hidden, weights, width, route):
    own, rows, depth = hidden.shape
    parts = rows // CAP
    tiles = tiles_of(width)
    tile = width // 2 // tiles
    out_spec = pl.BlockSpec((parts // 2, 1, CAP, tile), lambda j, n, at: (0, j, 0, n))
    return pl.pallas_call(
        functools.partial(down_kernel, route=route),
        grid_spec=pltpu.PrefetchScalarGridSpec(
            num_scalar_prefetch=1,
            grid=(own, 2 * tiles),
            in_specs=[
                pl.BlockSpec((1, rows, depth), lambda j, n, at: (j, 0, 0)),
                pl.BlockSpec(
                    (1, depth, tile),
                    lambda j, n, at: (j, 0, (at[1] ^ (2 * chunk + n // tiles)) * tiles + n % tiles),
                ),
            ],
            out_specs=[out_spec] * 2,
        ),
        out_shape=[jax.ShapeDtypeStruct((parts // 2, own, CAP, width), BF16)] * 2,
        compiler_params=params(32, 2),
        cost_estimate=pl.CostEstimate(
            flops=2 * own * rows * width * depth,
            bytes_accessed=2 * own * width * depth,
            transcendentals=0,
        ),
        name=f"down_{chunk}",
    )(place, hidden, weights)


def combine_kernel(normed, placement, *refs):
    blocks, (mine, theirs) = refs[:-2], refs[-2:]
    own = blocks[0].shape[0]
    features = normed.shape[1]
    replies = jnp.concatenate(
        [block[j].astype(F32) for block in blocks for j in range(own)], axis=0
    ).astype(BF16)
    combined = dot(placement[...], replies, 0, 0)
    mine[...] = normed[...].astype(F32) + combined[:, :features]
    theirs[...] = combined[:, features:].astype(BF16)


def after(x, *others):
    return lax.optimization_barrier((x, *others))[0]


def route_of(bits, n):
    keep = [0]
    for bit in reversed(bits[1:]):
        keep = keep + [m | bit for m in keep]
    return [m | bits[0] for m in keep], keep


def halve_kernel(kept, got, keep, send):
    half = keep.shape[0]
    total = kept[...].astype(F32) + got[...].astype(F32)
    keep[...] = total[:half]
    send[...] = total[half:].astype(BF16)


def halve(kept, got):
    shape = (kept.shape[0] // 2,) + kept.shape[1:]
    return pl.pallas_call(
        halve_kernel,
        in_specs=[VMEM] * 2,
        out_specs=[VMEM] * 2,
        out_shape=[jax.ShapeDtypeStruct(shape, F32), jax.ShapeDtypeStruct(shape, BF16)],
        compiler_params=params(32),
        name="partial_sums",
    )(kept, got)


def reply_kernel(kept, got, weight, out):
    total = kept[0].astype(F32) + got[0].astype(F32)
    out[...] = (total * weight[:, :, :1]).astype(BF16)


def reply_of(kept, got, weight):
    return pl.pallas_call(
        reply_kernel,
        in_specs=[VMEM] * 3,
        out_specs=VMEM,
        out_shape=jax.ShapeDtypeStruct(kept.shape[1:], BF16),
        compiler_params=params(32),
        name="reply",
    )(kept, got, weight)


def prefix_by_doubling(states, decay, me, n):
    decay_before, steps = jnp.ones_like(decay), []
    bits = bits_of(n)
    for bit in bits:
        upper = (me & bit) != 0
        partner_decay = swap(decay, "ctx", n, bit)
        steps.append((upper, decay_before, decay, partner_decay))
        decay_before = jnp.where(upper, decay_before * partner_decay, decay_before)
        decay = decay * partner_decay
    incoming = []
    for half, total in enumerate(states):
        before = jnp.zeros((), F32)
        for bit, (upper, d_before, d_total, d_partner) in zip(bits, steps):
            last = bit == bits[-1]
            partner = swap(total, "ctx", n, bit, lambda i: not last or not i & bit).astype(F32)
            before = before + jnp.where(upper, d_before[half], 0.0) * partner
            if not last:
                total = (
                    jnp.where(upper, 1.0, d_partner[half]) * total.astype(F32)
                    + jnp.where(upper, d_total[half], 1.0) * partner
                ).astype(BF16)
        incoming.append(before.astype(BF16))
    return incoming


def prefix_of_four(states, decay, me):
    high, low = (me & 2) != 0, (me & 1) != 0
    near = swap(decay, "ctx", 4, 1)
    far = swap(decay, "ctx", 4, 3)
    one, two = states
    got_one = swap(one, "ctx", 4, 1, lambda i: i != 3).astype(F32)
    got_two = swap(two, "ctx", 4, 2, lambda i: i < 2).astype(F32)
    sent_one = jnp.where(low, 1.0, near[0]) * one.astype(F32) + jnp.where(low, decay[0], 1.0) * got_one
    sent_two = (
        jnp.where(high & low, 0.0, 1.0) * two.astype(F32)
        + jnp.where(high, jnp.where(low, 1.0, far[1] * decay[1]), 0.0) * got_two
    )
    last_one = swap(sent_one.astype(BF16), "ctx", 4, 2, lambda i: i < 2).astype(F32)
    last_two = swap(sent_two.astype(BF16), "ctx", 4, 1, lambda i: i != 1).astype(F32)
    return [
        (jnp.where(low, 1.0, 0.0) * got_one + jnp.where(low, near[0], 1.0) * last_one).astype(BF16),
        (jnp.where(low, near[1], far[1]) * got_two + last_two).astype(BF16),
    ]


def body(n_ctx, n_exp, queries, keys, values, log_decay, norm_gain, router, expert_up, expert_down, expert_ids):
    requests, length, features = queries.shape
    heads = log_decay.shape[2]
    dim = features // heads
    experts = router.shape[1]
    own = expert_up.shape[0]
    tokens = requests * length
    halves = 2 if requests % 2 == 0 else 1
    pairs = requests * heads // halves
    chunks = n_exp // 2
    width = 2 * features
    me = lax.axis_index("ctx")
    place = jnp.stack([me, lax.axis_index("exp")]).astype(jnp.int32)
    struct = jax.ShapeDtypeStruct
    decay_rows = jnp.transpose(log_decay, (2, 0, 1)).reshape(heads * requests, length)

    states = pl.pallas_call(
        state_kernel,
        in_specs=[pl.BlockSpec(memory_space=pl.ANY)] * 2 + [VMEM],
        out_specs=[VMEM] * halves,
        out_shape=[struct((pairs, dim, dim), BF16)] * halves,
        scratch_shapes=[
            pltpu.VMEM(keys.shape, BF16),
            pltpu.VMEM(values.shape, BF16),
            pltpu.SemaphoreType.DMA((2, requests)),
        ],
        compiler_params=params(32),
        name="local_state",
    )(keys, values, decay_rows)
    decay = jnp.exp(jnp.sum(log_decay, axis=1)).reshape(halves, pairs, 1, 1)
    if n_ctx == 4 and halves == 2:
        incoming = prefix_of_four(states, decay, me)
    else:
        incoming = prefix_by_doubling(states, decay, me, n_ctx)

    inside, placement, other = pl.pallas_call(
        inside_kernel,
        in_specs=[SMEM] + [VMEM] * 5,
        out_specs=[VMEM] * 3,
        out_shape=[
            struct((requests, length, features), F32),
            struct((chunks * own * CAP, tokens), BF16),
            struct((own * CAP, 128), jnp.int32),
        ],
        compiler_params=params(32),
        name="inside_and_placement",
    )(place, queries, keys, values, decay_rows, jnp.transpose(expert_ids, (1, 2, 0)))

    normed = pl.pallas_call(
        output_kernel,
        in_specs=[VMEM] * (4 + halves),
        out_specs=VMEM,
        out_shape=struct((tokens, features), BF16),
        compiler_params=params(32),
        name="normed",
    )(queries, inside, decay_rows, norm_gain.reshape(1, features), *incoming)

    outgoing = pl.pallas_call(
        dispatch_kernel,
        in_specs=[VMEM] * 3,
        out_specs=[VMEM] * chunks,
        out_shape=[struct((own, CAP, width), BF16)] * chunks,
        compiler_params=params(32),
        name="dispatch",
    )(placement, normed, swap(normed, "exp", n_exp, 1))
    arrived = [outgoing[0]] + [swap(outgoing[k], "exp", n_exp, 2 * k) for k in range(1, chunks)]
    weight = pl.pallas_call(
        gate_kernel,
        in_specs=[SMEM] + [VMEM] * (2 + chunks),
        out_specs=VMEM,
        out_shape=struct((own, CAP, 128), F32),
        compiler_params=params(32),
        name="gate",
    )(place, other, router.T, *arrived)

    bits = bits_of(n_ctx)
    orders = [bits if k % 2 == 0 else bits[::-1] for k in range(chunks)]

    def gather_round(have, bit, token):
        found = {}
        for rel, block in have.items():
            found[rel | bit] = swap(block if token is None else after(block, token), "ctx", n_ctx, bit)
        return {**have, **found}

    total = None
    gathered = [None] * chunks
    for k in range(chunks):
        have = {0: arrived[k]}
        for bit in orders[k]:
            have = gather_round(have, bit, total if k >= 2 else None)
        gathered[k] = [have[rel] for rel in range(n_ctx)]
        if k >= 1:
            total = up_chunk(place, k - 1, gathered[k - 1], expert_up, total, False)
    hidden = up_chunk(place, chunks - 1, gathered[-1], expert_up, after(total, weight), True)

    pending, returned = [], [None] * chunks

    def advance(token):
        k, step, kept, got = pending.pop(0)
        got = after(got, token)
        if step + 1 < len(bits):
            kept, sent = halve(kept, got)
            pending.append((k, step + 1, kept, swap(sent, "ctx", n_ctx, orders[k][step + 1])))
            return sent
        reply = reply_of(kept, got, weight)
        returned[k] = swap(reply, "exp", n_exp, 2 * k) if k else reply
        return reply

    token = hidden
    for k in reversed(range(chunks)):
        sent, kept = down_chunk(
            place, k, after(hidden, token), expert_down, width, route_of(orders[k], n_ctx)
        )
        pending.append((k, 0, kept, swap(sent, "ctx", n_ctx, orders[k][0])))
        token = advance(sent) if k < chunks - 2 else sent
    while pending:
        token = advance(token)

    mine, theirs = pl.pallas_call(
        combine_kernel,
        in_specs=[VMEM] * (2 + chunks),
        out_specs=[VMEM] * 2,
        out_shape=[struct((tokens, features), F32), struct((tokens, features), BF16)],
        compiler_params=params(32),
        name="combine",
    )(normed, placement, *returned)
    out = mine + swap(theirs, "exp", n_exp, 1).astype(F32)
    return out.astype(BF16).reshape(requests, length, features)


def solution(mesh):
    in_specs = (
        P(None, "ctx", "exp"),
        P(None, "ctx", "exp"),
        P(None, "ctx", "exp"),
        P(None, "ctx", "exp"),
        P("exp"),
        P(),
        P("exp", None, "ctx"),
        P("exp", "ctx", None),
        P("ctx", None, None),
    )
    out_specs = P(None, "ctx", "exp")
    run = functools.partial(body, mesh.shape["ctx"], mesh.shape["exp"])
    return jax.shard_map(run, mesh=mesh, in_specs=in_specs, out_specs=out_specs, check_vma=False)
```

```python
import functools

import jax
import jax.numpy as jnp
from jax import lax
from jax.experimental import pallas as pl
from jax.experimental.pallas import tpu as pltpu
from jax.sharding import PartitionSpec as P

CAP = 40
F32 = jnp.float32
BF16 = jnp.bfloat16
VMEM = pl.BlockSpec(memory_space=pltpu.VMEM)
SMEM = pl.BlockSpec(memory_space=pltpu.SMEM)
ANY = pl.BlockSpec(memory_space=pl.ANY)


def params(mib):
    return pltpu.CompilerParams(vmem_limit_bytes=mib << 20)


def bits_of(n):
    return [1 << b for b in range(n.bit_length() - 1)]


def swap(x, axis, n, k, keep=lambda i: True):
    return lax.ppermute(x, axis, [(i, i ^ k) for i in range(n) if keep(i)])


def dot(a, b, ca=1, cb=0, **kw):
    return lax.dot_general(a, b, (((ca,), (cb,)), ((), ())), preferred_element_type=F32, **kw)


def iota(shape, dim):
    return lax.broadcasted_iota(jnp.int32, shape, dim)


def running_sum(log_decay):
    length = log_decay.shape[1]
    tril = (iota((length, length), 0) >= iota((length, length), 1)).astype(F32)
    return dot(tril, log_decay, 1, 1, precision=lax.Precision.HIGHEST)


def running_sum_rows(log_decay):
    length = log_decay.shape[1]
    triu = (iota((length, length), 0) <= iota((length, length), 1)).astype(F32)
    return dot(log_decay, triu, precision=lax.Precision.HIGHEST)


def state_kernel(keys, values, log_decay, *refs):
    states, (key_buf, value_buf, sems) = refs[:-3], refs[-3:]
    requests, length, features = keys.shape
    heads = log_decay.shape[0] // requests
    dim = features // heads
    per = requests // len(states)
    copies = []
    for r in range(requests):
        pair = (
            pltpu.make_async_copy(keys.at[r], key_buf.at[r], sems.at[0, r]),
            pltpu.make_async_copy(values.at[r], value_buf.at[r], sems.at[1, r]),
        )
        for copy in pair:
            copy.start()
        copies.append(pair)
    cum = running_sum(log_decay[...])
    fade = jnp.exp(cum[length - 1 : length, :] - cum)
    for r in range(requests):
        for copy in copies[r]:
            copy.wait()
        for h in range(heads):
            lanes = slice(h * dim, (h + 1) * dim)
            at = h * requests + r
            faded = (key_buf[r, :, lanes].astype(F32) * fade[:, at : at + 1]).astype(BF16)
            states[r // per][(r % per) * heads + h] = dot(
                faded, value_buf[r, :, lanes], 0, 0
            ).astype(BF16)


def inside_kernel(place, queries, keys, values, log_decay, ids, inside, placement, other):
    requests, length, features = keys.shape
    heads = log_decay.shape[0] // requests
    dim = features // heads
    causal = iota((length, length), 0) >= iota((length, length), 1)
    cum = running_sum(log_decay[...])
    rows = running_sum_rows(log_decay[...])
    for r in range(requests):
        for h in range(heads):
            lanes = slice(h * dim, (h + 1) * dim)
            at = h * requests + r
            spread = cum[:, at : at + 1] - rows[at : at + 1, :]
            mask = jnp.where(causal, jnp.exp(jnp.minimum(spread, 0.0)), 0.0)
            scores = dot(queries[r, :, lanes], keys[r, :, lanes], 1, 1)
            inside[r, :, lanes] = dot((scores * mask).astype(BF16), values[r, :, lanes])
    slots, tokens = placement.shape
    experts = slots // CAP
    own = other.shape[0] // CAP
    owner = place[1]
    expert_row = iota((experts, tokens), 0)
    relative = sum((expert_row >= own * k).astype(jnp.int32) for k in range(1, experts // own))
    expert = ((2 * relative) ^ owner) * own + (expert_row - relative * own)
    first = jnp.concatenate([ids[r, 0:1, :] for r in range(requests)], axis=1)
    second = jnp.concatenate([ids[r, 1:2, :] for r in range(requests)], axis=1)
    named = (first == expert) | (second == expert)
    row = iota((tokens, tokens), 0)
    col = iota((tokens, tokens), 1)

    def order(i):
        request = sum((i >= length * k).astype(jnp.int32) for k in range(1, requests))
        return (i - request * length) * requests + request

    earlier = (order(row) < order(col)).astype(BF16)
    before = dot(named.astype(BF16), earlier)
    code = jnp.where(named, before, -1.0).astype(BF16)
    slot_row = iota((slots, experts), 0)
    slot_expert = iota((slots, experts), 1)
    spread_rows = (slot_row >= slot_expert * CAP) & (slot_row < slot_expert * CAP + CAP)
    codes = dot(spread_rows.astype(BF16), code)
    row_of = iota((slots, tokens), 0)
    expert_of = ((row_of.astype(F32) + 0.5) * (1.0 / CAP)).astype(jnp.int32)
    taken = codes == (row_of - expert_of * CAP).astype(F32)
    placement[...] = taken.astype(BF16)
    both = (first + second).astype(F32)
    mine = jnp.sum(jnp.where(taken[: own * CAP], both, 0.0), axis=1, keepdims=True)
    me = owner * own + expert_of[: own * CAP, :1]
    other[...] = jnp.broadcast_to(mine.astype(jnp.int32) - me, other.shape)


def output_kernel(queries, inside, log_decay, gain, *refs):
    incoming, normed = refs[:-1], refs[-1]
    requests, length, features = queries.shape
    heads = log_decay.shape[0] // requests
    dim = features // heads
    per = requests // len(incoming)
    grow = jnp.exp(running_sum(log_decay[...]))
    for r in range(requests):
        for h in range(heads):
            lanes = slice(h * dim, (h + 1) * dim)
            at = h * requests + r
            carried = dot(queries[r, :, lanes], incoming[r // per][(r % per) * heads + h])
            out = inside[r, :, lanes] + grow[:, at : at + 1] * carried
            square = jnp.mean(out * out, axis=1, keepdims=True) + 1e-05
            normed[r * length : (r + 1) * length, lanes] = (
                out * lax.rsqrt(square) * gain[0:1, lanes]
            ).astype(BF16)


def dispatch_kernel(placement, *refs):
    sides, blocks = refs[:2], refs[2:]
    own, cap, width = blocks[0].shape
    for i, side in enumerate(sides):
        routed = dot(placement[...], side[...])
        lanes = slice(i * width // 2, (i + 1) * width // 2)
        for k, block in enumerate(blocks):
            for j in range(own):
                at = (k * own + j) * cap
                block[j, :, lanes] = routed[at : at + cap].astype(BF16)


def gate_kernel(place, other, router, *refs):
    blocks, weight = refs[:-1], refs[-1]
    own, cap, width = blocks[0].shape
    half = width // 2
    owner = place[1]
    experts = router.shape[0]
    for j in range(own):
        logits = jnp.zeros((cap, experts), F32)
        for k, block in enumerate(blocks):
            for side in range(2):
                at = pl.multiple_of((owner ^ (2 * k + side)) * half, half)
                logits = logits + dot(
                    block[j, :, side * half : (side + 1) * half], router[:, pl.ds(at, half)], 1, 1
                )
        col = iota((cap, experts), 1)
        mine = jnp.sum(jnp.where(col == owner * own + j, logits, 0.0), axis=1, keepdims=True)
        theirs_at = other[j * cap : (j + 1) * cap, :1]
        theirs = jnp.sum(jnp.where(col == theirs_at, logits, 0.0), axis=1, keepdims=True)
        weight[j] = jnp.broadcast_to(1.0 / (1.0 + jnp.exp(theirs - mine)), (cap, 128))


def tiles_of(rows):
    return 2 if rows % 512 == 0 else 1


def up_kernel(place, weights, *refs, chunk, parts, first, last):
    blocks, (out, buffer, sems) = refs[:parts], refs[-3:]
    own, steps, depth, _ = buffer.shape
    tiles = steps // 2
    owner = place[1]

    def at(t):
        return pl.multiple_of(((owner ^ (2 * chunk + t // tiles)) * tiles + t % tiles) * depth, depth)

    copies = []
    for j in range(own):
        for t in range(steps):
            copy = pltpu.make_async_copy(
                weights.at[j, pl.ds(at(t), depth), :], buffer.at[j, t], sems.at[j, t]
            )
            copy.start()
            copies.append(copy)
    for j in range(own):
        total = None if first else refs[parts][j]
        for t in range(steps):
            lanes = slice(t * depth, (t + 1) * depth)
            x = jnp.concatenate([b[j, :, lanes].astype(F32) for b in blocks], axis=0).astype(BF16)
            copies[j * steps + t].wait()
            part = dot(x, buffer[j, t])
            total = part if total is None else total + part
        out[j] = (total / (1.0 + jnp.exp(-total))).astype(BF16) if last else total


def up_chunk(place, chunk, blocks, weights, total, last):
    own, _, hidden = weights.shape
    cap, width = blocks[0].shape[1:]
    parts = len(blocks)
    rows = parts * cap
    steps = 2 * tiles_of(width // 2)
    first = total is None
    return pl.pallas_call(
        functools.partial(up_kernel, chunk=chunk, parts=parts, first=first, last=last),
        in_specs=[SMEM, ANY] + [VMEM] * (parts + (not first)),
        out_specs=VMEM,
        out_shape=jax.ShapeDtypeStruct((own, rows, hidden), BF16 if last else F32),
        scratch_shapes=[
            pltpu.VMEM((own, steps, width // steps, hidden), BF16),
            pltpu.SemaphoreType.DMA((own, steps)),
        ],
        compiler_params=params(32),
        cost_estimate=pl.CostEstimate(
            flops=2 * own * rows * width * hidden,
            bytes_accessed=2 * own * width * hidden,
            transcendentals=0,
        ),
        name=f"up_{chunk}",
    )(place, weights, *blocks, *([] if first else [total]))


def down_kernel(place, weights, hidden, *refs, chunk, route):
    outs, (buffer, sems) = refs[:-2], refs[-2:]
    own, steps, depth, half = buffer.shape
    owner = place[1]
    copies = []
    for j in range(own):
        for t in range(steps):
            col = pl.multiple_of((owner ^ (2 * chunk + t // (steps // 2))) * half, half)
            row = (t % (steps // 2)) * depth
            copy = pltpu.make_async_copy(
                weights.at[j, row : row + depth, pl.ds(col, half)], buffer.at[j, t], sems.at[j, t]
            )
            copy.start()
            copies.append(copy)
    for j in range(own):
        for side in range(2):
            total = None
            for t in range(steps // 2):
                copies[j * steps + side * (steps // 2) + t].wait()
                part = dot(
                    hidden[j, :, t * depth : (t + 1) * depth], buffer[j, side * (steps // 2) + t]
                )
                total = part if total is None else total + part
            lanes = slice(side * half, (side + 1) * half)
            for out, members in zip(outs, route):
                for i, member in enumerate(members):
                    out[i, j, :, lanes] = total[member * CAP : (member + 1) * CAP].astype(BF16)


def down_chunk(place, chunk, hidden, weights, width, route):
    own, rows, depth = hidden.shape
    parts = rows // CAP
    tiles = tiles_of(depth)
    return pl.pallas_call(
        functools.partial(down_kernel, chunk=chunk, route=route),
        in_specs=[SMEM, ANY, VMEM],
        out_specs=[VMEM] * 2,
        out_shape=[jax.ShapeDtypeStruct((parts // 2, own, CAP, width), BF16)] * 2,
        scratch_shapes=[
            pltpu.VMEM((own, 2 * tiles, depth // tiles, width // 2), BF16),
            pltpu.SemaphoreType.DMA((own, 2 * tiles)),
        ],
        compiler_params=params(32),
        cost_estimate=pl.CostEstimate(
            flops=2 * own * rows * width * depth,
            bytes_accessed=2 * own * width * depth,
            transcendentals=0,
        ),
        name=f"down_{chunk}",
    )(place, weights, hidden)


def combine_kernel(normed, placement, *refs):
    blocks, (mine, theirs) = refs[:-2], refs[-2:]
    own = blocks[0].shape[0]
    features = normed.shape[1]
    replies = jnp.concatenate(
        [block[j].astype(F32) for block in blocks for j in range(own)], axis=0
    ).astype(BF16)
    combined = dot(placement[...], replies, 0, 0)
    mine[...] = normed[...].astype(F32) + combined[:, :features]
    theirs[...] = combined[:, features:].astype(BF16)


def after(x, *others):
    return lax.optimization_barrier((x, *others))[0]


def route_of(bits, n):
    keep = [0]
    for bit in reversed(bits[1:]):
        keep = keep + [m | bit for m in keep]
    return [m | bits[0] for m in keep], keep


def halve_kernel(kept, got, keep, send):
    half = keep.shape[0]
    total = kept[...].astype(F32) + got[...].astype(F32)
    keep[...] = total[:half]
    send[...] = total[half:].astype(BF16)


def halve(kept, got):
    shape = (kept.shape[0] // 2,) + kept.shape[1:]
    return pl.pallas_call(
        halve_kernel,
        in_specs=[VMEM] * 2,
        out_specs=[VMEM] * 2,
        out_shape=[jax.ShapeDtypeStruct(shape, F32), jax.ShapeDtypeStruct(shape, BF16)],
        compiler_params=params(32),
        name="partial_sums",
    )(kept, got)


def reply_kernel(kept, got, weight, out):
    total = kept[0].astype(F32) + got[0].astype(F32)
    out[...] = (total * weight[:, :, :1]).astype(BF16)


def reply_of(kept, got, weight):
    return pl.pallas_call(
        reply_kernel,
        in_specs=[VMEM] * 3,
        out_specs=VMEM,
        out_shape=jax.ShapeDtypeStruct(kept.shape[1:], BF16),
        compiler_params=params(32),
        name="reply",
    )(kept, got, weight)


def prefix_by_doubling(states, decay, me, n):
    decay_before, steps = jnp.ones_like(decay), []
    bits = bits_of(n)
    for bit in bits:
        upper = (me & bit) != 0
        partner_decay = swap(decay, "ctx", n, bit)
        steps.append((upper, decay_before, decay, partner_decay))
        decay_before = jnp.where(upper, decay_before * partner_decay, decay_before)
        decay = decay * partner_decay
    incoming = []
    for half, total in enumerate(states):
        before = jnp.zeros((), F32)
        for bit, (upper, d_before, d_total, d_partner) in zip(bits, steps):
            last = bit == bits[-1]
            partner = swap(total, "ctx", n, bit, lambda i: not last or not i & bit).astype(F32)
            before = before + jnp.where(upper, d_before[half], 0.0) * partner
            if not last:
                total = (
                    jnp.where(upper, 1.0, d_partner[half]) * total.astype(F32)
                    + jnp.where(upper, d_total[half], 1.0) * partner
                ).astype(BF16)
        incoming.append(before.astype(BF16))
    return incoming


def prefix_of_four(states, decay, me):
    high, low = (me & 2) != 0, (me & 1) != 0
    near = swap(decay, "ctx", 4, 1)
    far = swap(decay, "ctx", 4, 3)
    one, two = states
    got_one = swap(one, "ctx", 4, 1, lambda i: i != 3).astype(F32)
    got_two = swap(two, "ctx", 4, 2, lambda i: i < 2).astype(F32)
    sent_one = jnp.where(low, 1.0, near[0]) * one.astype(F32) + jnp.where(low, decay[0], 1.0) * got_one
    sent_two = (
        jnp.where(high & low, 0.0, 1.0) * two.astype(F32)
        + jnp.where(high, jnp.where(low, 1.0, far[1] * decay[1]), 0.0) * got_two
    )
    last_one = swap(sent_one.astype(BF16), "ctx", 4, 2, lambda i: i < 2).astype(F32)
    last_two = swap(sent_two.astype(BF16), "ctx", 4, 1, lambda i: i != 1).astype(F32)
    return [
        (jnp.where(low, 1.0, 0.0) * got_one + jnp.where(low, near[0], 1.0) * last_one).astype(BF16),
        (jnp.where(low, near[1], far[1]) * got_two + last_two).astype(BF16),
    ]


def body(n_ctx, n_exp, queries, keys, values, log_decay, norm_gain, router, expert_up, expert_down, expert_ids):
    requests, length, features = queries.shape
    heads = log_decay.shape[2]
    dim = features // heads
    experts = router.shape[1]
    own = expert_up.shape[0]
    tokens = requests * length
    halves = 2 if requests % 2 == 0 else 1
    pairs = requests * heads // halves
    chunks = n_exp // 2
    width = 2 * features
    me = lax.axis_index("ctx")
    place = jnp.stack([me, lax.axis_index("exp")]).astype(jnp.int32)
    struct = jax.ShapeDtypeStruct
    decay_rows = jnp.transpose(log_decay, (2, 0, 1)).reshape(heads * requests, length)

    states = pl.pallas_call(
        state_kernel,
        in_specs=[ANY] * 2 + [VMEM],
        out_specs=[VMEM] * halves,
        out_shape=[struct((pairs, dim, dim), BF16)] * halves,
        scratch_shapes=[
            pltpu.VMEM(keys.shape, BF16),
            pltpu.VMEM(values.shape, BF16),
            pltpu.SemaphoreType.DMA((2, requests)),
        ],
        compiler_params=params(60),
        name="local_state",
    )(keys, values, decay_rows)
    decay = jnp.exp(jnp.sum(after(log_decay, *states), axis=1)).reshape(halves, pairs, 1, 1)
    if n_ctx == 4 and halves == 2:
        incoming = prefix_of_four(states, decay, me)
    else:
        incoming = prefix_by_doubling(states, decay, me, n_ctx)

    inside, placement, other = pl.pallas_call(
        inside_kernel,
        in_specs=[SMEM] + [VMEM] * 5,
        out_specs=[VMEM] * 3,
        out_shape=[
            struct((requests, length, features), F32),
            struct((chunks * own * CAP, tokens), BF16),
            struct((own * CAP, 128), jnp.int32),
        ],
        compiler_params=params(32),
        name="inside_and_placement",
    )(place, queries, keys, values, decay_rows, jnp.transpose(expert_ids, (1, 2, 0)))

    normed = pl.pallas_call(
        output_kernel,
        in_specs=[VMEM] * (4 + halves),
        out_specs=VMEM,
        out_shape=struct((tokens, features), BF16),
        compiler_params=params(32),
        name="normed",
    )(queries, inside, decay_rows, norm_gain.reshape(1, features), *incoming)

    outgoing = pl.pallas_call(
        dispatch_kernel,
        in_specs=[VMEM] * 3,
        out_specs=[VMEM] * chunks,
        out_shape=[struct((own, CAP, width), BF16)] * chunks,
        compiler_params=params(32),
        name="dispatch",
    )(placement, normed, swap(normed, "exp", n_exp, 1))
    arrived = [outgoing[0]] + [swap(outgoing[k], "exp", n_exp, 2 * k) for k in range(1, chunks)]
    weight = pl.pallas_call(
        gate_kernel,
        in_specs=[SMEM] + [VMEM] * (2 + chunks),
        out_specs=VMEM,
        out_shape=struct((own, CAP, 128), F32),
        compiler_params=params(32),
        name="gate",
    )(place, other, router.T, *arrived)

    bits = bits_of(n_ctx)
    orders = [bits if k % 2 == 0 else bits[::-1] for k in range(chunks)]

    def gather_round(have, bit, token):
        found = {}
        for rel, block in have.items():
            found[rel | bit] = swap(block if token is None else after(block, token), "ctx", n_ctx, bit)
        return {**have, **found}

    total = None
    gathered = [None] * chunks
    for k in range(chunks):
        have = {0: arrived[k]}
        for bit in orders[k]:
            have = gather_round(have, bit, None)
        gathered[k] = [have[rel] for rel in range(n_ctx)]
    gathered[0][0] = after(gathered[0][0], weight)
    for k in range(chunks):
        total = up_chunk(place, k, gathered[k], expert_up, total, k == chunks - 1)
    hidden = total

    pending, returned = [], [None] * chunks

    def advance(token):
        k, step, kept, got = pending.pop(0)
        got = after(got, token)
        if step + 1 < len(bits):
            kept, sent = halve(kept, got)
            pending.append((k, step + 1, kept, swap(sent, "ctx", n_ctx, orders[k][step + 1])))
            return sent
        reply = reply_of(kept, got, weight)
        returned[k] = swap(reply, "exp", n_exp, 2 * k) if k else reply
        return reply

    token = hidden
    for k in reversed(range(chunks)):
        sent, kept = down_chunk(
            place, k, after(hidden, token), expert_down, width, route_of(orders[k], n_ctx)
        )
        pending.append((k, 0, kept, swap(sent, "ctx", n_ctx, orders[k][0])))
        token = advance(sent) if k < chunks - 2 else sent
    while pending:
        token = advance(token)

    mine, theirs = pl.pallas_call(
        combine_kernel,
        in_specs=[VMEM] * (2 + chunks),
        out_specs=[VMEM] * 2,
        out_shape=[struct((tokens, features), F32), struct((tokens, features), BF16)],
        compiler_params=params(32),
        name="combine",
    )(normed, placement, *returned)
    out = mine + swap(theirs, "exp", n_exp, 1).astype(F32)
    return out.astype(BF16).reshape(requests, length, features)


def solution(mesh):
    in_specs = (
        P(None, "ctx", "exp"),
        P(None, "ctx", "exp"),
        P(None, "ctx", "exp"),
        P(None, "ctx", "exp"),
        P("exp"),
        P(),
        P("exp", None, "ctx"),
        P("exp", "ctx", None),
        P("ctx", None, None),
    )
    out_specs = P(None, "ctx", "exp")
    run = functools.partial(body, mesh.shape["ctx"], mesh.shape["exp"])
    return jax.shard_map(run, mesh=mesh, in_specs=in_specs, out_specs=out_specs, check_vma=False)
```

```python
import functools

import jax
import jax.numpy as jnp
from jax import lax
from jax.experimental import pallas as pl
from jax.experimental.pallas import tpu as pltpu
from jax.sharding import PartitionSpec as P

CAP = 40
F32 = jnp.float32
BF16 = jnp.bfloat16
VMEM = pl.BlockSpec(memory_space=pltpu.VMEM)
SMEM = pl.BlockSpec(memory_space=pltpu.SMEM)
ANY = pl.BlockSpec(memory_space=pl.ANY)


def params(mib):
    return pltpu.CompilerParams(vmem_limit_bytes=mib << 20)


def bits_of(n):
    return [1 << b for b in range(n.bit_length() - 1)]


def swap(x, axis, n, k, keep=lambda i: True):
    return lax.ppermute(x, axis, [(i, i ^ k) for i in range(n) if keep(i)])


def dot(a, b, ca=1, cb=0, **kw):
    return lax.dot_general(a, b, (((ca,), (cb,)), ((), ())), preferred_element_type=F32, **kw)


def iota(shape, dim):
    return lax.broadcasted_iota(jnp.int32, shape, dim)


def running_sum(log_decay):
    length = log_decay.shape[1]
    tril = (iota((length, length), 0) >= iota((length, length), 1)).astype(F32)
    return dot(tril, log_decay, 1, 1, precision=lax.Precision.HIGHEST)


def running_sum_rows(log_decay):
    length = log_decay.shape[1]
    triu = (iota((length, length), 0) <= iota((length, length), 1)).astype(F32)
    return dot(log_decay, triu, precision=lax.Precision.HIGHEST)


def state_kernel(keys, values, log_decay, *refs):
    states, (key_buf, value_buf, sems) = refs[:-3], refs[-3:]
    requests, length, features = keys.shape
    heads = log_decay.shape[0] // requests
    dim = features // heads
    per = requests // len(states)
    copies = []
    for r in range(requests):
        pair = (
            pltpu.make_async_copy(keys.at[r], key_buf.at[r], sems.at[0, r]),
            pltpu.make_async_copy(values.at[r], value_buf.at[r], sems.at[1, r]),
        )
        for copy in pair:
            copy.start()
        copies.append(pair)
    cum = running_sum(log_decay[...])
    fade = jnp.exp(cum[length - 1 : length, :] - cum)
    for r in range(requests):
        for copy in copies[r]:
            copy.wait()
        for h in range(heads):
            lanes = slice(h * dim, (h + 1) * dim)
            at = h * requests + r
            faded = (key_buf[r, :, lanes].astype(F32) * fade[:, at : at + 1]).astype(BF16)
            states[r // per][(r % per) * heads + h] = dot(
                faded, value_buf[r, :, lanes], 0, 0
            ).astype(BF16)


def inside_kernel(place, queries, keys, values, log_decay, ids, inside, placement, other):
    requests, length, features = keys.shape
    heads = log_decay.shape[0] // requests
    dim = features // heads
    causal = iota((length, length), 0) >= iota((length, length), 1)
    cum = running_sum(log_decay[...])
    rows = running_sum_rows(log_decay[...])
    for r in range(requests):
        for h in range(heads):
            lanes = slice(h * dim, (h + 1) * dim)
            at = h * requests + r
            spread = cum[:, at : at + 1] - rows[at : at + 1, :]
            mask = jnp.where(causal, jnp.exp(jnp.minimum(spread, 0.0)), 0.0)
            scores = dot(queries[r, :, lanes], keys[r, :, lanes], 1, 1)
            inside[r, :, lanes] = dot((scores * mask).astype(BF16), values[r, :, lanes])
    slots, tokens = placement.shape
    experts = slots // CAP
    own = other.shape[0] // CAP
    owner = place[1]
    expert_row = iota((experts, tokens), 0)
    relative = sum((expert_row >= own * k).astype(jnp.int32) for k in range(1, experts // own))
    expert = ((2 * relative) ^ owner) * own + (expert_row - relative * own)
    first = jnp.concatenate([ids[r, 0:1, :] for r in range(requests)], axis=1)
    second = jnp.concatenate([ids[r, 1:2, :] for r in range(requests)], axis=1)
    named = (first == expert) | (second == expert)
    row = iota((tokens, tokens), 0)
    col = iota((tokens, tokens), 1)

    def order(i):
        request = sum((i >= length * k).astype(jnp.int32) for k in range(1, requests))
        return (i - request * length) * requests + request

    earlier = (order(row) < order(col)).astype(BF16)
    before = dot(named.astype(BF16), earlier)
    code = jnp.where(named, before, -1.0).astype(BF16)
    slot_row = iota((slots, experts), 0)
    slot_expert = iota((slots, experts), 1)
    spread_rows = (slot_row >= slot_expert * CAP) & (slot_row < slot_expert * CAP + CAP)
    codes = dot(spread_rows.astype(BF16), code)
    row_of = iota((slots, tokens), 0)
    expert_of = ((row_of.astype(F32) + 0.5) * (1.0 / CAP)).astype(jnp.int32)
    taken = codes == (row_of - expert_of * CAP).astype(F32)
    placement[...] = taken.astype(BF16)
    both = (first + second).astype(F32)
    mine = jnp.sum(jnp.where(taken[: own * CAP], both, 0.0), axis=1, keepdims=True)
    me = owner * own + expert_of[: own * CAP, :1]
    other[...] = jnp.broadcast_to(mine.astype(jnp.int32) - me, other.shape)


def output_kernel(queries, inside, log_decay, gain, *refs):
    incoming, normed = refs[:-1], refs[-1]
    requests, length, features = queries.shape
    heads = log_decay.shape[0] // requests
    dim = features // heads
    per = requests // len(incoming)
    grow = jnp.exp(running_sum(log_decay[...]))
    for r in range(requests):
        for h in range(heads):
            lanes = slice(h * dim, (h + 1) * dim)
            at = h * requests + r
            carried = dot(queries[r, :, lanes], incoming[r // per][(r % per) * heads + h])
            out = inside[r, :, lanes] + grow[:, at : at + 1] * carried
            square = jnp.mean(out * out, axis=1, keepdims=True) + 1e-05
            normed[r * length : (r + 1) * length, lanes] = (
                out * lax.rsqrt(square) * gain[0:1, lanes]
            ).astype(BF16)


def dispatch_kernel(placement, *refs):
    sides, blocks = refs[:2], refs[2:]
    own, cap, width = blocks[0].shape
    for i, side in enumerate(sides):
        routed = dot(placement[...], side[...])
        lanes = slice(i * width // 2, (i + 1) * width // 2)
        for k, block in enumerate(blocks):
            for j in range(own):
                at = (k * own + j) * cap
                block[j, :, lanes] = routed[at : at + cap].astype(BF16)


def gate_kernel(place, other, router, *refs):
    blocks, weight = refs[:-1], refs[-1]
    own, cap, width = blocks[0].shape
    half = width // 2
    owner = place[1]
    experts = router.shape[0]
    for j in range(own):
        logits = jnp.zeros((cap, experts), F32)
        for k, block in enumerate(blocks):
            for side in range(2):
                at = pl.multiple_of((owner ^ (2 * k + side)) * half, half)
                logits = logits + dot(
                    block[j, :, side * half : (side + 1) * half], router[:, pl.ds(at, half)], 1, 1
                )
        col = iota((cap, experts), 1)
        mine = jnp.sum(jnp.where(col == owner * own + j, logits, 0.0), axis=1, keepdims=True)
        theirs_at = other[j * cap : (j + 1) * cap, :1]
        theirs = jnp.sum(jnp.where(col == theirs_at, logits, 0.0), axis=1, keepdims=True)
        weight[j] = jnp.broadcast_to(1.0 / (1.0 + jnp.exp(theirs - mine)), (cap, 128))


def tiles_of(rows):
    return 2 if rows % 512 == 0 else 1


def up_kernel(place, weights, *refs, chunk, parts, first, last):
    blocks, (out, buffer, sems) = refs[:parts], refs[-3:]
    own, _, half, _ = buffer.shape
    tiles = sems.shape[2]
    depth = half // tiles
    owner = place[1]
    copies = []
    for j in range(own):
        for side in range(2):
            row = pl.multiple_of((owner ^ (2 * chunk + side)) * half, half)
            tile_copies = []
            for t in range(tiles):
                copy = pltpu.make_async_copy(
                    weights.at[j, pl.ds(row + t * depth, depth), :],
                    buffer.at[j, side, t * depth : (t + 1) * depth],
                    sems.at[j, side, t],
                )
                copy.start()
                tile_copies.append(copy)
            copies.append(tile_copies)
    for j in range(own):
        total = None if first else refs[parts][j]
        for side in range(2):
            lanes = slice(side * half, (side + 1) * half)
            x = jnp.concatenate([b[j, :, lanes].astype(F32) for b in blocks], axis=0).astype(BF16)
            for copy in copies[2 * j + side]:
                copy.wait()
            part = dot(x, buffer[j, side])
            total = part if total is None else total + part
        out[j] = (total / (1.0 + jnp.exp(-total))).astype(BF16) if last else total


def up_chunk(place, chunk, blocks, weights, total, last):
    own, _, hidden = weights.shape
    cap, width = blocks[0].shape[1:]
    parts = len(blocks)
    rows = parts * cap
    tiles = tiles_of(width // 2)
    first = total is None
    return pl.pallas_call(
        functools.partial(up_kernel, chunk=chunk, parts=parts, first=first, last=last),
        in_specs=[SMEM, ANY] + [VMEM] * (parts + (not first)),
        out_specs=VMEM,
        out_shape=jax.ShapeDtypeStruct((own, rows, hidden), BF16 if last else F32),
        scratch_shapes=[
            pltpu.VMEM((own, 2, width // 2, hidden), BF16),
            pltpu.SemaphoreType.DMA((own, 2, tiles)),
        ],
        compiler_params=params(32),
        cost_estimate=pl.CostEstimate(
            flops=2 * own * rows * width * hidden,
            bytes_accessed=2 * own * width * hidden,
            transcendentals=0,
        ),
        name=f"up_{chunk}",
    )(place, weights, *blocks, *([] if first else [total]))


def down_kernel(place, weights, hidden, *refs, chunk, route):
    outs, (buffer, sems) = refs[:-2], refs[-2:]
    own, steps, depth, half = buffer.shape
    owner = place[1]
    copies = []
    for j in range(own):
        for t in range(steps):
            col = pl.multiple_of((owner ^ (2 * chunk + t // (steps // 2))) * half, half)
            row = (t % (steps // 2)) * depth
            copy = pltpu.make_async_copy(
                weights.at[j, row : row + depth, pl.ds(col, half)], buffer.at[j, t], sems.at[j, t]
            )
            copy.start()
            copies.append(copy)
    for j in range(own):
        for side in range(2):
            total = None
            for t in range(steps // 2):
                copies[j * steps + side * (steps // 2) + t].wait()
                part = dot(
                    hidden[j, :, t * depth : (t + 1) * depth], buffer[j, side * (steps // 2) + t]
                )
                total = part if total is None else total + part
            lanes = slice(side * half, (side + 1) * half)
            for out, members in zip(outs, route):
                for i, member in enumerate(members):
                    out[i, j, :, lanes] = total[member * CAP : (member + 1) * CAP].astype(BF16)


def down_chunk(place, chunk, hidden, weights, width, route):
    own, rows, depth = hidden.shape
    parts = rows // CAP
    tiles = tiles_of(depth)
    return pl.pallas_call(
        functools.partial(down_kernel, chunk=chunk, route=route),
        in_specs=[SMEM, ANY, VMEM],
        out_specs=[VMEM] * 2,
        out_shape=[jax.ShapeDtypeStruct((parts // 2, own, CAP, width), BF16)] * 2,
        scratch_shapes=[
            pltpu.VMEM((own, 2 * tiles, depth // tiles, width // 2), BF16),
            pltpu.SemaphoreType.DMA((own, 2 * tiles)),
        ],
        compiler_params=params(32),
        cost_estimate=pl.CostEstimate(
            flops=2 * own * rows * width * depth,
            bytes_accessed=2 * own * width * depth,
            transcendentals=0,
        ),
        name=f"down_{chunk}",
    )(place, weights, hidden)


def combine_kernel(normed, placement, *refs):
    blocks, (mine, theirs) = refs[:-2], refs[-2:]
    own = blocks[0].shape[0]
    features = normed.shape[1]
    replies = jnp.concatenate(
        [block[j].astype(F32) for block in blocks for j in range(own)], axis=0
    ).astype(BF16)
    combined = dot(placement[...], replies, 0, 0)
    mine[...] = normed[...].astype(F32) + combined[:, :features]
    theirs[...] = combined[:, features:].astype(BF16)


def after(x, *others):
    return lax.optimization_barrier((x, *others))[0]


def route_of(bits, n):
    keep = [0]
    for bit in reversed(bits[1:]):
        keep = keep + [m | bit for m in keep]
    return [m | bits[0] for m in keep], keep


def halve_kernel(kept, got, keep, send):
    half = keep.shape[0]
    total = kept[...].astype(F32) + got[...].astype(F32)
    keep[...] = total[:half]
    send[...] = total[half:].astype(BF16)


def halve(kept, got):
    shape = (kept.shape[0] // 2,) + kept.shape[1:]
    return pl.pallas_call(
        halve_kernel,
        in_specs=[VMEM] * 2,
        out_specs=[VMEM] * 2,
        out_shape=[jax.ShapeDtypeStruct(shape, F32), jax.ShapeDtypeStruct(shape, BF16)],
        compiler_params=params(32),
        name="partial_sums",
    )(kept, got)


def reply_kernel(kept, got, weight, out):
    total = kept[0].astype(F32) + got[0].astype(F32)
    out[...] = (total * weight[:, :, :1]).astype(BF16)


def reply_of(kept, got, weight):
    return pl.pallas_call(
        reply_kernel,
        in_specs=[VMEM] * 3,
        out_specs=VMEM,
        out_shape=jax.ShapeDtypeStruct(kept.shape[1:], BF16),
        compiler_params=params(32),
        name="reply",
    )(kept, got, weight)


def prefix_by_doubling(states, decay, me, n):
    decay_before, steps = jnp.ones_like(decay), []
    bits = bits_of(n)
    for bit in bits:
        upper = (me & bit) != 0
        partner_decay = swap(decay, "ctx", n, bit)
        steps.append((upper, decay_before, decay, partner_decay))
        decay_before = jnp.where(upper, decay_before * partner_decay, decay_before)
        decay = decay * partner_decay
    incoming = []
    for half, total in enumerate(states):
        before = jnp.zeros((), F32)
        for bit, (upper, d_before, d_total, d_partner) in zip(bits, steps):
            last = bit == bits[-1]
            partner = swap(total, "ctx", n, bit, lambda i: not last or not i & bit).astype(F32)
            before = before + jnp.where(upper, d_before[half], 0.0) * partner
            if not last:
                total = (
                    jnp.where(upper, 1.0, d_partner[half]) * total.astype(F32)
                    + jnp.where(upper, d_total[half], 1.0) * partner
                ).astype(BF16)
        incoming.append(before.astype(BF16))
    return incoming


def prefix_of_four(states, decay, me):
    high, low = (me & 2) != 0, (me & 1) != 0
    near = swap(decay, "ctx", 4, 1)
    far = swap(decay, "ctx", 4, 3)
    one, two = states
    got_one = swap(one, "ctx", 4, 1, lambda i: i != 3).astype(F32)
    got_two = swap(two, "ctx", 4, 2, lambda i: i < 2).astype(F32)
    sent_one = jnp.where(low, 1.0, near[0]) * one.astype(F32) + jnp.where(low, decay[0], 1.0) * got_one
    sent_two = (
        jnp.where(high & low, 0.0, 1.0) * two.astype(F32)
        + jnp.where(high, jnp.where(low, 1.0, far[1] * decay[1]), 0.0) * got_two
    )
    last_one = swap(sent_one.astype(BF16), "ctx", 4, 2, lambda i: i < 2).astype(F32)
    last_two = swap(sent_two.astype(BF16), "ctx", 4, 1, lambda i: i != 1).astype(F32)
    return [
        (jnp.where(low, 1.0, 0.0) * got_one + jnp.where(low, near[0], 1.0) * last_one).astype(BF16),
        (jnp.where(low, near[1], far[1]) * got_two + last_two).astype(BF16),
    ]


def body(n_ctx, n_exp, queries, keys, values, log_decay, norm_gain, router, expert_up, expert_down, expert_ids):
    requests, length, features = queries.shape
    heads = log_decay.shape[2]
    dim = features // heads
    experts = router.shape[1]
    own = expert_up.shape[0]
    tokens = requests * length
    halves = 2 if requests % 2 == 0 else 1
    pairs = requests * heads // halves
    chunks = n_exp // 2
    width = 2 * features
    me = lax.axis_index("ctx")
    place = jnp.stack([me, lax.axis_index("exp")]).astype(jnp.int32)
    struct = jax.ShapeDtypeStruct
    decay_rows = jnp.transpose(log_decay, (2, 0, 1)).reshape(heads * requests, length)

    states = pl.pallas_call(
        state_kernel,
        in_specs=[ANY] * 2 + [VMEM],
        out_specs=[VMEM] * halves,
        out_shape=[struct((pairs, dim, dim), BF16)] * halves,
        scratch_shapes=[
            pltpu.VMEM(keys.shape, BF16),
            pltpu.VMEM(values.shape, BF16),
            pltpu.SemaphoreType.DMA((2, requests)),
        ],
        compiler_params=params(60),
        name="local_state",
    )(keys, values, decay_rows)
    decay = jnp.exp(jnp.sum(after(log_decay, *states), axis=1)).reshape(halves, pairs, 1, 1)
    if n_ctx == 4 and halves == 2:
        incoming = prefix_of_four(states, decay, me)
    else:
        incoming = prefix_by_doubling(states, decay, me, n_ctx)

    inside, placement, other = pl.pallas_call(
        inside_kernel,
        in_specs=[SMEM] + [VMEM] * 5,
        out_specs=[VMEM] * 3,
        out_shape=[
            struct((requests, length, features), F32),
            struct((chunks * own * CAP, tokens), BF16),
            struct((own * CAP, 128), jnp.int32),
        ],
        compiler_params=params(32),
        name="inside_and_placement",
    )(place, queries, keys, values, decay_rows, jnp.transpose(expert_ids, (1, 2, 0)))

    normed = pl.pallas_call(
        output_kernel,
        in_specs=[VMEM] * (4 + halves),
        out_specs=VMEM,
        out_shape=struct((tokens, features), BF16),
        compiler_params=params(32),
        name="normed",
    )(queries, inside, decay_rows, norm_gain.reshape(1, features), *incoming)

    outgoing = pl.pallas_call(
        dispatch_kernel,
        in_specs=[VMEM] * 3,
        out_specs=[VMEM] * chunks,
        out_shape=[struct((own, CAP, width), BF16)] * chunks,
        compiler_params=params(32),
        name="dispatch",
    )(placement, normed, swap(normed, "exp", n_exp, 1))
    arrived = [outgoing[0]] + [swap(outgoing[k], "exp", n_exp, 2 * k) for k in range(1, chunks)]
    weight = pl.pallas_call(
        gate_kernel,
        in_specs=[SMEM] + [VMEM] * (2 + chunks),
        out_specs=VMEM,
        out_shape=struct((own, CAP, 128), F32),
        compiler_params=params(32),
        name="gate",
    )(place, other, router.T, *arrived)

    bits = bits_of(n_ctx)
    orders = [bits if k % 2 == 0 else bits[::-1] for k in range(chunks)]

    totals = [None] * chunks
    gathered = [None] * chunks

    def project(k):
        total = totals[k - 1] if k else None
        if k == chunks - 2:
            total = after(total, weight)
        totals[k] = up_chunk(place, k, gathered[k], expert_up, total, k == chunks - 1)
        return totals[k]

    for k in range(chunks):
        have = {0: arrived[k]}
        for bit in orders[k]:
            token = project(k - 3) if k >= 3 and bit == orders[k][0] else None
            if k == chunks - 1 and k >= 2 and bit == orders[k][-1] and len(bits) > 1:
                token = project(k - 2)
            found = {}
            for rel, block in have.items():
                if token is not None:
                    block = after(block, token)
                found[rel | bit] = swap(block, "ctx", n_ctx, bit)
            have.update(found)
        gathered[k] = [have[rel] for rel in range(n_ctx)]
    for k in range(chunks):
        if totals[k] is None:
            project(k)
    hidden = totals[-1]

    order = list(reversed(range(chunks)))
    open_sums, returned, token = {}, [None] * chunks, hidden
    for i in range(chunks + 3):
        if i < chunks:
            k = order[i]
            sent, kept = down_chunk(
                place, k, after(hidden, token), expert_down, width, route_of(orders[k], n_ctx)
            )
            open_sums[k] = kept, swap(sent, "ctx", n_ctx, orders[k][0])
            token = sent
        if 2 <= i < chunks + 2:
            k = order[i - 2]
            for bit in orders[k][1:]:
                kept, got = open_sums[k]
                kept, sent = halve(kept, after(got, token))
                open_sums[k] = kept, swap(sent, "ctx", n_ctx, bit)
                token = sent
        if i >= 3:
            k = order[i - 3]
            kept, got = open_sums[k]
            early = [returned[order[i - 5]]] if i >= 5 else []
            token = reply_of(kept, after(got, token, *early), weight)
            returned[k] = swap(token, "exp", n_exp, 2 * k) if k else token

    mine, theirs = pl.pallas_call(
        combine_kernel,
        in_specs=[VMEM] * (2 + chunks),
        out_specs=[VMEM] * 2,
        out_shape=[struct((tokens, features), F32), struct((tokens, features), BF16)],
        compiler_params=params(32),
        name="combine",
    )(normed, placement, *returned)
    out = mine + swap(theirs, "exp", n_exp, 1).astype(F32)
    return out.astype(BF16).reshape(requests, length, features)


def solution(mesh):
    in_specs = (
        P(None, "ctx", "exp"),
        P(None, "ctx", "exp"),
        P(None, "ctx", "exp"),
        P(None, "ctx", "exp"),
        P("exp"),
        P(),
        P("exp", None, "ctx"),
        P("exp", "ctx", None),
        P("ctx", None, None),
    )
    out_specs = P(None, "ctx", "exp")
    run = functools.partial(body, mesh.shape["ctx"], mesh.shape["exp"])
    return jax.shard_map(run, mesh=mesh, in_specs=in_specs, out_specs=out_specs, check_vma=False)
```

```python
import functools

import jax
import jax.numpy as jnp
from jax import lax
from jax.experimental import pallas as pl
from jax.experimental.pallas import tpu as pltpu
from jax.sharding import PartitionSpec as P

CAP = 40
F32 = jnp.float32
BF16 = jnp.bfloat16
VMEM = pl.BlockSpec(memory_space=pltpu.VMEM)
SMEM = pl.BlockSpec(memory_space=pltpu.SMEM)
ANY = pl.BlockSpec(memory_space=pl.ANY)


def params(mib):
    return pltpu.CompilerParams(vmem_limit_bytes=mib << 20)


def bits_of(n):
    return [1 << b for b in range(n.bit_length() - 1)]


def swap(x, axis, n, k, keep=lambda i: True):
    return lax.ppermute(x, axis, [(i, i ^ k) for i in range(n) if keep(i)])


def dot(a, b, ca=1, cb=0, **kw):
    return lax.dot_general(a, b, (((ca,), (cb,)), ((), ())), preferred_element_type=F32, **kw)


def iota(shape, dim):
    return lax.broadcasted_iota(jnp.int32, shape, dim)


def running_sum(log_decay):
    length = log_decay.shape[1]
    tril = (iota((length, length), 0) >= iota((length, length), 1)).astype(F32)
    return dot(tril, log_decay, 1, 1, precision=lax.Precision.HIGHEST)


def running_sum_rows(log_decay):
    length = log_decay.shape[1]
    triu = (iota((length, length), 0) <= iota((length, length), 1)).astype(F32)
    return dot(log_decay, triu, precision=lax.Precision.HIGHEST)


def piece_copies(weights, kind, expert, chunk, owner, buffer, sems):
    copies = []
    for side in range(2):
        rows, cols = buffer.shape[1:]
        tiles = sems.shape[1]
        depth = rows // tiles
        first = (owner ^ (2 * chunk + side)) * (rows if kind == "up" else cols)
        for t in range(tiles):
            if kind == "up":
                source = weights.at[expert, pl.ds(pl.multiple_of(first + t * depth, depth), depth), :]
            else:
                source = weights.at[
                    expert, t * depth : (t + 1) * depth, pl.ds(pl.multiple_of(first, cols), cols)
                ]
            copies.append(
                pltpu.make_async_copy(
                    source, buffer.at[side, t * depth : (t + 1) * depth], sems.at[side, t]
                )
            )
    return copies


def piece_shape(kind, weights, chunks):
    rows, cols = weights.shape[1:]
    return (2, rows // (2 * chunks), cols) if kind == "up" else (2, rows, cols // (2 * chunks))


def with_held(kernel, pieces, place, up, down, *refs):
    sems, refs = refs[-1], refs[:-1]
    outs = refs[len(refs) - len(pieces) :] if pieces else ()
    copies = []
    for i, (kind, chunk) in enumerate(pieces):
        source = up if kind == "up" else down
        copies += piece_copies(source, kind, 0, chunk, place[1], outs[i], sems.at[i])
    for copy in copies:
        copy.start()
    if kernel is not None:
        kernel(place, *refs[: len(refs) - len(pieces)])
    for copy in copies:
        copy.wait()


def call_with_held(kernel, pieces, chunks, place, up, down, args, out_shape, name):
    shapes = [
        jax.ShapeDtypeStruct(piece_shape(kind, up if kind == "up" else down, chunks), BF16)
        for kind, _ in pieces
    ]
    outs = pl.pallas_call(
        functools.partial(with_held, kernel, pieces),
        in_specs=[SMEM, ANY, ANY] + [VMEM] * len(args),
        out_specs=[VMEM] * (len(out_shape) + len(shapes)),
        out_shape=list(out_shape) + shapes,
        scratch_shapes=[pltpu.SemaphoreType.DMA((len(pieces), 2, 2))],
        compiler_params=params(24),
        name=name,
    )(place, up, down, *args)
    return outs[: len(out_shape)], dict(zip(pieces, outs[len(out_shape) :]))


def state_kernel(keys, values, log_decay, *refs):
    states, (key_buf, value_buf, sems) = refs[:-3], refs[-3:]
    requests, length, features = keys.shape
    heads = log_decay.shape[0] // requests
    dim = features // heads
    per = requests // len(states)
    copies = []
    for r in range(requests):
        pair = (
            pltpu.make_async_copy(keys.at[r], key_buf.at[r], sems.at[0, r]),
            pltpu.make_async_copy(values.at[r], value_buf.at[r], sems.at[1, r]),
        )
        for copy in pair:
            copy.start()
        copies.append(pair)
    cum = running_sum(log_decay[...])
    fade = jnp.exp(cum[length - 1 : length, :] - cum)
    for r in range(requests):
        for copy in copies[r]:
            copy.wait()
        for h in range(heads):
            lanes = slice(h * dim, (h + 1) * dim)
            at = h * requests + r
            faded = (key_buf[r, :, lanes].astype(F32) * fade[:, at : at + 1]).astype(BF16)
            states[r // per][(r % per) * heads + h] = dot(
                faded, value_buf[r, :, lanes], 0, 0
            ).astype(BF16)


def inside_kernel(place, queries, keys, values, log_decay, ids, inside, placement, other):
    requests, length, features = keys.shape
    heads = log_decay.shape[0] // requests
    dim = features // heads
    causal = iota((length, length), 0) >= iota((length, length), 1)
    cum = running_sum(log_decay[...])
    rows = running_sum_rows(log_decay[...])
    for r in range(requests):
        for h in range(heads):
            lanes = slice(h * dim, (h + 1) * dim)
            at = h * requests + r
            spread = cum[:, at : at + 1] - rows[at : at + 1, :]
            mask = jnp.where(causal, jnp.exp(jnp.minimum(spread, 0.0)), 0.0)
            scores = dot(queries[r, :, lanes], keys[r, :, lanes], 1, 1)
            inside[r, :, lanes] = dot((scores * mask).astype(BF16), values[r, :, lanes])
    slots, tokens = placement.shape
    experts = slots // CAP
    own = other.shape[0] // CAP
    owner = place[1]
    expert_row = iota((experts, tokens), 0)
    relative = sum((expert_row >= own * k).astype(jnp.int32) for k in range(1, experts // own))
    expert = ((2 * relative) ^ owner) * own + (expert_row - relative * own)
    first = jnp.concatenate([ids[r, 0:1, :] for r in range(requests)], axis=1)
    second = jnp.concatenate([ids[r, 1:2, :] for r in range(requests)], axis=1)
    named = (first == expert) | (second == expert)
    row = iota((tokens, tokens), 0)
    col = iota((tokens, tokens), 1)

    def order(i):
        request = sum((i >= length * k).astype(jnp.int32) for k in range(1, requests))
        return (i - request * length) * requests + request

    earlier = (order(row) < order(col)).astype(BF16)
    before = dot(named.astype(BF16), earlier)
    code = jnp.where(named, before, -1.0).astype(BF16)
    slot_row = iota((slots, experts), 0)
    slot_expert = iota((slots, experts), 1)
    spread_rows = (slot_row >= slot_expert * CAP) & (slot_row < slot_expert * CAP + CAP)
    codes = dot(spread_rows.astype(BF16), code)
    row_of = iota((slots, tokens), 0)
    expert_of = ((row_of.astype(F32) + 0.5) * (1.0 / CAP)).astype(jnp.int32)
    taken = codes == (row_of - expert_of * CAP).astype(F32)
    placement[...] = taken.astype(BF16)
    both = (first + second).astype(F32)
    mine = jnp.sum(jnp.where(taken[: own * CAP], both, 0.0), axis=1, keepdims=True)
    me = owner * own + expert_of[: own * CAP, :1]
    other[...] = jnp.broadcast_to(mine.astype(jnp.int32) - me, other.shape)


def output_kernel(place, queries, inside, log_decay, gain, *refs):
    incoming, normed = refs[:-1], refs[-1]
    requests, length, features = queries.shape
    heads = log_decay.shape[0] // requests
    dim = features // heads
    per = requests // len(incoming)
    grow = jnp.exp(running_sum(log_decay[...]))
    for r in range(requests):
        for h in range(heads):
            lanes = slice(h * dim, (h + 1) * dim)
            at = h * requests + r
            carried = dot(queries[r, :, lanes], incoming[r // per][(r % per) * heads + h])
            out = inside[r, :, lanes] + grow[:, at : at + 1] * carried
            square = jnp.mean(out * out, axis=1, keepdims=True) + 1e-05
            normed[r * length : (r + 1) * length, lanes] = (
                out * lax.rsqrt(square) * gain[0:1, lanes]
            ).astype(BF16)


def dispatch_kernel(placement, *refs):
    sides, blocks = refs[:2], refs[2:]
    own, cap, width = blocks[0].shape
    for i, side in enumerate(sides):
        routed = dot(placement[...], side[...])
        lanes = slice(i * width // 2, (i + 1) * width // 2)
        for k, block in enumerate(blocks):
            for j in range(own):
                at = (k * own + j) * cap
                block[j, :, lanes] = routed[at : at + cap].astype(BF16)


def gate_kernel(place, other, router, *refs):
    blocks, weight = refs[:-1], refs[-1]
    own, cap, width = blocks[0].shape
    half = width // 2
    owner = place[1]
    experts = router.shape[0]
    for j in range(own):
        logits = jnp.zeros((cap, experts), F32)
        for k, block in enumerate(blocks):
            for side in range(2):
                at = pl.multiple_of((owner ^ (2 * k + side)) * half, half)
                logits = logits + dot(
                    block[j, :, side * half : (side + 1) * half], router[:, pl.ds(at, half)], 1, 1
                )
        col = iota((cap, experts), 1)
        mine = jnp.sum(jnp.where(col == owner * own + j, logits, 0.0), axis=1, keepdims=True)
        theirs_at = other[j * cap : (j + 1) * cap, :1]
        theirs = jnp.sum(jnp.where(col == theirs_at, logits, 0.0), axis=1, keepdims=True)
        weight[j] = jnp.broadcast_to(1.0 / (1.0 + jnp.exp(theirs - mine)), (cap, 128))


def project_kernel(place, up, down, *refs, chunks, parts, first, last, held, route):
    refs = list(refs)
    blocks = {k: [refs.pop(0) for _ in range(parts)] for k in chunks}
    ready = {piece: refs.pop(0) for piece in held}
    before = None if first else refs.pop(0)
    sems, buffers = refs.pop(), {}
    pieces = [("up", j, k) for j in range(up.shape[0]) for k in chunks]
    if last:
        pieces += [("down", j, chunks[-1]) for j in range(up.shape[0])]
    pieces = [(kind, j, k) for kind, j, k in pieces if j or (kind, k) not in ready]
    for piece in reversed(pieces):
        buffers[piece] = refs.pop()
    out, outs = refs[0], refs[1:]
    copies = {}
    for i, (kind, j, k) in enumerate(pieces):
        copies[kind, j, k] = piece_copies(
            up if kind == "up" else down, kind, j, k, place[1], buffers[kind, j, k], sems.at[i]
        )
        for copy in copies[kind, j, k]:
            copy.start()

    def weights_of(kind, j, k, side):
        if (kind, j, k) not in buffers:
            return ready[kind, k][side]
        mine = copies[kind, j, k]
        for copy in mine[side * len(mine) // 2 : (side + 1) * len(mine) // 2]:
            copy.wait()
        return buffers[kind, j, k][side]

    for j in range(up.shape[0]):
        total = None if first else before[j]
        for k in chunks:
            half = blocks[k][0].shape[2] // 2
            for side in range(2):
                lanes = slice(side * half, (side + 1) * half)
                x = jnp.concatenate([b[j, :, lanes].astype(F32) for b in blocks[k]], axis=0)
                part = dot(x.astype(BF16), weights_of("up", j, k, side))
                total = part if total is None else total + part
        out[j] = (total / (1.0 + jnp.exp(-total))).astype(BF16) if last else total
    if last:
        for j in range(up.shape[0]):
            for side in range(2):
                lanes = slice(side * half, (side + 1) * half)
                result = dot(out[j], weights_of("down", j, chunks[-1], side))
                for ref, members in zip(outs, route):
                    for i, member in enumerate(members):
                        ref[i, j, :, lanes] = result[member * CAP : (member + 1) * CAP].astype(BF16)


def project(place, chunks, count, gathered, up, down, held, total, route):
    own, _, hidden = up.shape
    cap, width = gathered[chunks[0]][0].shape[1:]
    parts = len(gathered[chunks[0]])
    rows = parts * cap
    first, last = total is None, route is not None
    wanted = [("up", k) for k in chunks] + ([("down", chunks[-1])] if last else [])
    ready = [piece for piece in wanted if piece in held]
    loose = [(kind, k) for kind, k in wanted for j in range(own) if j or (kind, k) not in held]
    scratch = [
        pltpu.VMEM(piece_shape(kind, up if kind == "up" else down, count), BF16)
        for kind in ("up", "down")
        for other, _ in loose
        if other == kind
    ]
    struct = jax.ShapeDtypeStruct
    out_shape = [struct((own, rows, hidden), BF16 if last else F32)]
    if last:
        out_shape += [struct((parts // 2, own, cap, width), BF16)] * 2
    work = (len(chunks) + last) * own * width * hidden
    blocks = [block for k in chunks for block in gathered[k]]
    return pl.pallas_call(
        functools.partial(
            project_kernel,
            chunks=chunks,
            parts=parts,
            first=first,
            last=last,
            held=ready,
            route=route,
        ),
        in_specs=[SMEM, ANY, ANY] + [VMEM] * (len(blocks) + len(ready) + (not first)),
        out_specs=[VMEM] * len(out_shape),
        out_shape=out_shape,
        scratch_shapes=scratch + [pltpu.SemaphoreType.DMA((max(len(scratch), 1), 2, 2))],
        compiler_params=params(24),
        cost_estimate=pl.CostEstimate(
            flops=2 * rows * work, bytes_accessed=2 * work, transcendentals=0
        ),
        name=f"project_{chunks[0]}",
    )(
        place,
        up,
        down,
        *blocks,
        *[held[piece] for piece in ready],
        *([] if first else [total]),
    )


def down_kernel(place, weights, hidden, *refs, chunk, route):
    outs, (buffer, sems) = refs[:-2], refs[-2:]
    own = hidden.shape[0]
    half = buffer.shape[3]
    copies = []
    for j in range(own):
        mine = piece_copies(weights, "down", j, chunk, place[1], buffer.at[j], sems.at[j])
        for copy in mine:
            copy.start()
        copies.append(mine)
    for j in range(own):
        for side in range(2):
            for copy in copies[j][2 * side : 2 * side + 2]:
                copy.wait()
            result = dot(hidden[j], buffer[j, side])
            lanes = slice(side * half, (side + 1) * half)
            for out, members in zip(outs, route):
                for i, member in enumerate(members):
                    out[i, j, :, lanes] = result[member * CAP : (member + 1) * CAP].astype(BF16)


def down_chunk(place, chunk, count, hidden, weights, route):
    own, rows, depth = hidden.shape
    parts = rows // CAP
    shape = piece_shape("down", weights, count)
    width = 2 * shape[2]
    return pl.pallas_call(
        functools.partial(down_kernel, chunk=chunk, route=route),
        in_specs=[SMEM, ANY, VMEM],
        out_specs=[VMEM] * 2,
        out_shape=[jax.ShapeDtypeStruct((parts // 2, own, CAP, width), BF16)] * 2,
        scratch_shapes=[pltpu.VMEM((own, *shape), BF16), pltpu.SemaphoreType.DMA((own, 2, 2))],
        compiler_params=params(24),
        cost_estimate=pl.CostEstimate(
            flops=2 * own * rows * width * depth,
            bytes_accessed=2 * own * width * depth,
            transcendentals=0,
        ),
        name=f"down_{chunk}",
    )(place, weights, hidden)


def combine_kernel(normed, placement, *refs):
    blocks, (mine, theirs) = refs[:-2], refs[-2:]
    own = blocks[0].shape[0]
    features = normed.shape[1]
    replies = jnp.concatenate(
        [block[j].astype(F32) for block in blocks for j in range(own)], axis=0
    ).astype(BF16)
    combined = dot(placement[...], replies, 0, 0)
    mine[...] = normed[...].astype(F32) + combined[:, :features]
    theirs[...] = combined[:, features:].astype(BF16)


def after(x, *others):
    return lax.optimization_barrier((x, *others))[0]


def route_of(bits, n):
    keep = [0]
    for bit in reversed(bits[1:]):
        keep = keep + [m | bit for m in keep]
    return [m | bits[0] for m in keep], keep


def halve_kernel(kept, got, keep, send):
    half = keep.shape[0]
    total = kept[...].astype(F32) + got[...].astype(F32)
    keep[...] = total[:half]
    send[...] = total[half:].astype(BF16)


def halve(kept, got):
    shape = (kept.shape[0] // 2,) + kept.shape[1:]
    return pl.pallas_call(
        halve_kernel,
        in_specs=[VMEM] * 2,
        out_specs=[VMEM] * 2,
        out_shape=[jax.ShapeDtypeStruct(shape, F32), jax.ShapeDtypeStruct(shape, BF16)],
        compiler_params=params(24),
        name="partial_sums",
    )(kept, got)


def reply_kernel(kept, got, weight, out):
    total = kept[0].astype(F32) + got[0].astype(F32)
    out[...] = (total * weight[:, :, :1]).astype(BF16)


def reply_of(kept, got, weight):
    return pl.pallas_call(
        reply_kernel,
        in_specs=[VMEM] * 3,
        out_specs=VMEM,
        out_shape=jax.ShapeDtypeStruct(kept.shape[1:], BF16),
        compiler_params=params(24),
        name="reply",
    )(kept, got, weight)


def prefix_by_doubling(states, decay, me, n):
    decay_before, steps = jnp.ones_like(decay), []
    bits = bits_of(n)
    for bit in bits:
        upper = (me & bit) != 0
        partner_decay = swap(decay, "ctx", n, bit)
        steps.append((upper, decay_before, decay, partner_decay))
        decay_before = jnp.where(upper, decay_before * partner_decay, decay_before)
        decay = decay * partner_decay
    incoming = []
    for half, total in enumerate(states):
        before = jnp.zeros((), F32)
        for bit, (upper, d_before, d_total, d_partner) in zip(bits, steps):
            last = bit == bits[-1]
            partner = swap(total, "ctx", n, bit, lambda i: not last or not i & bit).astype(F32)
            before = before + jnp.where(upper, d_before[half], 0.0) * partner
            if not last:
                total = (
                    jnp.where(upper, 1.0, d_partner[half]) * total.astype(F32)
                    + jnp.where(upper, d_total[half], 1.0) * partner
                ).astype(BF16)
        incoming.append(before.astype(BF16))
    return incoming


def prefix_of_four(states, decay, me, token):
    high, low = (me & 2) != 0, (me & 1) != 0
    near = swap(decay, "ctx", 4, 1)
    far = swap(decay, "ctx", 4, 3)
    one, two = states
    got_one = after(swap(one, "ctx", 4, 1, lambda i: i != 3), *token).astype(F32)
    got_two = swap(two, "ctx", 4, 2, lambda i: i < 2).astype(F32)
    sent_one = jnp.where(low, 1.0, near[0]) * one.astype(F32) + jnp.where(low, decay[0], 1.0) * got_one
    sent_two = (
        jnp.where(high & low, 0.0, 1.0) * two.astype(F32)
        + jnp.where(high, jnp.where(low, 1.0, far[1] * decay[1]), 0.0) * got_two
    )
    last_one = swap(sent_one.astype(BF16), "ctx", 4, 2, lambda i: i < 2).astype(F32)
    last_two = swap(sent_two.astype(BF16), "ctx", 4, 1, lambda i: i != 1).astype(F32)
    return [
        (jnp.where(low, 1.0, 0.0) * got_one + jnp.where(low, near[0], 1.0) * last_one).astype(BF16),
        (jnp.where(low, near[1], far[1]) * got_two + last_two).astype(BF16),
    ]


def body(n_ctx, n_exp, queries, keys, values, log_decay, norm_gain, router, expert_up, expert_down, expert_ids):
    requests, length, features = queries.shape
    heads = log_decay.shape[2]
    dim = features // heads
    experts = router.shape[1]
    own = expert_up.shape[0]
    tokens = requests * length
    halves = 2 if requests % 2 == 0 else 1
    pairs = requests * heads // halves
    chunks = n_exp // 2
    width = 2 * features
    me = lax.axis_index("ctx")
    place = jnp.stack([me, lax.axis_index("exp")]).astype(jnp.int32)
    struct = jax.ShapeDtypeStruct
    early_pieces = [("up", k) for k in range(min(2, chunks - 2))]
    later_pieces = [("up", k) for k in range(max(chunks - 2, 0), chunks)]
    last_pieces = [("down", chunks - 1)]
    decay_rows = jnp.transpose(log_decay, (2, 0, 1)).reshape(heads * requests, length)

    states = pl.pallas_call(
        state_kernel,
        in_specs=[ANY] * 2 + [VMEM],
        out_specs=[VMEM] * halves,
        out_shape=[struct((pairs, dim, dim), BF16)] * halves,
        scratch_shapes=[
            pltpu.VMEM(keys.shape, BF16),
            pltpu.VMEM(values.shape, BF16),
            pltpu.SemaphoreType.DMA((2, requests)),
        ],
        compiler_params=params(60),
        name="local_state",
    )(keys, values, decay_rows)
    decay = jnp.exp(jnp.sum(after(log_decay, *states), axis=1)).reshape(halves, pairs, 1, 1)
    _, held = call_with_held(
        None, early_pieces, chunks, after(place, *states), expert_up, expert_down, [], [], "early_weights"
    )
    if n_ctx == 4 and halves == 2:
        incoming = prefix_of_four(states, decay, me, list(held.values()))
    else:
        incoming = prefix_by_doubling(states, decay, me, n_ctx)

    (inside, placement, other), more = call_with_held(
        inside_kernel,
        later_pieces,
        chunks,
        place,
        expert_up,
        expert_down,
        [queries, keys, values, decay_rows, jnp.transpose(expert_ids, (1, 2, 0))],
        [
            struct((requests, length, features), F32),
            struct((chunks * own * CAP, tokens), BF16),
            struct((own * CAP, 128), jnp.int32),
        ],
        "inside_and_placement",
    )
    held = {**held, **more}
    (normed,), more = call_with_held(
        output_kernel,
        last_pieces,
        chunks,
        place,
        expert_up,
        expert_down,
        [queries, inside, decay_rows, norm_gain.reshape(1, features), *incoming],
        [struct((tokens, features), BF16)],
        "normed",
    )
    held = {**held, **more}

    outgoing = pl.pallas_call(
        dispatch_kernel,
        in_specs=[VMEM] * 3,
        out_specs=[VMEM] * chunks,
        out_shape=[struct((own, CAP, width), BF16)] * chunks,
        compiler_params=params(24),
        name="dispatch",
    )(placement, normed, swap(normed, "exp", n_exp, 1))
    arrived = [outgoing[0]] + [swap(outgoing[k], "exp", n_exp, 2 * k) for k in range(1, chunks)]
    weight = pl.pallas_call(
        gate_kernel,
        in_specs=[SMEM] + [VMEM] * (2 + chunks),
        out_specs=VMEM,
        out_shape=struct((own, CAP, 128), F32),
        compiler_params=params(24),
        name="gate",
    )(place, other, router.T, *arrived)

    bits = bits_of(n_ctx)
    orders = [bits if k % 2 == 0 else bits[::-1] for k in range(chunks)]

    routes = [route_of(order, n_ctx) for order in orders]
    gathered = [None] * chunks
    total, done = None, 0

    def advance(upto):
        nonlocal total, done
        for k in range(done, upto + 1):
            (total,) = project(
                place, [k], chunks, gathered, expert_up, expert_down, held, total, None
            )
        done = max(done, upto + 1)
        return total

    for k in range(chunks):
        have = {0: arrived[k]}
        for bit in orders[k]:
            token = advance(k - 3) if k >= 3 and bit == orders[k][0] else None
            if k == chunks - 1 and k >= 2 and bit == orders[k][-1] and len(bits) > 1:
                token = advance(k - 2)
            found = {}
            for rel, block in have.items():
                if token is not None and (rel or bit == orders[k][0]):
                    block = after(block, token)
                found[rel | bit] = swap(block, "ctx", n_ctx, bit)
            have.update(found)
        gathered[k] = [have[rel] for rel in range(n_ctx)]
    hidden, *far = project(
        after(place, weight),
        list(range(done, chunks)),
        chunks,
        gathered,
        expert_up,
        expert_down,
        held,
        total,
        routes[-1],
    )

    order = list(reversed(range(chunks)))
    open_sums, returned, token = {}, [None] * chunks, hidden
    for i in range(chunks + 3):
        if i < chunks:
            k = order[i]
            sent, kept = far
            if i:
                sent, kept = down_chunk(
                    place, k, chunks, after(hidden, token), expert_down, routes[k]
                )
            open_sums[k] = kept, swap(sent, "ctx", n_ctx, orders[k][0])
            token = sent
        if 2 <= i < chunks + 2:
            k = order[i - 2]
            for bit in orders[k][1:]:
                kept, got = open_sums[k]
                kept, sent = halve(kept, after(got, token))
                open_sums[k] = kept, swap(sent, "ctx", n_ctx, bit)
                token = sent
        if i >= 3:
            k = order[i - 3]
            kept, got = open_sums[k]
            early = [returned[order[i - 5]]] if i >= 5 else []
            token = reply_of(kept, after(got, token, *early), weight)
            returned[k] = swap(token, "exp", n_exp, 2 * k) if k else token

    mine, theirs = pl.pallas_call(
        combine_kernel,
        in_specs=[VMEM] * (2 + chunks),
        out_specs=[VMEM] * 2,
        out_shape=[struct((tokens, features), F32), struct((tokens, features), BF16)],
        compiler_params=params(24),
        name="combine",
    )(normed, placement, *returned)
    out = mine + swap(theirs, "exp", n_exp, 1).astype(F32)
    return out.astype(BF16).reshape(requests, length, features)


def solution(mesh):
    in_specs = (
        P(None, "ctx", "exp"),
        P(None, "ctx", "exp"),
        P(None, "ctx", "exp"),
        P(None, "ctx", "exp"),
        P("exp"),
        P(),
        P("exp", None, "ctx"),
        P("exp", "ctx", None),
        P("ctx", None, None),
    )
    out_specs = P(None, "ctx", "exp")
    run = functools.partial(body, mesh.shape["ctx"], mesh.shape["exp"])
    return jax.shard_map(run, mesh=mesh, in_specs=in_specs, out_specs=out_specs, check_vma=False)
```

```python
import functools

import jax
import jax.numpy as jnp
from jax import lax
from jax.experimental import pallas as pl
from jax.experimental.pallas import tpu as pltpu
from jax.sharding import PartitionSpec as P

CAP = 40
F32 = jnp.float32
BF16 = jnp.bfloat16
VMEM = pl.BlockSpec(memory_space=pltpu.VMEM)
SMEM = pl.BlockSpec(memory_space=pltpu.SMEM)
ANY = pl.BlockSpec(memory_space=pl.ANY)


def params(mib):
    return pltpu.CompilerParams(vmem_limit_bytes=mib << 20)


def bits_of(n):
    return [1 << b for b in range(n.bit_length() - 1)]


def swap(x, axis, n, k, keep=lambda i: True):
    return lax.ppermute(x, axis, [(i, i ^ k) for i in range(n) if keep(i)])


def dot(a, b, ca=1, cb=0, **kw):
    return lax.dot_general(a, b, (((ca,), (cb,)), ((), ())), preferred_element_type=F32, **kw)


def iota(shape, dim):
    return lax.broadcasted_iota(jnp.int32, shape, dim)


def running_sum(log_decay):
    length = log_decay.shape[1]
    tril = (iota((length, length), 0) >= iota((length, length), 1)).astype(F32)
    return dot(tril, log_decay, 1, 1, precision=lax.Precision.HIGHEST)


def running_sum_rows(log_decay):
    length = log_decay.shape[1]
    triu = (iota((length, length), 0) <= iota((length, length), 1)).astype(F32)
    return dot(log_decay, triu, precision=lax.Precision.HIGHEST)


def piece_copies(weights, kind, expert, chunk, owner, buffer, sems):
    copies = []
    for side in range(2):
        rows, cols = buffer.shape[1:]
        tiles = sems.shape[1]
        depth = rows // tiles
        first = (owner ^ (2 * chunk + side)) * (rows if kind == "up" else cols)
        for t in range(tiles):
            if kind == "up":
                source = weights.at[expert, pl.ds(pl.multiple_of(first + t * depth, depth), depth), :]
            else:
                source = weights.at[
                    expert, t * depth : (t + 1) * depth, pl.ds(pl.multiple_of(first, cols), cols)
                ]
            copies.append(
                pltpu.make_async_copy(
                    source, buffer.at[side, t * depth : (t + 1) * depth], sems.at[side, t]
                )
            )
    return copies


def piece_shape(kind, weights, chunks):
    rows, cols = weights.shape[1:]
    return (2, rows // (2 * chunks), cols) if kind == "up" else (2, rows, cols // (2 * chunks))


def with_held(kernel, pieces, place, up, down, *refs):
    sems, refs = refs[-1], refs[:-1]
    outs = refs[len(refs) - len(pieces) :] if pieces else ()
    copies = []
    for i, (kind, chunk) in enumerate(pieces):
        source = up if kind == "up" else down
        copies += piece_copies(source, kind, 0, chunk, place[1], outs[i], sems.at[i])
    for copy in copies:
        copy.start()
    if kernel is not None:
        kernel(place, *refs[: len(refs) - len(pieces)])
    for copy in copies:
        copy.wait()


def call_with_held(kernel, pieces, chunks, place, up, down, args, out_shape, name):
    shapes = [
        jax.ShapeDtypeStruct(piece_shape(kind, up if kind == "up" else down, chunks), BF16)
        for kind, _ in pieces
    ]
    outs = pl.pallas_call(
        functools.partial(with_held, kernel, pieces),
        in_specs=[SMEM, ANY, ANY] + [VMEM] * len(args),
        out_specs=[VMEM] * (len(out_shape) + len(shapes)),
        out_shape=list(out_shape) + shapes,
        scratch_shapes=[pltpu.SemaphoreType.DMA((max(len(pieces), 1), 2, 2))],
        compiler_params=params(24),
        name=name,
    )(place, up, down, *args)
    return outs[: len(out_shape)], dict(zip(pieces, outs[len(out_shape) :]))


def state_kernel(keys, values, log_decay, *refs):
    states, (key_buf, value_buf, sems) = refs[:-3], refs[-3:]
    requests, length, features = keys.shape
    heads = log_decay.shape[0] // requests
    dim = features // heads
    per = requests // len(states)
    copies = []
    for r in range(requests):
        pair = (
            pltpu.make_async_copy(keys.at[r], key_buf.at[r], sems.at[0, r]),
            pltpu.make_async_copy(values.at[r], value_buf.at[r], sems.at[1, r]),
        )
        for copy in pair:
            copy.start()
        copies.append(pair)
    cum = running_sum(log_decay[...])
    fade = jnp.exp(cum[length - 1 : length, :] - cum)
    for r in range(requests):
        for copy in copies[r]:
            copy.wait()
        for h in range(heads):
            lanes = slice(h * dim, (h + 1) * dim)
            at = h * requests + r
            faded = (key_buf[r, :, lanes].astype(F32) * fade[:, at : at + 1]).astype(BF16)
            states[r // per][(r % per) * heads + h] = dot(
                faded, value_buf[r, :, lanes], 0, 0
            ).astype(BF16)


def inside_kernel(place, queries, keys, values, log_decay, ids, inside, placement, other):
    requests, length, features = keys.shape
    heads = log_decay.shape[0] // requests
    dim = features // heads
    causal = iota((length, length), 0) >= iota((length, length), 1)
    cum = running_sum(log_decay[...])
    rows = running_sum_rows(log_decay[...])
    for r in range(requests):
        for h in range(heads):
            lanes = slice(h * dim, (h + 1) * dim)
            at = h * requests + r
            spread = cum[:, at : at + 1] - rows[at : at + 1, :]
            mask = jnp.where(causal, jnp.exp(jnp.minimum(spread, 0.0)), 0.0)
            scores = dot(queries[r, :, lanes], keys[r, :, lanes], 1, 1)
            inside[r, :, lanes] = dot((scores * mask).astype(BF16), values[r, :, lanes])
    slots, tokens = placement.shape
    experts = slots // CAP
    own = other.shape[0] // CAP
    owner = place[1]
    expert_row = iota((experts, tokens), 0)
    relative = sum((expert_row >= own * k).astype(jnp.int32) for k in range(1, experts // own))
    expert = ((2 * relative) ^ owner) * own + (expert_row - relative * own)
    first = jnp.concatenate([ids[r, 0:1, :] for r in range(requests)], axis=1)
    second = jnp.concatenate([ids[r, 1:2, :] for r in range(requests)], axis=1)
    named = (first == expert) | (second == expert)
    row = iota((tokens, tokens), 0)
    col = iota((tokens, tokens), 1)

    def order(i):
        request = sum((i >= length * k).astype(jnp.int32) for k in range(1, requests))
        return (i - request * length) * requests + request

    earlier = (order(row) < order(col)).astype(BF16)
    before = dot(named.astype(BF16), earlier)
    code = jnp.where(named, before, -1.0).astype(BF16)
    slot_row = iota((slots, experts), 0)
    slot_expert = iota((slots, experts), 1)
    spread_rows = (slot_row >= slot_expert * CAP) & (slot_row < slot_expert * CAP + CAP)
    codes = dot(spread_rows.astype(BF16), code)
    row_of = iota((slots, tokens), 0)
    expert_of = ((row_of.astype(F32) + 0.5) * (1.0 / CAP)).astype(jnp.int32)
    taken = codes == (row_of - expert_of * CAP).astype(F32)
    placement[...] = taken.astype(BF16)
    both = (first + second).astype(F32)
    mine = jnp.sum(jnp.where(taken[: own * CAP], both, 0.0), axis=1, keepdims=True)
    me = owner * own + expert_of[: own * CAP, :1]
    other[...] = jnp.broadcast_to(mine.astype(jnp.int32) - me, other.shape)


def output_kernel(place, queries, inside, log_decay, gain, *refs):
    incoming, normed = refs[:-1], refs[-1]
    requests, length, features = queries.shape
    heads = log_decay.shape[0] // requests
    dim = features // heads
    per = requests // len(incoming)
    grow = jnp.exp(running_sum(log_decay[...]))
    for r in range(requests):
        for h in range(heads):
            lanes = slice(h * dim, (h + 1) * dim)
            at = h * requests + r
            carried = dot(queries[r, :, lanes], incoming[r // per][(r % per) * heads + h])
            out = inside[r, :, lanes] + grow[:, at : at + 1] * carried
            square = jnp.mean(out * out, axis=1, keepdims=True) + 1e-05
            normed[r * length : (r + 1) * length, lanes] = (
                out * lax.rsqrt(square) * gain[0:1, lanes]
            ).astype(BF16)


def dispatch_kernel(placement, *refs):
    sides, blocks = refs[:2], refs[2:]
    own, cap, width = blocks[0].shape
    for i, side in enumerate(sides):
        routed = dot(placement[...], side[...])
        lanes = slice(i * width // 2, (i + 1) * width // 2)
        for k, block in enumerate(blocks):
            for j in range(own):
                at = (k * own + j) * cap
                block[j, :, lanes] = routed[at : at + cap].astype(BF16)


def gate_kernel(place, other, router, *refs):
    blocks, weight = refs[:-1], refs[-1]
    own, cap, width = blocks[0].shape
    half = width // 2
    owner = place[1]
    experts = router.shape[0]
    for j in range(own):
        logits = jnp.zeros((cap, experts), F32)
        for k, block in enumerate(blocks):
            for side in range(2):
                at = pl.multiple_of((owner ^ (2 * k + side)) * half, half)
                logits = logits + dot(
                    block[j, :, side * half : (side + 1) * half], router[:, pl.ds(at, half)], 1, 1
                )
        col = iota((cap, experts), 1)
        mine = jnp.sum(jnp.where(col == owner * own + j, logits, 0.0), axis=1, keepdims=True)
        theirs_at = other[j * cap : (j + 1) * cap, :1]
        theirs = jnp.sum(jnp.where(col == theirs_at, logits, 0.0), axis=1, keepdims=True)
        weight[j] = jnp.broadcast_to(1.0 / (1.0 + jnp.exp(theirs - mine)), (cap, 128))


def project_kernel(place, up, down, *refs, chunks, parts, first, last, held, route):
    refs = list(refs)
    blocks = {k: [refs.pop(0) for _ in range(parts)] for k in chunks}
    ready = {piece: refs.pop(0) for piece in held}
    before = None if first else refs.pop(0)
    sems, buffers = refs.pop(), {}
    pieces = [("up", j, k) for j in range(up.shape[0]) for k in chunks]
    if last:
        pieces += [("down", j, chunks[-1]) for j in range(up.shape[0])]
    pieces = [(kind, j, k) for kind, j, k in pieces if j or (kind, k) not in ready]
    for piece in reversed(pieces):
        buffers[piece] = refs.pop()
    out, outs = refs[0], refs[1:]
    copies = {}
    for i, (kind, j, k) in enumerate(pieces):
        copies[kind, j, k] = piece_copies(
            up if kind == "up" else down, kind, j, k, place[1], buffers[kind, j, k], sems.at[i]
        )
        for copy in copies[kind, j, k]:
            copy.start()

    def weights_of(kind, j, k, side):
        if (kind, j, k) not in buffers:
            return ready[kind, k][side]
        mine = copies[kind, j, k]
        for copy in mine[side * len(mine) // 2 : (side + 1) * len(mine) // 2]:
            copy.wait()
        return buffers[kind, j, k][side]

    for j in range(up.shape[0]):
        total = None if first else before[j]
        for k in chunks:
            half = blocks[k][0].shape[2] // 2
            for side in range(2):
                lanes = slice(side * half, (side + 1) * half)
                x = jnp.concatenate([b[j, :, lanes].astype(F32) for b in blocks[k]], axis=0)
                part = dot(x.astype(BF16), weights_of("up", j, k, side))
                total = part if total is None else total + part
        out[j] = (total / (1.0 + jnp.exp(-total))).astype(BF16) if last else total
    if last:
        for j in range(up.shape[0]):
            for side in range(2):
                lanes = slice(side * half, (side + 1) * half)
                result = dot(out[j], weights_of("down", j, chunks[-1], side))
                for ref, members in zip(outs, route):
                    for i, member in enumerate(members):
                        ref[i, j, :, lanes] = result[member * CAP : (member + 1) * CAP].astype(BF16)


def project(place, chunks, count, gathered, up, down, held, total, route):
    own, _, hidden = up.shape
    cap, width = gathered[chunks[0]][0].shape[1:]
    parts = len(gathered[chunks[0]])
    rows = parts * cap
    first, last = total is None, route is not None
    wanted = [("up", k) for k in chunks] + ([("down", chunks[-1])] if last else [])
    ready = [piece for piece in wanted if piece in held]
    loose = [(kind, k) for kind, k in wanted for j in range(own) if j or (kind, k) not in held]
    scratch = [
        pltpu.VMEM(piece_shape(kind, up if kind == "up" else down, count), BF16)
        for kind in ("up", "down")
        for other, _ in loose
        if other == kind
    ]
    struct = jax.ShapeDtypeStruct
    out_shape = [struct((own, rows, hidden), BF16 if last else F32)]
    if last:
        out_shape += [struct((parts // 2, own, cap, width), BF16)] * 2
    work = (len(chunks) + last) * own * width * hidden
    blocks = [block for k in chunks for block in gathered[k]]
    return pl.pallas_call(
        functools.partial(
            project_kernel,
            chunks=chunks,
            parts=parts,
            first=first,
            last=last,
            held=ready,
            route=route,
        ),
        in_specs=[SMEM, ANY, ANY] + [VMEM] * (len(blocks) + len(ready) + (not first)),
        out_specs=[VMEM] * len(out_shape),
        out_shape=out_shape,
        scratch_shapes=scratch + [pltpu.SemaphoreType.DMA((max(len(scratch), 1), 2, 2))],
        compiler_params=params(24),
        cost_estimate=pl.CostEstimate(
            flops=2 * rows * work, bytes_accessed=2 * work, transcendentals=0
        ),
        name=f"project_{chunks[0]}",
    )(
        place,
        up,
        down,
        *blocks,
        *[held[piece] for piece in ready],
        *([] if first else [total]),
    )


def down_kernel(place, weights, hidden, *refs, chunk, route):
    outs, (buffer, sems) = refs[:-2], refs[-2:]
    own = hidden.shape[0]
    half = buffer.shape[3]
    copies = []
    for j in range(own):
        mine = piece_copies(weights, "down", j, chunk, place[1], buffer.at[j], sems.at[j])
        for copy in mine:
            copy.start()
        copies.append(mine)
    for j in range(own):
        for side in range(2):
            for copy in copies[j][2 * side : 2 * side + 2]:
                copy.wait()
            result = dot(hidden[j], buffer[j, side])
            lanes = slice(side * half, (side + 1) * half)
            for out, members in zip(outs, route):
                for i, member in enumerate(members):
                    out[i, j, :, lanes] = result[member * CAP : (member + 1) * CAP].astype(BF16)


def down_chunk(place, chunk, count, hidden, weights, route):
    own, rows, depth = hidden.shape
    parts = rows // CAP
    shape = piece_shape("down", weights, count)
    width = 2 * shape[2]
    return pl.pallas_call(
        functools.partial(down_kernel, chunk=chunk, route=route),
        in_specs=[SMEM, ANY, VMEM],
        out_specs=[VMEM] * 2,
        out_shape=[jax.ShapeDtypeStruct((parts // 2, own, CAP, width), BF16)] * 2,
        scratch_shapes=[pltpu.VMEM((own, *shape), BF16), pltpu.SemaphoreType.DMA((own, 2, 2))],
        compiler_params=params(24),
        cost_estimate=pl.CostEstimate(
            flops=2 * own * rows * width * depth,
            bytes_accessed=2 * own * width * depth,
            transcendentals=0,
        ),
        name=f"down_{chunk}",
    )(place, weights, hidden)


def combine_kernel(normed, placement, *refs):
    blocks, (mine, theirs) = refs[:-2], refs[-2:]
    own = blocks[0].shape[0]
    features = normed.shape[1]
    replies = jnp.concatenate(
        [block[j].astype(F32) for block in blocks for j in range(own)], axis=0
    ).astype(BF16)
    combined = dot(placement[...], replies, 0, 0)
    mine[...] = normed[...].astype(F32) + combined[:, :features]
    theirs[...] = combined[:, features:].astype(BF16)


def after(x, *others):
    return lax.optimization_barrier((x, *others))[0]


def route_of(bits, n):
    keep = [0]
    for bit in reversed(bits[1:]):
        keep = keep + [m | bit for m in keep]
    return [m | bits[0] for m in keep], keep


def halve_kernel(kept, got, keep, send):
    half = keep.shape[0]
    total = kept[...].astype(F32) + got[...].astype(F32)
    keep[...] = total[:half]
    send[...] = total[half:].astype(BF16)


def halve(kept, got):
    shape = (kept.shape[0] // 2,) + kept.shape[1:]
    return pl.pallas_call(
        halve_kernel,
        in_specs=[VMEM] * 2,
        out_specs=[VMEM] * 2,
        out_shape=[jax.ShapeDtypeStruct(shape, F32), jax.ShapeDtypeStruct(shape, BF16)],
        compiler_params=params(24),
        name="partial_sums",
    )(kept, got)


def reply_kernel(kept, got, weight, out):
    total = kept[0].astype(F32) + got[0].astype(F32)
    out[...] = (total * weight[:, :, :1]).astype(BF16)


def reply_of(kept, got, weight):
    return pl.pallas_call(
        reply_kernel,
        in_specs=[VMEM] * 3,
        out_specs=VMEM,
        out_shape=jax.ShapeDtypeStruct(kept.shape[1:], BF16),
        compiler_params=params(24),
        name="reply",
    )(kept, got, weight)


def prefix_by_doubling(states, decay, me, n):
    decay_before, steps = jnp.ones_like(decay), []
    bits = bits_of(n)
    for bit in bits:
        upper = (me & bit) != 0
        partner_decay = swap(decay, "ctx", n, bit)
        steps.append((upper, decay_before, decay, partner_decay))
        decay_before = jnp.where(upper, decay_before * partner_decay, decay_before)
        decay = decay * partner_decay
    incoming = []
    for half, total in enumerate(states):
        before = jnp.zeros((), F32)
        for bit, (upper, d_before, d_total, d_partner) in zip(bits, steps):
            last = bit == bits[-1]
            partner = swap(total, "ctx", n, bit, lambda i: not last or not i & bit).astype(F32)
            before = before + jnp.where(upper, d_before[half], 0.0) * partner
            if not last:
                total = (
                    jnp.where(upper, 1.0, d_partner[half]) * total.astype(F32)
                    + jnp.where(upper, d_total[half], 1.0) * partner
                ).astype(BF16)
        incoming.append(before.astype(BF16))
    return incoming


def prefix_of_four(states, decay, me, beside_first, beside_last):
    high, low = (me & 2) != 0, (me & 1) != 0
    near = swap(decay, "ctx", 4, 1)
    far = swap(decay, "ctx", 4, 3)
    one, two = states
    first = beside_first(one)
    got_one = after(swap(one, "ctx", 4, 1, lambda i: i != 3), *first).astype(F32)
    got_two = swap(two, "ctx", 4, 2, lambda i: i < 2).astype(F32)
    sent_one = jnp.where(low, 1.0, near[0]) * one.astype(F32) + jnp.where(low, decay[0], 1.0) * got_one
    sent_two = (
        jnp.where(high & low, 0.0, 1.0) * two.astype(F32)
        + jnp.where(high, jnp.where(low, 1.0, far[1] * decay[1]), 0.0) * got_two
    )
    sent_one, sent_two = sent_one.astype(BF16), sent_two.astype(BF16)
    last = beside_last(sent_two)
    last_one = after(swap(sent_one, "ctx", 4, 2, lambda i: i < 2), *last).astype(F32)
    last_two = swap(sent_two, "ctx", 4, 1, lambda i: i != 1).astype(F32)
    return [
        (jnp.where(low, 1.0, 0.0) * got_one + jnp.where(low, near[0], 1.0) * last_one).astype(BF16),
        (jnp.where(low, near[1], far[1]) * got_two + last_two).astype(BF16),
    ]


def body(n_ctx, n_exp, queries, keys, values, log_decay, norm_gain, router, expert_up, expert_down, expert_ids):
    requests, length, features = queries.shape
    heads = log_decay.shape[2]
    dim = features // heads
    experts = router.shape[1]
    own = expert_up.shape[0]
    tokens = requests * length
    halves = 2 if requests % 2 == 0 else 1
    pairs = requests * heads // halves
    chunks = n_exp // 2
    width = 2 * features
    me = lax.axis_index("ctx")
    place = jnp.stack([me, lax.axis_index("exp")]).astype(jnp.int32)
    struct = jax.ShapeDtypeStruct
    early_pieces = [("up", k) for k in range(max(chunks - 2, 0), chunks)] + [("down", chunks - 1)]
    decay_rows = jnp.transpose(log_decay, (2, 0, 1)).reshape(heads * requests, length)

    states = pl.pallas_call(
        state_kernel,
        in_specs=[ANY] * 2 + [VMEM],
        out_specs=[VMEM] * halves,
        out_shape=[struct((pairs, dim, dim), BF16)] * halves,
        scratch_shapes=[
            pltpu.VMEM(keys.shape, BF16),
            pltpu.VMEM(values.shape, BF16),
            pltpu.SemaphoreType.DMA((2, requests)),
        ],
        compiler_params=params(60),
        name="local_state",
    )(keys, values, decay_rows)
    decay = jnp.exp(jnp.sum(after(log_decay, *states), axis=1)).reshape(halves, pairs, 1, 1)
    part = {}

    def beside_first(token):
        part["inside"], _ = call_with_held(
            inside_kernel,
            [],
            chunks,
            after(place, token),
            expert_up,
            expert_down,
            [queries, keys, values, decay_rows, jnp.transpose(expert_ids, (1, 2, 0))],
            [
                struct((requests, length, features), F32),
                struct((chunks * own * CAP, tokens), BF16),
                struct((own * CAP, 128), jnp.int32),
            ],
            "inside_and_placement",
        )
        return part["inside"][:1]

    def beside_last(token):
        _, part["held"] = call_with_held(
            None, early_pieces, chunks, after(place, token), expert_up, expert_down, [], [], "early_weights"
        )
        return list(part["held"].values())

    if n_ctx == 4 and halves == 2:
        incoming = prefix_of_four(states, decay, me, beside_first, beside_last)
    else:
        incoming = prefix_by_doubling(states, decay, me, n_ctx)
        beside_first(states[0])
        beside_last(states[0])
    inside, placement, other = part["inside"]
    held = part["held"]
    (normed,), _ = call_with_held(
        output_kernel,
        [],
        chunks,
        place,
        expert_up,
        expert_down,
        [queries, inside, decay_rows, norm_gain.reshape(1, features), *incoming],
        [struct((tokens, features), BF16)],
        "normed",
    )

    outgoing = pl.pallas_call(
        dispatch_kernel,
        in_specs=[VMEM] * 3,
        out_specs=[VMEM] * chunks,
        out_shape=[struct((own, CAP, width), BF16)] * chunks,
        compiler_params=params(24),
        name="dispatch",
    )(placement, normed, swap(normed, "exp", n_exp, 1))
    arrived = [outgoing[0]] + [swap(outgoing[k], "exp", n_exp, 2 * k) for k in range(1, chunks)]
    weight = pl.pallas_call(
        gate_kernel,
        in_specs=[SMEM] + [VMEM] * (2 + chunks),
        out_specs=VMEM,
        out_shape=struct((own, CAP, 128), F32),
        compiler_params=params(24),
        name="gate",
    )(place, other, router.T, *arrived)

    bits = bits_of(n_ctx)
    orders = [bits if k % 2 == 0 else bits[::-1] for k in range(chunks)]

    routes = [route_of(order, n_ctx) for order in orders]
    gathered = [None] * chunks
    for k in range(chunks):
        have = {0: arrived[k]}
        if k == 1:
            have[0] = after(arrived[k], *[gathered[0][bit] for bit in bits])
        for bit in orders[k]:
            have.update({rel | bit: swap(a, "ctx", n_ctx, bit) for rel, a in list(have.items())})
        gathered[k] = [have[rel] for rel in range(n_ctx)]
    total, done = None, max(chunks - 2, 0)
    for k in range(done):
        (total,) = project(
            after(place, arrived[-1]), [k], chunks, gathered, expert_up, expert_down, held, total, None
        )
    hidden, *far = project(
        after(place, weight),
        list(range(done, chunks)),
        chunks,
        gathered,
        expert_up,
        expert_down,
        held,
        total,
        routes[-1],
    )

    order = list(reversed(range(chunks)))
    open_sums, returned, token = {}, [None] * chunks, hidden
    for i in range(chunks + 3):
        if i < chunks:
            k = order[i]
            sent, kept = far
            if i:
                sent, kept = down_chunk(
                    place, k, chunks, after(hidden, token), expert_down, routes[k]
                )
            open_sums[k] = kept, swap(sent, "ctx", n_ctx, orders[k][0])
            token = sent
        if 2 <= i < chunks + 2:
            k = order[i - 2]
            for bit in orders[k][1:]:
                kept, got = open_sums[k]
                kept, sent = halve(kept, after(got, token))
                open_sums[k] = kept, swap(sent, "ctx", n_ctx, bit)
                token = sent
        if i >= 3:
            k = order[i - 3]
            kept, got = open_sums[k]
            early = [returned[order[i - 5]]] if i >= 5 else []
            token = reply_of(kept, after(got, token, *early), weight)
            returned[k] = swap(token, "exp", n_exp, 2 * k) if k else token

    mine, theirs = pl.pallas_call(
        combine_kernel,
        in_specs=[VMEM] * (2 + chunks),
        out_specs=[VMEM] * 2,
        out_shape=[struct((tokens, features), F32), struct((tokens, features), BF16)],
        compiler_params=params(24),
        name="combine",
    )(normed, placement, *returned)
    out = mine + swap(theirs, "exp", n_exp, 1).astype(F32)
    return out.astype(BF16).reshape(requests, length, features)


def solution(mesh):
    in_specs = (
        P(None, "ctx", "exp"),
        P(None, "ctx", "exp"),
        P(None, "ctx", "exp"),
        P(None, "ctx", "exp"),
        P("exp"),
        P(),
        P("exp", None, "ctx"),
        P("exp", "ctx", None),
        P("ctx", None, None),
    )
    out_specs = P(None, "ctx", "exp")
    run = functools.partial(body, mesh.shape["ctx"], mesh.shape["exp"])
    return jax.shard_map(run, mesh=mesh, in_specs=in_specs, out_specs=out_specs, check_vma=False)
```

```python
import functools

import jax
import jax.numpy as jnp
from jax import lax
from jax.experimental import pallas as pl
from jax.experimental.pallas import tpu as pltpu
from jax.sharding import PartitionSpec as P

CAP = 40
F32 = jnp.float32
BF16 = jnp.bfloat16
VMEM = pl.BlockSpec(memory_space=pltpu.VMEM)
SMEM = pl.BlockSpec(memory_space=pltpu.SMEM)
ANY = pl.BlockSpec(memory_space=pl.ANY)


def params(mib):
    return pltpu.CompilerParams(vmem_limit_bytes=mib << 20)


def bits_of(n):
    return [1 << b for b in range(n.bit_length() - 1)]


def swap(x, axis, n, k, keep=lambda i: True):
    return lax.ppermute(x, axis, [(i, i ^ k) for i in range(n) if keep(i)])


def dot(a, b, ca=1, cb=0, **kw):
    return lax.dot_general(a, b, (((ca,), (cb,)), ((), ())), preferred_element_type=F32, **kw)


def iota(shape, dim):
    return lax.broadcasted_iota(jnp.int32, shape, dim)


def running_sum(log_decay):
    length = log_decay.shape[1]
    tril = (iota((length, length), 0) >= iota((length, length), 1)).astype(F32)
    return dot(tril, log_decay, 1, 1, precision=lax.Precision.HIGHEST)


def running_sum_rows(log_decay):
    length = log_decay.shape[1]
    triu = (iota((length, length), 0) <= iota((length, length), 1)).astype(F32)
    return dot(log_decay, triu, precision=lax.Precision.HIGHEST)


def piece_copies(weights, kind, expert, chunk, owner, buffer, sems):
    copies = []
    for side in range(2):
        rows, cols = buffer.shape[1:]
        tiles = sems.shape[1]
        depth = rows // tiles
        first = (owner ^ (2 * chunk + side)) * (rows if kind == "up" else cols)
        for t in range(tiles):
            if kind == "up":
                source = weights.at[expert, pl.ds(pl.multiple_of(first + t * depth, depth), depth), :]
            else:
                source = weights.at[
                    expert, t * depth : (t + 1) * depth, pl.ds(pl.multiple_of(first, cols), cols)
                ]
            copies.append(
                pltpu.make_async_copy(
                    source, buffer.at[side, t * depth : (t + 1) * depth], sems.at[side, t]
                )
            )
    return copies


def piece_shape(kind, weights, chunks):
    rows, cols = weights.shape[1:]
    return (2, rows // (2 * chunks), cols) if kind == "up" else (2, rows, cols // (2 * chunks))


def with_held(kernel, pieces, place, up, down, *refs):
    sems, refs = refs[-1], refs[:-1]
    outs = refs[len(refs) - len(pieces) :] if pieces else ()
    copies = []
    for i, (kind, chunk) in enumerate(pieces):
        source = up if kind == "up" else down
        copies += piece_copies(source, kind, 0, chunk, place[1], outs[i], sems.at[i])
    for copy in copies:
        copy.start()
    if kernel is not None:
        kernel(place, *refs[: len(refs) - len(pieces)])
    for copy in copies:
        copy.wait()


def call_with_held(kernel, pieces, chunks, place, up, down, args, out_shape, name):
    shapes = [
        jax.ShapeDtypeStruct(piece_shape(kind, up if kind == "up" else down, chunks), BF16)
        for kind, _ in pieces
    ]
    outs = pl.pallas_call(
        functools.partial(with_held, kernel, pieces),
        in_specs=[SMEM, ANY, ANY] + [VMEM] * len(args),
        out_specs=[VMEM] * (len(out_shape) + len(shapes)),
        out_shape=list(out_shape) + shapes,
        scratch_shapes=[pltpu.SemaphoreType.DMA((max(len(pieces), 1), 2, 2))],
        compiler_params=params(24),
        name=name,
    )(place, up, down, *args)
    return outs[: len(out_shape)], dict(zip(pieces, outs[len(out_shape) :]))


def state_kernel(keys, values, log_decay, *refs):
    states, (key_buf, value_buf, sems) = refs[:-3], refs[-3:]
    requests, length, features = keys.shape
    heads = log_decay.shape[0] // requests
    dim = features // heads
    per = requests // len(states)
    copies = []
    for r in range(requests):
        pair = (
            pltpu.make_async_copy(keys.at[r], key_buf.at[r], sems.at[0, r]),
            pltpu.make_async_copy(values.at[r], value_buf.at[r], sems.at[1, r]),
        )
        for copy in pair:
            copy.start()
        copies.append(pair)
    cum = running_sum(log_decay[...])
    fade = jnp.exp(cum[length - 1 : length, :] - cum)
    for r in range(requests):
        for copy in copies[r]:
            copy.wait()
        for h in range(heads):
            lanes = slice(h * dim, (h + 1) * dim)
            at = h * requests + r
            faded = (key_buf[r, :, lanes].astype(F32) * fade[:, at : at + 1]).astype(BF16)
            states[r // per][(r % per) * heads + h] = dot(
                faded, value_buf[r, :, lanes], 0, 0
            ).astype(BF16)


def inside_kernel(place, queries, keys, values, log_decay, ids, inside, placement, other, *scratch):
    sources, buffers, sems = (queries, keys, values), scratch[:3], scratch[3]
    requests, length, features = keys.shape
    heads = log_decay.shape[0] // requests
    dim = features // heads
    copies = []
    for r in range(requests):
        mine = [
            pltpu.make_async_copy(source.at[r], buffer.at[r], sems.at[i, r])
            for i, (source, buffer) in enumerate(zip(sources, buffers))
        ]
        for copy in mine:
            copy.start()
        copies.append(mine)
    place_tokens(place, ids, placement, other, requests, length)
    queries, keys, values = buffers
    causal = iota((length, length), 0) >= iota((length, length), 1)
    cum = running_sum(log_decay[...])
    rows = running_sum_rows(log_decay[...])
    for r in range(requests):
        for copy in copies[r]:
            copy.wait()
        for h in range(heads):
            lanes = slice(h * dim, (h + 1) * dim)
            at = h * requests + r
            spread = cum[:, at : at + 1] - rows[at : at + 1, :]
            mask = jnp.where(causal, jnp.exp(jnp.minimum(spread, 0.0)), 0.0)
            scores = dot(queries[r, :, lanes], keys[r, :, lanes], 1, 1)
            inside[r, :, lanes] = dot((scores * mask).astype(BF16), values[r, :, lanes])


def place_tokens(place, ids, placement, other, requests, length):
    slots, tokens = placement.shape
    experts = slots // CAP
    own = other.shape[0] // CAP
    owner = place[1]
    expert_row = iota((experts, tokens), 0)
    relative = sum((expert_row >= own * k).astype(jnp.int32) for k in range(1, experts // own))
    expert = ((2 * relative) ^ owner) * own + (expert_row - relative * own)
    first = jnp.concatenate([ids[r, 0:1, :] for r in range(requests)], axis=1)
    second = jnp.concatenate([ids[r, 1:2, :] for r in range(requests)], axis=1)
    named = (first == expert) | (second == expert)
    row = iota((tokens, tokens), 0)
    col = iota((tokens, tokens), 1)

    def order(i):
        request = sum((i >= length * k).astype(jnp.int32) for k in range(1, requests))
        return (i - request * length) * requests + request

    earlier = (order(row) < order(col)).astype(BF16)
    before = dot(named.astype(BF16), earlier)
    code = jnp.where(named, before, -1.0).astype(BF16)
    slot_row = iota((slots, experts), 0)
    slot_expert = iota((slots, experts), 1)
    spread_rows = (slot_row >= slot_expert * CAP) & (slot_row < slot_expert * CAP + CAP)
    codes = dot(spread_rows.astype(BF16), code)
    row_of = iota((slots, tokens), 0)
    expert_of = ((row_of.astype(F32) + 0.5) * (1.0 / CAP)).astype(jnp.int32)
    taken = codes == (row_of - expert_of * CAP).astype(F32)
    placement[...] = taken.astype(BF16)
    both = (first + second).astype(F32)
    mine = jnp.sum(jnp.where(taken[: own * CAP], both, 0.0), axis=1, keepdims=True)
    me = owner * own + expert_of[: own * CAP, :1]
    other[...] = jnp.broadcast_to(mine.astype(jnp.int32) - me, other.shape)


def output_kernel(place, queries, inside, log_decay, gain, *refs):
    incoming, normed = refs[:-1], refs[-1]
    requests, length, features = queries.shape
    heads = log_decay.shape[0] // requests
    dim = features // heads
    per = requests // len(incoming)
    grow = jnp.exp(running_sum(log_decay[...]))
    for r in range(requests):
        for h in range(heads):
            lanes = slice(h * dim, (h + 1) * dim)
            at = h * requests + r
            carried = dot(queries[r, :, lanes], incoming[r // per][(r % per) * heads + h])
            out = inside[r, :, lanes] + grow[:, at : at + 1] * carried
            square = jnp.mean(out * out, axis=1, keepdims=True) + 1e-05
            normed[r * length : (r + 1) * length, lanes] = (
                out * lax.rsqrt(square) * gain[0:1, lanes]
            ).astype(BF16)


def dispatch_kernel(placement, *refs):
    sides, blocks = refs[:2], refs[2:]
    own, cap, width = blocks[0].shape
    for i, side in enumerate(sides):
        routed = dot(placement[...], side[...])
        lanes = slice(i * width // 2, (i + 1) * width // 2)
        for k, block in enumerate(blocks):
            for j in range(own):
                at = (k * own + j) * cap
                block[j, :, lanes] = routed[at : at + cap].astype(BF16)


def gate_kernel(place, other, router, *refs):
    blocks, weight = refs[:-1], refs[-1]
    own, cap, width = blocks[0].shape
    half = width // 2
    owner = place[1]
    experts = router.shape[0]
    for j in range(own):
        logits = jnp.zeros((cap, experts), F32)
        for k, block in enumerate(blocks):
            for side in range(2):
                at = pl.multiple_of((owner ^ (2 * k + side)) * half, half)
                logits = logits + dot(
                    block[j, :, side * half : (side + 1) * half], router[:, pl.ds(at, half)], 1, 1
                )
        col = iota((cap, experts), 1)
        mine = jnp.sum(jnp.where(col == owner * own + j, logits, 0.0), axis=1, keepdims=True)
        theirs_at = other[j * cap : (j + 1) * cap, :1]
        theirs = jnp.sum(jnp.where(col == theirs_at, logits, 0.0), axis=1, keepdims=True)
        weight[j] = jnp.broadcast_to(1.0 / (1.0 + jnp.exp(theirs - mine)), (cap, 128))


def project_kernel(place, up, down, *refs, chunks, parts, first, last, held, route):
    refs = list(refs)
    blocks = {k: [refs.pop(0) for _ in range(parts)] for k in chunks}
    ready = {piece: refs.pop(0) for piece in held}
    before = None if first else refs.pop(0)
    sems, buffers = refs.pop(), {}
    pieces = [("up", j, k) for j in range(up.shape[0]) for k in chunks]
    if last:
        pieces += [("down", j, chunks[-1]) for j in range(up.shape[0])]
    pieces = [(kind, j, k) for kind, j, k in pieces if j or (kind, k) not in ready]
    for piece in reversed(pieces):
        buffers[piece] = refs.pop()
    out, outs = refs[0], refs[1:]
    copies = {}
    for i, (kind, j, k) in enumerate(pieces):
        copies[kind, j, k] = piece_copies(
            up if kind == "up" else down, kind, j, k, place[1], buffers[kind, j, k], sems.at[i]
        )
        for copy in copies[kind, j, k]:
            copy.start()

    def weights_of(kind, j, k, side):
        if (kind, j, k) not in buffers:
            return ready[kind, k][side]
        mine = copies[kind, j, k]
        for copy in mine[side * len(mine) // 2 : (side + 1) * len(mine) // 2]:
            copy.wait()
        return buffers[kind, j, k][side]

    for j in range(up.shape[0]):
        total = None if first else before[j]
        for k in chunks:
            half = blocks[k][0].shape[2] // 2
            for side in range(2):
                lanes = slice(side * half, (side + 1) * half)
                x = jnp.concatenate([b[j, :, lanes].astype(F32) for b in blocks[k]], axis=0)
                part = dot(x.astype(BF16), weights_of("up", j, k, side))
                total = part if total is None else total + part
        out[j] = (total / (1.0 + jnp.exp(-total))).astype(BF16) if last else total
    if last:
        for j in range(up.shape[0]):
            for side in range(2):
                lanes = slice(side * half, (side + 1) * half)
                result = dot(out[j], weights_of("down", j, chunks[-1], side))
                for ref, members in zip(outs, route):
                    for i, member in enumerate(members):
                        ref[i, j, :, lanes] = result[member * CAP : (member + 1) * CAP].astype(BF16)


def project(place, chunks, count, gathered, up, down, held, total, route):
    own, _, hidden = up.shape
    cap, width = gathered[chunks[0]][0].shape[1:]
    parts = len(gathered[chunks[0]])
    rows = parts * cap
    first, last = total is None, route is not None
    wanted = [("up", k) for k in chunks] + ([("down", chunks[-1])] if last else [])
    ready = [piece for piece in wanted if piece in held]
    loose = [(kind, k) for kind, k in wanted for j in range(own) if j or (kind, k) not in held]
    scratch = [
        pltpu.VMEM(piece_shape(kind, up if kind == "up" else down, count), BF16)
        for kind in ("up", "down")
        for other, _ in loose
        if other == kind
    ]
    struct = jax.ShapeDtypeStruct
    out_shape = [struct((own, rows, hidden), BF16 if last else F32)]
    if last:
        out_shape += [struct((parts // 2, own, cap, width), BF16)] * 2
    work = (len(chunks) + last) * own * width * hidden
    blocks = [block for k in chunks for block in gathered[k]]
    return pl.pallas_call(
        functools.partial(
            project_kernel,
            chunks=chunks,
            parts=parts,
            first=first,
            last=last,
            held=ready,
            route=route,
        ),
        in_specs=[SMEM, ANY, ANY] + [VMEM] * (len(blocks) + len(ready) + (not first)),
        out_specs=[VMEM] * len(out_shape),
        out_shape=out_shape,
        scratch_shapes=scratch + [pltpu.SemaphoreType.DMA((max(len(scratch), 1), 2, 2))],
        compiler_params=params(24),
        cost_estimate=pl.CostEstimate(
            flops=2 * rows * work, bytes_accessed=2 * work, transcendentals=0
        ),
        name=f"project_{chunks[0]}",
    )(
        place,
        up,
        down,
        *blocks,
        *[held[piece] for piece in ready],
        *([] if first else [total]),
    )


def down_kernel(place, weights, hidden, *refs, chunk, route):
    outs, (buffer, sems) = refs[:-2], refs[-2:]
    own = hidden.shape[0]
    half = buffer.shape[3]
    copies = []
    for j in range(own):
        mine = piece_copies(weights, "down", j, chunk, place[1], buffer.at[j], sems.at[j])
        for copy in mine:
            copy.start()
        copies.append(mine)
    for j in range(own):
        for side in range(2):
            for copy in copies[j][2 * side : 2 * side + 2]:
                copy.wait()
            result = dot(hidden[j], buffer[j, side])
            lanes = slice(side * half, (side + 1) * half)
            for out, members in zip(outs, route):
                for i, member in enumerate(members):
                    out[i, j, :, lanes] = result[member * CAP : (member + 1) * CAP].astype(BF16)


def down_chunk(place, chunk, count, hidden, weights, route):
    own, rows, depth = hidden.shape
    parts = rows // CAP
    shape = piece_shape("down", weights, count)
    width = 2 * shape[2]
    return pl.pallas_call(
        functools.partial(down_kernel, chunk=chunk, route=route),
        in_specs=[SMEM, ANY, VMEM],
        out_specs=[VMEM] * 2,
        out_shape=[jax.ShapeDtypeStruct((parts // 2, own, CAP, width), BF16)] * 2,
        scratch_shapes=[pltpu.VMEM((own, *shape), BF16), pltpu.SemaphoreType.DMA((own, 2, 2))],
        compiler_params=params(24),
        cost_estimate=pl.CostEstimate(
            flops=2 * own * rows * width * depth,
            bytes_accessed=2 * own * width * depth,
            transcendentals=0,
        ),
        name=f"down_{chunk}",
    )(place, weights, hidden)


def combine_kernel(normed, placement, *refs):
    blocks, (mine, theirs) = refs[:-2], refs[-2:]
    own = blocks[0].shape[0]
    features = normed.shape[1]
    replies = jnp.concatenate(
        [block[j].astype(F32) for block in blocks for j in range(own)], axis=0
    ).astype(BF16)
    combined = dot(placement[...], replies, 0, 0)
    mine[...] = normed[...].astype(F32) + combined[:, :features]
    theirs[...] = combined[:, features:].astype(BF16)


def after(x, *others):
    return lax.optimization_barrier((x, *others))[0]


def route_of(bits, n):
    keep = [0]
    for bit in reversed(bits[1:]):
        keep = keep + [m | bit for m in keep]
    return [m | bits[0] for m in keep], keep


def halve_kernel(kept, got, keep, send):
    half = keep.shape[0]
    total = kept[...].astype(F32) + got[...].astype(F32)
    keep[...] = total[:half]
    send[...] = total[half:].astype(BF16)


def halve(kept, got):
    shape = (kept.shape[0] // 2,) + kept.shape[1:]
    return pl.pallas_call(
        halve_kernel,
        in_specs=[VMEM] * 2,
        out_specs=[VMEM] * 2,
        out_shape=[jax.ShapeDtypeStruct(shape, F32), jax.ShapeDtypeStruct(shape, BF16)],
        compiler_params=params(24),
        name="partial_sums",
    )(kept, got)


def reply_kernel(kept, got, weight, out):
    total = kept[0].astype(F32) + got[0].astype(F32)
    out[...] = (total * weight[:, :, :1]).astype(BF16)


def reply_of(kept, got, weight):
    return pl.pallas_call(
        reply_kernel,
        in_specs=[VMEM] * 3,
        out_specs=VMEM,
        out_shape=jax.ShapeDtypeStruct(kept.shape[1:], BF16),
        compiler_params=params(24),
        name="reply",
    )(kept, got, weight)


def prefix_by_doubling(states, decay, me, n):
    decay_before, steps = jnp.ones_like(decay), []
    bits = bits_of(n)
    for bit in bits:
        upper = (me & bit) != 0
        partner_decay = swap(decay, "ctx", n, bit)
        steps.append((upper, decay_before, decay, partner_decay))
        decay_before = jnp.where(upper, decay_before * partner_decay, decay_before)
        decay = decay * partner_decay
    incoming = []
    for half, total in enumerate(states):
        before = jnp.zeros((), F32)
        for bit, (upper, d_before, d_total, d_partner) in zip(bits, steps):
            last = bit == bits[-1]
            partner = swap(total, "ctx", n, bit, lambda i: not last or not i & bit).astype(F32)
            before = before + jnp.where(upper, d_before[half], 0.0) * partner
            if not last:
                total = (
                    jnp.where(upper, 1.0, d_partner[half]) * total.astype(F32)
                    + jnp.where(upper, d_total[half], 1.0) * partner
                ).astype(BF16)
        incoming.append(before.astype(BF16))
    return incoming


def prefix_of_four(states, decay, me, beside_first, beside_last):
    high, low = (me & 2) != 0, (me & 1) != 0
    near = swap(decay, "ctx", 4, 1, lambda i: i in (1, 2))
    far = swap(decay, "ctx", 4, 3, lambda i: i == 1)
    one, two = states
    first = beside_first(one)
    got_one = after(swap(one, "ctx", 4, 1, lambda i: i != 3), *first).astype(F32)
    got_two = swap(two, "ctx", 4, 2, lambda i: i < 2).astype(F32)
    sent_one = jnp.where(low, 1.0, near[0]) * one.astype(F32) + jnp.where(low, decay[0], 1.0) * got_one
    sent_two = (
        jnp.where(high & low, 0.0, 1.0) * two.astype(F32)
        + jnp.where(high, jnp.where(low, 1.0, far[1] * decay[1]), 0.0) * got_two
    )
    sent_one, sent_two = sent_one.astype(BF16), sent_two.astype(BF16)
    last = beside_last(sent_two)
    last_one = after(swap(sent_one, "ctx", 4, 2, lambda i: i < 2), *last).astype(F32)
    last_two = swap(sent_two, "ctx", 4, 1, lambda i: i != 1).astype(F32)
    return [
        (jnp.where(low, 1.0, 0.0) * got_one + jnp.where(low, near[0], 1.0) * last_one).astype(BF16),
        (jnp.where(low, near[1], far[1]) * got_two + last_two).astype(BF16),
    ]


def body(n_ctx, n_exp, queries, keys, values, log_decay, norm_gain, router, expert_up, expert_down, expert_ids):
    requests, length, features = queries.shape
    heads = log_decay.shape[2]
    dim = features // heads
    experts = router.shape[1]
    own = expert_up.shape[0]
    tokens = requests * length
    halves = 2 if requests % 2 == 0 else 1
    pairs = requests * heads // halves
    chunks = n_exp // 2
    width = 2 * features
    me = lax.axis_index("ctx")
    place = jnp.stack([me, lax.axis_index("exp")]).astype(jnp.int32)
    struct = jax.ShapeDtypeStruct
    early_pieces = [("up", k) for k in range(max(chunks - 2, 0), chunks)] + [("down", chunks - 1)]
    decay_rows = jnp.transpose(log_decay, (2, 0, 1)).reshape(heads * requests, length)

    states = pl.pallas_call(
        state_kernel,
        in_specs=[ANY] * 2 + [VMEM],
        out_specs=[VMEM] * halves,
        out_shape=[struct((pairs, dim, dim), BF16)] * halves,
        scratch_shapes=[
            pltpu.VMEM(keys.shape, BF16),
            pltpu.VMEM(values.shape, BF16),
            pltpu.SemaphoreType.DMA((2, requests)),
        ],
        compiler_params=params(60),
        name="local_state",
    )(keys, values, decay_rows)
    decay = jnp.exp(jnp.sum(after(log_decay, *states), axis=1)).reshape(halves, pairs, 1, 1)
    part = {}

    def beside_first(token):
        part["inside"] = pl.pallas_call(
            inside_kernel,
            in_specs=[SMEM] + [ANY] * 3 + [VMEM] * 2,
            out_specs=[VMEM] * 3,
            out_shape=[
                struct((requests, length, features), F32),
                struct((chunks * own * CAP, tokens), BF16),
                struct((own * CAP, 128), jnp.int32),
            ],
            scratch_shapes=[pltpu.VMEM(keys.shape, BF16)] * 3
            + [pltpu.SemaphoreType.DMA((3, requests))],
            compiler_params=params(56),
            name="inside_and_placement",
        )(
            after(place, token),
            queries,
            keys,
            values,
            decay_rows,
            jnp.transpose(expert_ids, (1, 2, 0)),
        )
        return part["inside"][:1]

    def beside_last(token):
        _, part["held"] = call_with_held(
            None, early_pieces, chunks, after(place, token), expert_up, expert_down, [], [], "early_weights"
        )
        return list(part["held"].values())

    if n_ctx == 4 and halves == 2:
        incoming = prefix_of_four(states, decay, me, beside_first, beside_last)
    else:
        incoming = prefix_by_doubling(states, decay, me, n_ctx)
        beside_first(states[0])
        beside_last(states[0])
    inside, placement, other = part["inside"]
    held = part["held"]
    (normed,), _ = call_with_held(
        output_kernel,
        [],
        chunks,
        place,
        expert_up,
        expert_down,
        [queries, inside, decay_rows, norm_gain.reshape(1, features), *incoming],
        [struct((tokens, features), BF16)],
        "normed",
    )

    outgoing = pl.pallas_call(
        dispatch_kernel,
        in_specs=[VMEM] * 3,
        out_specs=[VMEM] * chunks,
        out_shape=[struct((own, CAP, width), BF16)] * chunks,
        compiler_params=params(24),
        name="dispatch",
    )(placement, normed, swap(normed, "exp", n_exp, 1))
    arrived = [outgoing[0]] + [swap(outgoing[k], "exp", n_exp, 2 * k) for k in range(1, chunks)]
    weight = pl.pallas_call(
        gate_kernel,
        in_specs=[SMEM] + [VMEM] * (2 + chunks),
        out_specs=VMEM,
        out_shape=struct((own, CAP, 128), F32),
        compiler_params=params(24),
        name="gate",
    )(place, other, router.T, *arrived)

    bits = bits_of(n_ctx)
    orders = [bits if k % 2 == 0 else bits[::-1] for k in range(chunks)]

    routes = [route_of(order, n_ctx) for order in orders]
    gathered = [None] * chunks
    for k in range(chunks):
        have = {0: arrived[k]}
        if k == 1:
            have[0] = after(arrived[k], *[gathered[0][bit] for bit in bits])
        for bit in orders[k]:
            have.update({rel | bit: swap(a, "ctx", n_ctx, bit) for rel, a in list(have.items())})
        gathered[k] = [have[rel] for rel in range(n_ctx)]
    total, done = None, max(chunks - 2, 0)
    for k in range(done):
        (total,) = project(
            after(place, arrived[-1]), [k], chunks, gathered, expert_up, expert_down, held, total, None
        )
    hidden, *far = project(
        after(place, weight),
        list(range(done, chunks)),
        chunks,
        gathered,
        expert_up,
        expert_down,
        held,
        total,
        routes[-1],
    )

    order = list(reversed(range(chunks)))
    open_sums, returned, token = {}, [None] * chunks, hidden
    for i in range(chunks + 3):
        if i < chunks:
            k = order[i]
            sent, kept = far
            if i:
                sent, kept = down_chunk(
                    place, k, chunks, after(hidden, token), expert_down, routes[k]
                )
            open_sums[k] = kept, swap(sent, "ctx", n_ctx, orders[k][0])
            token = sent
        if 2 <= i < chunks + 2:
            k = order[i - 2]
            for bit in orders[k][1:]:
                kept, got = open_sums[k]
                kept, sent = halve(kept, after(got, token))
                open_sums[k] = kept, swap(sent, "ctx", n_ctx, bit)
                token = sent
        if i >= 3:
            k = order[i - 3]
            kept, got = open_sums[k]
            early = [returned[m] for m in order[:-2]] if i == chunks + 2 else []
            token = reply_of(kept, after(got, token, *early), weight)
            returned[k] = swap(token, "exp", n_exp, 2 * k) if k else token

    mine, theirs = pl.pallas_call(
        combine_kernel,
        in_specs=[VMEM] * (2 + chunks),
        out_specs=[VMEM] * 2,
        out_shape=[struct((tokens, features), F32), struct((tokens, features), BF16)],
        compiler_params=params(24),
        name="combine",
    )(normed, placement, *returned)
    out = mine + swap(theirs, "exp", n_exp, 1).astype(F32)
    return out.astype(BF16).reshape(requests, length, features)


def solution(mesh):
    in_specs = (
        P(None, "ctx", "exp"),
        P(None, "ctx", "exp"),
        P(None, "ctx", "exp"),
        P(None, "ctx", "exp"),
        P("exp"),
        P(),
        P("exp", None, "ctx"),
        P("exp", "ctx", None),
        P("ctx", None, None),
    )
    out_specs = P(None, "ctx", "exp")
    run = functools.partial(body, mesh.shape["ctx"], mesh.shape["exp"])
    return jax.shard_map(run, mesh=mesh, in_specs=in_specs, out_specs=out_specs, check_vma=False)
```

```python
import functools

import jax
import jax.numpy as jnp
from jax import lax
from jax.experimental import pallas as pl
from jax.experimental.pallas import tpu as pltpu
from jax.sharding import PartitionSpec as P

CAP = 40
F32 = jnp.float32
BF16 = jnp.bfloat16
VMEM = pl.BlockSpec(memory_space=pltpu.VMEM)
SMEM = pl.BlockSpec(memory_space=pltpu.SMEM)
ANY = pl.BlockSpec(memory_space=pl.ANY)


def params(mib):
    return pltpu.CompilerParams(vmem_limit_bytes=mib << 20)


def bits_of(n):
    return [1 << b for b in range(n.bit_length() - 1)]


def swap(x, axis, n, k, keep=lambda i: True):
    return lax.ppermute(x, axis, [(i, i ^ k) for i in range(n) if keep(i)])


def dot(a, b, ca=1, cb=0, **kw):
    return lax.dot_general(a, b, (((ca,), (cb,)), ((), ())), preferred_element_type=F32, **kw)


def iota(shape, dim):
    return lax.broadcasted_iota(jnp.int32, shape, dim)


def running_sum(log_decay):
    length = log_decay.shape[1]
    tril = (iota((length, length), 0) >= iota((length, length), 1)).astype(F32)
    return dot(tril, log_decay, 1, 1, precision=lax.Precision.HIGHEST)


def running_sum_rows(log_decay):
    length = log_decay.shape[1]
    triu = (iota((length, length), 0) <= iota((length, length), 1)).astype(F32)
    return dot(log_decay, triu, precision=lax.Precision.HIGHEST)


def piece_copies(weights, kind, expert, chunk, owner, buffer, sems):
    copies = []
    for side in range(2):
        rows, cols = buffer.shape[1:]
        tiles = sems.shape[1]
        depth = rows // tiles
        first = (owner ^ (2 * chunk + side)) * (rows if kind == "up" else cols)
        for t in range(tiles):
            if kind == "up":
                source = weights.at[expert, pl.ds(pl.multiple_of(first + t * depth, depth), depth), :]
            else:
                source = weights.at[
                    expert, t * depth : (t + 1) * depth, pl.ds(pl.multiple_of(first, cols), cols)
                ]
            copies.append(
                pltpu.make_async_copy(
                    source, buffer.at[side, t * depth : (t + 1) * depth], sems.at[side, t]
                )
            )
    return copies


def piece_shape(kind, weights, chunks):
    rows, cols = weights.shape[1:]
    return (2, rows // (2 * chunks), cols) if kind == "up" else (2, rows, cols // (2 * chunks))


def with_held(kernel, pieces, place, up, down, *refs):
    sems, refs = refs[-1], refs[:-1]
    outs = refs[len(refs) - len(pieces) :] if pieces else ()
    copies = []
    for i, (kind, chunk) in enumerate(pieces):
        source = up if kind == "up" else down
        copies += piece_copies(source, kind, 0, chunk, place[1], outs[i], sems.at[i])
    for copy in copies:
        copy.start()
    if kernel is not None:
        kernel(place, *refs[: len(refs) - len(pieces)])
    for copy in copies:
        copy.wait()


def call_with_held(kernel, pieces, chunks, place, up, down, args, out_shape, name):
    shapes = [
        jax.ShapeDtypeStruct(piece_shape(kind, up if kind == "up" else down, chunks), BF16)
        for kind, _ in pieces
    ]
    outs = pl.pallas_call(
        functools.partial(with_held, kernel, pieces),
        in_specs=[SMEM, ANY, ANY] + [VMEM] * len(args),
        out_specs=[VMEM] * (len(out_shape) + len(shapes)),
        out_shape=list(out_shape) + shapes,
        scratch_shapes=[pltpu.SemaphoreType.DMA((max(len(pieces), 1), 2, 2))],
        compiler_params=params(24),
        name=name,
    )(place, up, down, *args)
    return outs[: len(out_shape)], dict(zip(pieces, outs[len(out_shape) :]))


def state_kernel(keys, values, log_decay, *refs):
    states, (key_buf, value_buf, sems) = refs[:-3], refs[-3:]
    requests, length, features = keys.shape
    heads = log_decay.shape[0] // requests
    dim = features // heads
    per = requests // len(states)
    copies = []
    for r in range(requests):
        pair = (
            pltpu.make_async_copy(keys.at[r], key_buf.at[r], sems.at[0, r]),
            pltpu.make_async_copy(values.at[r], value_buf.at[r], sems.at[1, r]),
        )
        for copy in pair:
            copy.start()
        copies.append(pair)
    cum = running_sum(log_decay[...])
    fade = jnp.exp(cum[length - 1 : length, :] - cum)
    for r in range(requests):
        for copy in copies[r]:
            copy.wait()
        for h in range(heads):
            lanes = slice(h * dim, (h + 1) * dim)
            at = h * requests + r
            faded = (key_buf[r, :, lanes].astype(F32) * fade[:, at : at + 1]).astype(BF16)
            states[r // per][(r % per) * heads + h] = dot(
                faded, value_buf[r, :, lanes], 0, 0
            ).astype(BF16)


def inside_kernel(place, queries, keys, values, log_decay, ids, inside, placement, other, *scratch):
    sources, buffers, sems = (queries, keys, values), scratch[:3], scratch[3]
    requests, length, features = keys.shape
    heads = log_decay.shape[0] // requests
    dim = features // heads
    copies = []
    for r in range(requests):
        mine = [
            pltpu.make_async_copy(source.at[r], buffer.at[r], sems.at[i, r])
            for i, (source, buffer) in enumerate(zip(sources, buffers))
        ]
        for copy in mine:
            copy.start()
        copies.append(mine)
    place_tokens(place, ids, placement, other, requests, length)
    queries, keys, values = buffers
    causal = iota((length, length), 0) >= iota((length, length), 1)
    cum = running_sum(log_decay[...])
    rows = running_sum_rows(log_decay[...])
    for r in range(requests):
        for copy in copies[r]:
            copy.wait()
        for h in range(heads):
            lanes = slice(h * dim, (h + 1) * dim)
            at = h * requests + r
            spread = cum[:, at : at + 1] - rows[at : at + 1, :]
            mask = jnp.where(causal, jnp.exp(jnp.minimum(spread, 0.0)), 0.0)
            scores = dot(queries[r, :, lanes], keys[r, :, lanes], 1, 1)
            inside[r, :, lanes] = dot((scores * mask).astype(BF16), values[r, :, lanes])


def place_tokens(place, ids, placement, other, requests, length):
    slots, tokens = placement.shape
    experts = slots // CAP
    own = other.shape[0] // CAP
    owner = place[1]
    expert_row = iota((experts, tokens), 0)
    relative = sum((expert_row >= own * k).astype(jnp.int32) for k in range(1, experts // own))
    expert = ((2 * relative) ^ owner) * own + (expert_row - relative * own)
    first = jnp.concatenate([ids[r, 0:1, :] for r in range(requests)], axis=1)
    second = jnp.concatenate([ids[r, 1:2, :] for r in range(requests)], axis=1)
    named = (first == expert) | (second == expert)
    row = iota((tokens, tokens), 0)
    col = iota((tokens, tokens), 1)

    def order(i):
        request = sum((i >= length * k).astype(jnp.int32) for k in range(1, requests))
        return (i - request * length) * requests + request

    earlier = (order(row) < order(col)).astype(BF16)
    before = dot(named.astype(BF16), earlier)
    code = jnp.where(named, before, -1.0).astype(BF16)
    slot_row = iota((slots, experts), 0)
    slot_expert = iota((slots, experts), 1)
    spread_rows = (slot_row >= slot_expert * CAP) & (slot_row < slot_expert * CAP + CAP)
    codes = dot(spread_rows.astype(BF16), code)
    row_of = iota((slots, tokens), 0)
    expert_of = ((row_of.astype(F32) + 0.5) * (1.0 / CAP)).astype(jnp.int32)
    taken = codes == (row_of - expert_of * CAP).astype(F32)
    placement[...] = taken.astype(BF16)
    both = (first + second).astype(F32)
    mine = jnp.sum(jnp.where(taken[: own * CAP], both, 0.0), axis=1, keepdims=True)
    me = owner * own + expert_of[: own * CAP, :1]
    other[...] = jnp.broadcast_to(mine.astype(jnp.int32) - me, other.shape)


def output_kernel(place, queries, inside, log_decay, gain, *refs):
    incoming, normed = refs[:-1], refs[-1]
    requests, length, features = queries.shape
    heads = log_decay.shape[0] // requests
    dim = features // heads
    per = requests // len(incoming)
    grow = jnp.exp(running_sum(log_decay[...]))
    for r in range(requests):
        for h in range(heads):
            lanes = slice(h * dim, (h + 1) * dim)
            at = h * requests + r
            carried = dot(queries[r, :, lanes], incoming[r // per][(r % per) * heads + h])
            out = inside[r, :, lanes] + grow[:, at : at + 1] * carried
            square = jnp.mean(out * out, axis=1, keepdims=True) + 1e-05
            normed[r * length : (r + 1) * length, lanes] = (
                out * lax.rsqrt(square) * gain[0:1, lanes]
            ).astype(BF16)


def dispatch_kernel(placement, *refs):
    sides, blocks = refs[:2], refs[2:]
    own, cap, width = blocks[0].shape
    for i, side in enumerate(sides):
        routed = dot(placement[...], side[...])
        lanes = slice(i * width // 2, (i + 1) * width // 2)
        for k, block in enumerate(blocks):
            for j in range(own):
                at = (k * own + j) * cap
                block[j, :, lanes] = routed[at : at + cap].astype(BF16)


def gate_kernel(place, other, router, *refs):
    blocks, weight = refs[:-1], refs[-1]
    own, cap, width = blocks[0].shape
    half = width // 2
    owner = place[1]
    experts = router.shape[0]
    for j in range(own):
        logits = jnp.zeros((cap, experts), F32)
        for k, block in enumerate(blocks):
            for side in range(2):
                at = pl.multiple_of((owner ^ (2 * k + side)) * half, half)
                logits = logits + dot(
                    block[j, :, side * half : (side + 1) * half], router[:, pl.ds(at, half)], 1, 1
                )
        col = iota((cap, experts), 1)
        mine = jnp.sum(jnp.where(col == owner * own + j, logits, 0.0), axis=1, keepdims=True)
        theirs_at = other[j * cap : (j + 1) * cap, :1]
        theirs = jnp.sum(jnp.where(col == theirs_at, logits, 0.0), axis=1, keepdims=True)
        weight[j] = jnp.broadcast_to(1.0 / (1.0 + jnp.exp(theirs - mine)), (cap, 128))


def project_kernel(place, up, down, *refs, chunks, parts, first, last, held, route):
    refs = list(refs)
    blocks = {k: [refs.pop(0) for _ in range(parts)] for k in chunks}
    ready = {piece: refs.pop(0) for piece in held}
    before = None if first else refs.pop(0)
    sems, buffers = refs.pop(), {}
    pieces = [("up", j, k) for j in range(up.shape[0]) for k in chunks]
    if last:
        pieces += [("down", j, chunks[-1]) for j in range(up.shape[0])]
    pieces = [(kind, j, k) for kind, j, k in pieces if j or (kind, k) not in ready]
    for piece in reversed(pieces):
        buffers[piece] = refs.pop()
    out, outs = refs[0], refs[1:]
    copies = {}
    for i, (kind, j, k) in enumerate(pieces):
        copies[kind, j, k] = piece_copies(
            up if kind == "up" else down, kind, j, k, place[1], buffers[kind, j, k], sems.at[i]
        )
        for copy in copies[kind, j, k]:
            copy.start()

    def weights_of(kind, j, k, side):
        if (kind, j, k) not in buffers:
            return ready[kind, k][side]
        mine = copies[kind, j, k]
        for copy in mine[side * len(mine) // 2 : (side + 1) * len(mine) // 2]:
            copy.wait()
        return buffers[kind, j, k][side]

    for j in range(up.shape[0]):
        total = None if first else before[j]
        for k in chunks:
            half = blocks[k][0].shape[2] // 2
            for side in range(2):
                lanes = slice(side * half, (side + 1) * half)
                x = jnp.concatenate([b[j, :, lanes].astype(F32) for b in blocks[k]], axis=0)
                part = dot(x.astype(BF16), weights_of("up", j, k, side))
                total = part if total is None else total + part
        out[j] = (total / (1.0 + jnp.exp(-total))).astype(BF16) if last else total
    if last:
        for j in range(up.shape[0]):
            for side in range(2):
                lanes = slice(side * half, (side + 1) * half)
                result = dot(out[j], weights_of("down", j, chunks[-1], side))
                for ref, members in zip(outs, route):
                    for i, member in enumerate(members):
                        ref[i, j, :, lanes] = result[member * CAP : (member + 1) * CAP].astype(BF16)


def project(place, chunks, count, gathered, up, down, held, total, route):
    own, _, hidden = up.shape
    cap, width = gathered[chunks[0]][0].shape[1:]
    parts = len(gathered[chunks[0]])
    rows = parts * cap
    first, last = total is None, route is not None
    wanted = [("up", k) for k in chunks] + ([("down", chunks[-1])] if last else [])
    ready = [piece for piece in wanted if piece in held]
    loose = [(kind, k) for kind, k in wanted for j in range(own) if j or (kind, k) not in held]
    scratch = [
        pltpu.VMEM(piece_shape(kind, up if kind == "up" else down, count), BF16)
        for kind in ("up", "down")
        for other, _ in loose
        if other == kind
    ]
    struct = jax.ShapeDtypeStruct
    out_shape = [struct((own, rows, hidden), BF16 if last else F32)]
    if last:
        out_shape += [struct((parts // 2, own, cap, width), BF16)] * 2
    work = (len(chunks) + last) * own * width * hidden
    blocks = [block for k in chunks for block in gathered[k]]
    return pl.pallas_call(
        functools.partial(
            project_kernel,
            chunks=chunks,
            parts=parts,
            first=first,
            last=last,
            held=ready,
            route=route,
        ),
        in_specs=[SMEM, ANY, ANY] + [VMEM] * (len(blocks) + len(ready) + (not first)),
        out_specs=[VMEM] * len(out_shape),
        out_shape=out_shape,
        scratch_shapes=scratch + [pltpu.SemaphoreType.DMA((max(len(scratch), 1), 2, 2))],
        compiler_params=params(24),
        cost_estimate=pl.CostEstimate(
            flops=2 * rows * work, bytes_accessed=2 * work, transcendentals=0
        ),
        name=f"project_{chunks[0]}",
    )(
        place,
        up,
        down,
        *blocks,
        *[held[piece] for piece in ready],
        *([] if first else [total]),
    )


def down_kernel(place, weights, hidden, *refs, chunk, route):
    outs, (buffer, sems) = refs[:-2], refs[-2:]
    own = hidden.shape[0]
    half = buffer.shape[3]
    copies = []
    for j in range(own):
        mine = piece_copies(weights, "down", j, chunk, place[1], buffer.at[j], sems.at[j])
        for copy in mine:
            copy.start()
        copies.append(mine)
    for j in range(own):
        for side in range(2):
            for copy in copies[j][2 * side : 2 * side + 2]:
                copy.wait()
            result = dot(hidden[j], buffer[j, side])
            lanes = slice(side * half, (side + 1) * half)
            for out, members in zip(outs, route):
                for i, member in enumerate(members):
                    out[i, j, :, lanes] = result[member * CAP : (member + 1) * CAP].astype(BF16)


def down_chunk(place, chunk, count, hidden, weights, route):
    own, rows, depth = hidden.shape
    parts = rows // CAP
    shape = piece_shape("down", weights, count)
    width = 2 * shape[2]
    return pl.pallas_call(
        functools.partial(down_kernel, chunk=chunk, route=route),
        in_specs=[SMEM, ANY, VMEM],
        out_specs=[VMEM] * 2,
        out_shape=[jax.ShapeDtypeStruct((parts // 2, own, CAP, width), BF16)] * 2,
        scratch_shapes=[pltpu.VMEM((own, *shape), BF16), pltpu.SemaphoreType.DMA((own, 2, 2))],
        compiler_params=params(24),
        cost_estimate=pl.CostEstimate(
            flops=2 * own * rows * width * depth,
            bytes_accessed=2 * own * width * depth,
            transcendentals=0,
        ),
        name=f"down_{chunk}",
    )(place, weights, hidden)


def combine_kernel(normed, placement, *refs):
    blocks, (mine, theirs) = refs[:-2], refs[-2:]
    own = blocks[0].shape[0]
    features = normed.shape[1]
    replies = jnp.concatenate(
        [block[j].astype(F32) for block in blocks for j in range(own)], axis=0
    ).astype(BF16)
    combined = dot(placement[...], replies, 0, 0)
    mine[...] = normed[...].astype(F32) + combined[:, :features]
    theirs[...] = combined[:, features:].astype(BF16)


def after(x, *others):
    return lax.optimization_barrier((x, *others))[0]


def route_of(bits, n):
    keep = [0]
    for bit in reversed(bits[1:]):
        keep = keep + [m | bit for m in keep]
    return [m | bits[0] for m in keep], keep


def halve_kernel(kept, got, keep, send):
    half = keep.shape[0]
    total = kept[...].astype(F32) + got[...].astype(F32)
    keep[...] = total[:half]
    send[...] = total[half:].astype(BF16)


def halve(kept, got):
    shape = (kept.shape[0] // 2,) + kept.shape[1:]
    return pl.pallas_call(
        halve_kernel,
        in_specs=[VMEM] * 2,
        out_specs=[VMEM] * 2,
        out_shape=[jax.ShapeDtypeStruct(shape, F32), jax.ShapeDtypeStruct(shape, BF16)],
        compiler_params=params(24),
        name="partial_sums",
    )(kept, got)


def reply_kernel(kept, got, weight, out):
    total = kept[0].astype(F32) + got[0].astype(F32)
    out[...] = (total * weight[:, :, :1]).astype(BF16)


def reply_of(kept, got, weight):
    return pl.pallas_call(
        reply_kernel,
        in_specs=[VMEM] * 3,
        out_specs=VMEM,
        out_shape=jax.ShapeDtypeStruct(kept.shape[1:], BF16),
        compiler_params=params(24),
        name="reply",
    )(kept, got, weight)


def prefix_by_doubling(states, decay, me, n):
    decay_before, steps = jnp.ones_like(decay), []
    bits = bits_of(n)
    for bit in bits:
        upper = (me & bit) != 0
        partner_decay = swap(decay, "ctx", n, bit)
        steps.append((upper, decay_before, decay, partner_decay))
        decay_before = jnp.where(upper, decay_before * partner_decay, decay_before)
        decay = decay * partner_decay
    incoming = []
    for half, total in enumerate(states):
        before = jnp.zeros((), F32)
        for bit, (upper, d_before, d_total, d_partner) in zip(bits, steps):
            last = bit == bits[-1]
            partner = swap(total, "ctx", n, bit, lambda i: not last or not i & bit).astype(F32)
            before = before + jnp.where(upper, d_before[half], 0.0) * partner
            if not last:
                total = (
                    jnp.where(upper, 1.0, d_partner[half]) * total.astype(F32)
                    + jnp.where(upper, d_total[half], 1.0) * partner
                ).astype(BF16)
        incoming.append(before.astype(BF16))
    return incoming


def prefix_of_four(states, decay, me, beside_first, beside_last):
    high, low = (me & 2) != 0, (me & 1) != 0
    near = swap(decay, "ctx", 4, 1)
    far = swap(decay, "ctx", 4, 3)
    one, two = states
    first = beside_first(one)
    got_one = after(swap(one, "ctx", 4, 1, lambda i: i != 3), *first).astype(F32)
    got_two = swap(two, "ctx", 4, 2, lambda i: i < 2).astype(F32)
    sent_one = jnp.where(low, 1.0, near[0]) * one.astype(F32) + jnp.where(low, decay[0], 1.0) * got_one
    sent_two = (
        jnp.where(high & low, 0.0, 1.0) * two.astype(F32)
        + jnp.where(high, jnp.where(low, 1.0, far[1] * decay[1]), 0.0) * got_two
    )
    sent_one, sent_two = sent_one.astype(BF16), sent_two.astype(BF16)
    last = beside_last(sent_two)
    last_one = after(swap(sent_one, "ctx", 4, 2, lambda i: i < 2), *last).astype(F32)
    last_two = swap(sent_two, "ctx", 4, 1, lambda i: i != 1).astype(F32)
    return [
        (jnp.where(low, 1.0, 0.0) * got_one + jnp.where(low, near[0], 1.0) * last_one).astype(BF16),
        (jnp.where(low, near[1], far[1]) * got_two + last_two).astype(BF16),
    ]


def body(n_ctx, n_exp, queries, keys, values, log_decay, norm_gain, router, expert_up, expert_down, expert_ids):
    requests, length, features = queries.shape
    heads = log_decay.shape[2]
    dim = features // heads
    experts = router.shape[1]
    own = expert_up.shape[0]
    tokens = requests * length
    halves = 2 if requests % 2 == 0 else 1
    pairs = requests * heads // halves
    chunks = n_exp // 2
    width = 2 * features
    me = lax.axis_index("ctx")
    place = jnp.stack([me, lax.axis_index("exp")]).astype(jnp.int32)
    struct = jax.ShapeDtypeStruct
    early_pieces = [("up", k) for k in ([1, 3] if chunks == 4 else range(max(chunks - 2, 0), chunks))] + [("down", chunks - 1)]
    decay_rows = jnp.transpose(log_decay, (2, 0, 1)).reshape(heads * requests, length)

    states = pl.pallas_call(
        state_kernel,
        in_specs=[ANY] * 2 + [VMEM],
        out_specs=[VMEM] * halves,
        out_shape=[struct((pairs, dim, dim), BF16)] * halves,
        scratch_shapes=[
            pltpu.VMEM(keys.shape, BF16),
            pltpu.VMEM(values.shape, BF16),
            pltpu.SemaphoreType.DMA((2, requests)),
        ],
        compiler_params=params(60),
        name="local_state",
    )(keys, values, decay_rows)
    decay = jnp.exp(jnp.sum(after(log_decay, *states), axis=1)).reshape(halves, pairs, 1, 1)
    part = {}

    def beside_first(token):
        part["inside"] = pl.pallas_call(
            inside_kernel,
            in_specs=[SMEM] + [ANY] * 3 + [VMEM] * 2,
            out_specs=[VMEM] * 3,
            out_shape=[
                struct((requests, length, features), F32),
                struct((chunks * own * CAP, tokens), BF16),
                struct((own * CAP, 128), jnp.int32),
            ],
            scratch_shapes=[pltpu.VMEM(keys.shape, BF16)] * 3
            + [pltpu.SemaphoreType.DMA((3, requests))],
            compiler_params=params(56),
            name="inside_and_placement",
        )(
            after(place, token),
            queries,
            keys,
            values,
            decay_rows,
            jnp.transpose(expert_ids, (1, 2, 0)),
        )
        return part["inside"][:1]

    def beside_last(token):
        _, part["held"] = call_with_held(
            None, early_pieces, chunks, after(place, token), expert_up, expert_down, [], [], "early_weights"
        )
        return list(part["held"].values())

    if n_ctx == 4 and halves == 2:
        incoming = prefix_of_four(states, decay, me, beside_first, beside_last)
    else:
        incoming = prefix_by_doubling(states, decay, me, n_ctx)
        beside_first(states[0])
        beside_last(states[0])
    inside, placement, other = part["inside"]
    held = part["held"]
    (normed,), _ = call_with_held(
        output_kernel,
        [],
        chunks,
        place,
        expert_up,
        expert_down,
        [queries, inside, decay_rows, norm_gain.reshape(1, features), *incoming],
        [struct((tokens, features), BF16)],
        "normed",
    )

    outgoing = pl.pallas_call(
        dispatch_kernel,
        in_specs=[VMEM] * 3,
        out_specs=[VMEM] * chunks,
        out_shape=[struct((own, CAP, width), BF16)] * chunks,
        compiler_params=params(24),
        name="dispatch",
    )(placement, normed, swap(normed, "exp", n_exp, 1))
    arrived = [outgoing[0]] + [swap(outgoing[k], "exp", n_exp, 2 * k) for k in range(1, chunks)]
    weight = pl.pallas_call(
        gate_kernel,
        in_specs=[SMEM] + [VMEM] * (2 + chunks),
        out_specs=VMEM,
        out_shape=struct((own, CAP, 128), F32),
        compiler_params=params(24),
        name="gate",
    )(place, other, router.T, *arrived)

    bits = bits_of(n_ctx)
    zs = [0, 2, 1] + list(range(3, chunks)) if chunks > 3 else list(range(chunks))
    orders = [bits if k % 2 == 0 else bits[::-1] for k in range(chunks)]

    routes = [route_of(order, n_ctx) for order in orders]
    gathered = {}
    total, done = None, max(chunks - 2, 0)

    def advance(i, *others):
        return project(
            after(place, *others), [zs[i]], chunks, gathered, expert_up, expert_down, held, total, None
        )[0]

    for i, k in enumerate(zs):
        have = {0: arrived[k]}
        if i == 1:
            have[0] = after(arrived[k], *[gathered[zs[0]][bit] for bit in bits])
        if i == 2:
            total = advance(0)
        if i >= 2 and i < 9:
            have[0] = after(arrived[k], total)
        for bit in orders[i]:
            have.update({rel | bit: swap(a, "ctx", n_ctx, bit) for rel, a in list(have.items())})
        gathered[k] = [have[rel] for rel in range(n_ctx)]
    for i in range(1 if chunks > 2 else 0, done):
        total = advance(i)
    hidden, *far = project(
        after(place, weight),
        zs[done:],
        chunks,
        gathered,
        expert_up,
        expert_down,
        held,
        total,
        routes[-1],
    )

    order = list(reversed(range(chunks)))
    open_sums, returned, token = {}, [None] * chunks, hidden
    for i in range(chunks + 3):
        if i < chunks:
            k = order[i]
            sent, kept = far
            if i:
                sent, kept = down_chunk(
                    place, k, chunks, after(hidden, token), expert_down, routes[k]
                )
            open_sums[k] = kept, swap(sent, "ctx", n_ctx, orders[k][0])
            token = sent
        if 2 <= i < chunks + 2:
            k = order[i - 2]
            for bit in orders[k][1:]:
                kept, got = open_sums[k]
                kept, sent = halve(kept, after(got, token))
                open_sums[k] = kept, swap(sent, "ctx", n_ctx, bit)
                token = sent
        if i >= 3:
            k = order[i - 3]
            kept, got = open_sums[k]
            early = [returned[m] for m in order[:-2]] if i == chunks + 2 else []
            token = reply_of(kept, after(got, token, *early), weight)
            returned[k] = swap(token, "exp", n_exp, 2 * k) if k else token

    mine, theirs = pl.pallas_call(
        combine_kernel,
        in_specs=[VMEM] * (2 + chunks),
        out_specs=[VMEM] * 2,
        out_shape=[struct((tokens, features), F32), struct((tokens, features), BF16)],
        compiler_params=params(24),
        name="combine",
    )(normed, placement, *returned)
    out = mine + swap(theirs, "exp", n_exp, 1).astype(F32)
    return out.astype(BF16).reshape(requests, length, features)


def solution(mesh):
    in_specs = (
        P(None, "ctx", "exp"),
        P(None, "ctx", "exp"),
        P(None, "ctx", "exp"),
        P(None, "ctx", "exp"),
        P("exp"),
        P(),
        P("exp", None, "ctx"),
        P("exp", "ctx", None),
        P("ctx", None, None),
    )
    out_specs = P(None, "ctx", "exp")
    run = functools.partial(body, mesh.shape["ctx"], mesh.shape["exp"])
    return jax.shard_map(run, mesh=mesh, in_specs=in_specs, out_specs=out_specs, check_vma=False)
```

```python
import functools

import jax
import jax.numpy as jnp
from jax import lax
from jax.experimental import pallas as pl
from jax.experimental.pallas import tpu as pltpu
from jax.sharding import PartitionSpec as P

CAP = 40
F32 = jnp.float32
BF16 = jnp.bfloat16
VMEM = pl.BlockSpec(memory_space=pltpu.VMEM)
SMEM = pl.BlockSpec(memory_space=pltpu.SMEM)
ANY = pl.BlockSpec(memory_space=pl.ANY)


def params(mib):
    return pltpu.CompilerParams(vmem_limit_bytes=mib << 20)


def bits_of(n):
    return [1 << b for b in range(n.bit_length() - 1)]


def swap(x, axis, n, k, keep=lambda i: True):
    return lax.ppermute(x, axis, [(i, i ^ k) for i in range(n) if keep(i)])


def dot(a, b, ca=1, cb=0, **kw):
    return lax.dot_general(a, b, (((ca,), (cb,)), ((), ())), preferred_element_type=F32, **kw)


def iota(shape, dim):
    return lax.broadcasted_iota(jnp.int32, shape, dim)


def running_sum(log_decay):
    length = log_decay.shape[1]
    tril = (iota((length, length), 0) >= iota((length, length), 1)).astype(F32)
    return dot(tril, log_decay, 1, 1, precision=lax.Precision.HIGHEST)


def running_sum_rows(log_decay):
    length = log_decay.shape[1]
    triu = (iota((length, length), 0) <= iota((length, length), 1)).astype(F32)
    return dot(log_decay, triu, precision=lax.Precision.HIGHEST)


def piece_copies(weights, kind, expert, chunk, owner, buffer, sems):
    copies = []
    for side in range(2):
        rows, cols = buffer.shape[1:]
        tiles = sems.shape[1]
        depth = rows // tiles
        first = (owner ^ (2 * chunk + side)) * (rows if kind == "up" else cols)
        for t in range(tiles):
            if kind == "up":
                source = weights.at[expert, pl.ds(pl.multiple_of(first + t * depth, depth), depth), :]
            else:
                source = weights.at[
                    expert, t * depth : (t + 1) * depth, pl.ds(pl.multiple_of(first, cols), cols)
                ]
            copies.append(
                pltpu.make_async_copy(
                    source, buffer.at[side, t * depth : (t + 1) * depth], sems.at[side, t]
                )
            )
    return copies


def piece_shape(kind, weights, chunks):
    rows, cols = weights.shape[1:]
    return (2, rows // (2 * chunks), cols) if kind == "up" else (2, rows, cols // (2 * chunks))


def with_held(kernel, pieces, place, up, down, *refs):
    sems, refs = refs[-1], refs[:-1]
    outs = refs[len(refs) - len(pieces) :] if pieces else ()
    copies = []
    for i, (kind, chunk) in enumerate(pieces):
        source = up if kind == "up" else down
        copies += piece_copies(source, kind, 0, chunk, place[1], outs[i], sems.at[i])
    for copy in copies:
        copy.start()
    if kernel is not None:
        kernel(place, *refs[: len(refs) - len(pieces)])
    for copy in copies:
        copy.wait()


def call_with_held(kernel, pieces, chunks, place, up, down, args, out_shape, name):
    shapes = [
        jax.ShapeDtypeStruct(piece_shape(kind, up if kind == "up" else down, chunks), BF16)
        for kind, _ in pieces
    ]
    outs = pl.pallas_call(
        functools.partial(with_held, kernel, pieces),
        in_specs=[SMEM, ANY, ANY] + [VMEM] * len(args),
        out_specs=[VMEM] * (len(out_shape) + len(shapes)),
        out_shape=list(out_shape) + shapes,
        scratch_shapes=[pltpu.SemaphoreType.DMA((max(len(pieces), 1), 2, 2))],
        compiler_params=params(24),
        name=name,
    )(place, up, down, *args)
    return outs[: len(out_shape)], dict(zip(pieces, outs[len(out_shape) :]))


def state_kernel(keys, values, log_decay, *refs):
    states, (key_buf, value_buf, sems) = refs[:-3], refs[-3:]
    requests, length, features = keys.shape
    heads = log_decay.shape[0] // requests
    dim = features // heads
    per = requests // len(states)
    copies = []
    for r in range(requests):
        pair = (
            pltpu.make_async_copy(keys.at[r], key_buf.at[r], sems.at[0, r]),
            pltpu.make_async_copy(values.at[r], value_buf.at[r], sems.at[1, r]),
        )
        for copy in pair:
            copy.start()
        copies.append(pair)
    cum = running_sum(log_decay[...])
    fade = jnp.exp(cum[length - 1 : length, :] - cum)
    for r in range(requests):
        for copy in copies[r]:
            copy.wait()
        for h in range(heads):
            lanes = slice(h * dim, (h + 1) * dim)
            at = h * requests + r
            faded = (key_buf[r, :, lanes].astype(F32) * fade[:, at : at + 1]).astype(BF16)
            states[r // per][(r % per) * heads + h] = dot(
                faded, value_buf[r, :, lanes], 0, 0
            ).astype(BF16)


def inside_kernel(place, queries, keys, values, log_decay, ids, inside, placement, other):
    requests, length, features = keys.shape
    heads = log_decay.shape[0] // requests
    dim = features // heads
    causal = iota((length, length), 0) >= iota((length, length), 1)
    cum = running_sum(log_decay[...])
    rows = running_sum_rows(log_decay[...])
    for r in range(requests):
        for h in range(heads):
            lanes = slice(h * dim, (h + 1) * dim)
            at = h * requests + r
            spread = cum[:, at : at + 1] - rows[at : at + 1, :]
            mask = jnp.where(causal, jnp.exp(jnp.minimum(spread, 0.0)), 0.0)
            scores = dot(queries[r, :, lanes], keys[r, :, lanes], 1, 1)
            inside[r, :, lanes] = dot((scores * mask).astype(BF16), values[r, :, lanes])
    slots, tokens = placement.shape
    experts = slots // CAP
    own = other.shape[0] // CAP
    owner = place[1]
    expert_row = iota((experts, tokens), 0)
    relative = sum((expert_row >= own * k).astype(jnp.int32) for k in range(1, experts // own))
    expert = ((2 * relative) ^ owner) * own + (expert_row - relative * own)
    first = jnp.concatenate([ids[r, 0:1, :] for r in range(requests)], axis=1)
    second = jnp.concatenate([ids[r, 1:2, :] for r in range(requests)], axis=1)
    named = (first == expert) | (second == expert)
    row = iota((tokens, tokens), 0)
    col = iota((tokens, tokens), 1)

    def order(i):
        request = sum((i >= length * k).astype(jnp.int32) for k in range(1, requests))
        return (i - request * length) * requests + request

    earlier = (order(row) < order(col)).astype(BF16)
    before = dot(named.astype(BF16), earlier)
    code = jnp.where(named, before, -1.0).astype(BF16)
    slot_row = iota((slots, experts), 0)
    slot_expert = iota((slots, experts), 1)
    spread_rows = (slot_row >= slot_expert * CAP) & (slot_row < slot_expert * CAP + CAP)
    codes = dot(spread_rows.astype(BF16), code)
    row_of = iota((slots, tokens), 0)
    expert_of = ((row_of.astype(F32) + 0.5) * (1.0 / CAP)).astype(jnp.int32)
    taken = codes == (row_of - expert_of * CAP).astype(F32)
    placement[...] = taken.astype(BF16)
    both = (first + second).astype(F32)
    mine = jnp.sum(jnp.where(taken[: own * CAP], both, 0.0), axis=1, keepdims=True)
    me = owner * own + expert_of[: own * CAP, :1]
    other[...] = jnp.broadcast_to(mine.astype(jnp.int32) - me, other.shape)


def output_kernel(place, queries, inside, log_decay, gain, *refs):
    incoming, normed = refs[:-1], refs[-1]
    requests, length, features = queries.shape
    heads = log_decay.shape[0] // requests
    dim = features // heads
    per = requests // len(incoming)
    grow = jnp.exp(running_sum(log_decay[...]))
    for r in range(requests):
        for h in range(heads):
            lanes = slice(h * dim, (h + 1) * dim)
            at = h * requests + r
            carried = dot(queries[r, :, lanes], incoming[r // per][(r % per) * heads + h])
            out = inside[r, :, lanes] + grow[:, at : at + 1] * carried
            square = jnp.mean(out * out, axis=1, keepdims=True) + 1e-05
            normed[r * length : (r + 1) * length, lanes] = (
                out * lax.rsqrt(square) * gain[0:1, lanes]
            ).astype(BF16)


def dispatch_kernel(placement, *refs):
    sides, blocks = refs[:2], refs[2:]
    own, cap, width = blocks[0].shape
    for i, side in enumerate(sides):
        routed = dot(placement[...], side[...])
        lanes = slice(i * width // 2, (i + 1) * width // 2)
        for k, block in enumerate(blocks):
            for j in range(own):
                at = (k * own + j) * cap
                block[j, :, lanes] = routed[at : at + cap].astype(BF16)


def gate_kernel(place, other, router, *refs):
    blocks, weight = refs[:-1], refs[-1]
    own, cap, width = blocks[0].shape
    half = width // 2
    owner = place[1]
    experts = router.shape[0]
    for j in range(own):
        logits = jnp.zeros((cap, experts), F32)
        for k, block in enumerate(blocks):
            for side in range(2):
                at = pl.multiple_of((owner ^ (2 * k + side)) * half, half)
                logits = logits + dot(
                    block[j, :, side * half : (side + 1) * half], router[:, pl.ds(at, half)], 1, 1
                )
        col = iota((cap, experts), 1)
        mine = jnp.sum(jnp.where(col == owner * own + j, logits, 0.0), axis=1, keepdims=True)
        theirs_at = other[j * cap : (j + 1) * cap, :1]
        theirs = jnp.sum(jnp.where(col == theirs_at, logits, 0.0), axis=1, keepdims=True)
        weight[j] = jnp.broadcast_to(1.0 / (1.0 + jnp.exp(theirs - mine)), (cap, 128))


def project_kernel(place, up, down, *refs, chunks, parts, first, last, held, route):
    refs = list(refs)
    blocks = {k: [refs.pop(0) for _ in range(parts)] for k in chunks}
    ready = {piece: refs.pop(0) for piece in held}
    before = None if first else refs.pop(0)
    sems, buffers = refs.pop(), {}
    pieces = [("up", j, k) for j in range(up.shape[0]) for k in chunks]
    if last:
        pieces += [("down", j, chunks[-1]) for j in range(up.shape[0])]
    pieces = [(kind, j, k) for kind, j, k in pieces if j or (kind, k) not in ready]
    for piece in reversed(pieces):
        buffers[piece] = refs.pop()
    out, outs = refs[0], refs[1:]
    copies = {}
    for i, (kind, j, k) in enumerate(pieces):
        copies[kind, j, k] = piece_copies(
            up if kind == "up" else down, kind, j, k, place[1], buffers[kind, j, k], sems.at[i]
        )
        for copy in copies[kind, j, k]:
            copy.start()

    def weights_of(kind, j, k, side):
        if (kind, j, k) not in buffers:
            return ready[kind, k][side]
        mine = copies[kind, j, k]
        for copy in mine[side * len(mine) // 2 : (side + 1) * len(mine) // 2]:
            copy.wait()
        return buffers[kind, j, k][side]

    for j in range(up.shape[0]):
        total = None if first else before[j]
        for k in chunks:
            half = blocks[k][0].shape[2] // 2
            for side in range(2):
                lanes = slice(side * half, (side + 1) * half)
                x = jnp.concatenate([b[j, :, lanes].astype(F32) for b in blocks[k]], axis=0)
                part = dot(x.astype(BF16), weights_of("up", j, k, side))
                total = part if total is None else total + part
        out[j] = (total / (1.0 + jnp.exp(-total))).astype(BF16) if last else total
    if last:
        for j in range(up.shape[0]):
            for side in range(2):
                lanes = slice(side * half, (side + 1) * half)
                result = dot(out[j], weights_of("down", j, chunks[-1], side))
                for ref, members in zip(outs, route):
                    for i, member in enumerate(members):
                        ref[i, j, :, lanes] = result[member * CAP : (member + 1) * CAP].astype(BF16)


def project(place, chunks, count, gathered, up, down, held, total, route):
    own, _, hidden = up.shape
    cap, width = gathered[chunks[0]][0].shape[1:]
    parts = len(gathered[chunks[0]])
    rows = parts * cap
    first, last = total is None, route is not None
    wanted = [("up", k) for k in chunks] + ([("down", chunks[-1])] if last else [])
    ready = [piece for piece in wanted if piece in held]
    loose = [(kind, k) for kind, k in wanted for j in range(own) if j or (kind, k) not in held]
    scratch = [
        pltpu.VMEM(piece_shape(kind, up if kind == "up" else down, count), BF16)
        for kind in ("up", "down")
        for other, _ in loose
        if other == kind
    ]
    struct = jax.ShapeDtypeStruct
    out_shape = [struct((own, rows, hidden), BF16 if last else F32)]
    if last:
        out_shape += [struct((parts // 2, own, cap, width), BF16)] * 2
    work = (len(chunks) + last) * own * width * hidden
    blocks = [block for k in chunks for block in gathered[k]]
    return pl.pallas_call(
        functools.partial(
            project_kernel,
            chunks=chunks,
            parts=parts,
            first=first,
            last=last,
            held=ready,
            route=route,
        ),
        in_specs=[SMEM, ANY, ANY] + [VMEM] * (len(blocks) + len(ready) + (not first)),
        out_specs=[VMEM] * len(out_shape),
        out_shape=out_shape,
        scratch_shapes=scratch + [pltpu.SemaphoreType.DMA((max(len(scratch), 1), 2, 2))],
        compiler_params=params(24),
        cost_estimate=pl.CostEstimate(
            flops=2 * rows * work, bytes_accessed=2 * work, transcendentals=0
        ),
        name=f"project_{chunks[0]}",
    )(
        place,
        up,
        down,
        *blocks,
        *[held[piece] for piece in ready],
        *([] if first else [total]),
    )


def down_kernel(place, weights, hidden, *refs, chunk, shares):
    outs, (buffer, sems) = refs[:-2], refs[-2:]
    own = hidden.shape[0]
    half = buffer.shape[3]
    copies = []
    for j in range(own):
        mine = piece_copies(weights, "down", j, chunk, place[1], buffer.at[j], sems.at[j])
        for copy in mine:
            copy.start()
        copies.append(mine)
    for j in range(own):
        (share,) = [i for i, (first, last, _) in enumerate(shares) if first <= j < last]
        first, _, route = shares[share]
        for side in range(2):
            for copy in copies[j][2 * side : 2 * side + 2]:
                copy.wait()
            result = dot(hidden[j], buffer[j, side])
            lanes = slice(side * half, (side + 1) * half)
            for out, members in zip(outs[2 * share : 2 * share + 2], route):
                for i, member in enumerate(members):
                    out[i, j - first, :, lanes] = result[member * CAP : (member + 1) * CAP].astype(BF16)


def down_chunk(place, chunk, count, hidden, weights, shares):
    own, rows, depth = hidden.shape
    parts = rows // CAP
    shape = piece_shape("down", weights, count)
    width = 2 * shape[2]
    outs = pl.pallas_call(
        functools.partial(down_kernel, chunk=chunk, shares=shares),
        in_specs=[SMEM, ANY, VMEM],
        out_specs=[VMEM] * (2 * len(shares)),
        out_shape=[
            jax.ShapeDtypeStruct((parts // 2, last - first, CAP, width), BF16)
            for first, last, _ in shares
            for _ in range(2)
        ],
        scratch_shapes=[pltpu.VMEM((own, *shape), BF16), pltpu.SemaphoreType.DMA((own, 2, 2))],
        compiler_params=params(24),
        cost_estimate=pl.CostEstimate(
            flops=2 * own * rows * width * depth,
            bytes_accessed=2 * own * width * depth,
            transcendentals=0,
        ),
        name=f"down_{chunk}",
    )(place, weights, hidden)
    return [tuple(outs[2 * i : 2 * i + 2]) for i in range(len(shares))]


def combine_kernel(normed, placement, *refs):
    blocks, (mine, theirs) = refs[:-2], refs[-2:]
    features = normed.shape[1]
    replies = jnp.concatenate(
        [block[j].astype(F32) for block in blocks for j in range(block.shape[0])], axis=0
    ).astype(BF16)
    combined = dot(placement[...], replies, 0, 0)
    mine[...] = normed[...].astype(F32) + combined[:, :features]
    theirs[...] = combined[:, features:].astype(BF16)


def after(x, *others):
    return lax.optimization_barrier((x, *others))[0]


def route_of(bits, n):
    keep = [0]
    for bit in reversed(bits[1:]):
        keep = keep + [m | bit for m in keep]
    return [m | bits[0] for m in keep], keep


def halve_kernel(kept, got, keep, send):
    half = keep.shape[0]
    total = kept[...].astype(F32) + got[...].astype(F32)
    keep[...] = total[:half]
    send[...] = total[half:].astype(BF16)


def halve(kept, got):
    shape = (kept.shape[0] // 2,) + kept.shape[1:]
    return pl.pallas_call(
        halve_kernel,
        in_specs=[VMEM] * 2,
        out_specs=[VMEM] * 2,
        out_shape=[jax.ShapeDtypeStruct(shape, F32), jax.ShapeDtypeStruct(shape, BF16)],
        compiler_params=params(24),
        name="partial_sums",
    )(kept, got)


def reply_kernel(kept, got, weight, out, *, first):
    total = kept[0].astype(F32) + got[0].astype(F32)
    out[...] = (total * weight[first : first + out.shape[0], :, :1]).astype(BF16)


def reply_of(kept, got, weight, first):
    return pl.pallas_call(
        functools.partial(reply_kernel, first=first),
        in_specs=[VMEM] * 3,
        out_specs=VMEM,
        out_shape=jax.ShapeDtypeStruct(kept.shape[1:], BF16),
        compiler_params=params(24),
        name="reply",
    )(kept, got, weight)


def prefix_by_doubling(states, decay, me, n):
    decay_before, steps = jnp.ones_like(decay), []
    bits = bits_of(n)
    for bit in bits:
        upper = (me & bit) != 0
        partner_decay = swap(decay, "ctx", n, bit)
        steps.append((upper, decay_before, decay, partner_decay))
        decay_before = jnp.where(upper, decay_before * partner_decay, decay_before)
        decay = decay * partner_decay
    incoming = []
    for half, total in enumerate(states):
        before = jnp.zeros((), F32)
        for bit, (upper, d_before, d_total, d_partner) in zip(bits, steps):
            last = bit == bits[-1]
            partner = swap(total, "ctx", n, bit, lambda i: not last or not i & bit).astype(F32)
            before = before + jnp.where(upper, d_before[half], 0.0) * partner
            if not last:
                total = (
                    jnp.where(upper, 1.0, d_partner[half]) * total.astype(F32)
                    + jnp.where(upper, d_total[half], 1.0) * partner
                ).astype(BF16)
        incoming.append(before.astype(BF16))
    return incoming


def prefix_of_four(states, decay, me, beside_first, beside_last):
    high, low = (me & 2) != 0, (me & 1) != 0
    near = swap(decay, "ctx", 4, 1)
    far = swap(decay, "ctx", 4, 3)
    one, two = states
    first = beside_first(one)
    got_one = after(swap(one, "ctx", 4, 1, lambda i: i != 3), *first).astype(F32)
    got_two = swap(two, "ctx", 4, 2, lambda i: i < 2).astype(F32)
    sent_one = jnp.where(low, 1.0, near[0]) * one.astype(F32) + jnp.where(low, decay[0], 1.0) * got_one
    sent_two = (
        jnp.where(high & low, 0.0, 1.0) * two.astype(F32)
        + jnp.where(high, jnp.where(low, 1.0, far[1] * decay[1]), 0.0) * got_two
    )
    sent_one, sent_two = sent_one.astype(BF16), sent_two.astype(BF16)
    last = beside_last(sent_two)
    last_one = after(swap(sent_one, "ctx", 4, 2, lambda i: i < 2), *last).astype(F32)
    last_two = swap(sent_two, "ctx", 4, 1, lambda i: i != 1).astype(F32)
    return [
        (jnp.where(low, 1.0, 0.0) * got_one + jnp.where(low, near[0], 1.0) * last_one).astype(BF16),
        (jnp.where(low, near[1], far[1]) * got_two + last_two).astype(BF16),
    ]


def body(n_ctx, n_exp, queries, keys, values, log_decay, norm_gain, router, expert_up, expert_down, expert_ids):
    requests, length, features = queries.shape
    heads = log_decay.shape[2]
    dim = features // heads
    experts = router.shape[1]
    own = expert_up.shape[0]
    tokens = requests * length
    halves = 2 if requests % 2 == 0 else 1
    pairs = requests * heads // halves
    chunks = n_exp // 2
    width = 2 * features
    me = lax.axis_index("ctx")
    place = jnp.stack([me, lax.axis_index("exp")]).astype(jnp.int32)
    struct = jax.ShapeDtypeStruct
    early_pieces = [("up", k) for k in range(max(chunks - 2, 0), chunks)] + [("down", chunks - 1)]
    decay_rows = jnp.transpose(log_decay, (2, 0, 1)).reshape(heads * requests, length)

    states = pl.pallas_call(
        state_kernel,
        in_specs=[ANY] * 2 + [VMEM],
        out_specs=[VMEM] * halves,
        out_shape=[struct((pairs, dim, dim), BF16)] * halves,
        scratch_shapes=[
            pltpu.VMEM(keys.shape, BF16),
            pltpu.VMEM(values.shape, BF16),
            pltpu.SemaphoreType.DMA((2, requests)),
        ],
        compiler_params=params(60),
        name="local_state",
    )(keys, values, decay_rows)
    decay = jnp.exp(jnp.sum(after(log_decay, *states), axis=1)).reshape(halves, pairs, 1, 1)
    part = {}

    def beside_first(token):
        part["inside"], _ = call_with_held(
            inside_kernel,
            [],
            chunks,
            after(place, token),
            expert_up,
            expert_down,
            [queries, keys, values, decay_rows, jnp.transpose(expert_ids, (1, 2, 0))],
            [
                struct((requests, length, features), F32),
                struct((chunks * own * CAP, tokens), BF16),
                struct((own * CAP, 128), jnp.int32),
            ],
            "inside_and_placement",
        )
        return part["inside"][:1]

    def beside_last(token):
        _, part["held"] = call_with_held(
            None, early_pieces, chunks, after(place, token), expert_up, expert_down, [], [], "early_weights"
        )
        return list(part["held"].values())

    if n_ctx == 4 and halves == 2:
        incoming = prefix_of_four(states, decay, me, beside_first, beside_last)
    else:
        incoming = prefix_by_doubling(states, decay, me, n_ctx)
        beside_first(states[0])
        beside_last(states[0])
    inside, placement, other = part["inside"]
    held = part["held"]
    (normed,), _ = call_with_held(
        output_kernel,
        [],
        chunks,
        place,
        expert_up,
        expert_down,
        [queries, inside, decay_rows, norm_gain.reshape(1, features), *incoming],
        [struct((tokens, features), BF16)],
        "normed",
    )

    outgoing = pl.pallas_call(
        dispatch_kernel,
        in_specs=[VMEM] * 3,
        out_specs=[VMEM] * chunks,
        out_shape=[struct((own, CAP, width), BF16)] * chunks,
        compiler_params=params(24),
        name="dispatch",
    )(placement, normed, swap(normed, "exp", n_exp, 1))
    arrived = [outgoing[0]] + [swap(outgoing[k], "exp", n_exp, 2 * k) for k in range(1, chunks)]
    weight = pl.pallas_call(
        gate_kernel,
        in_specs=[SMEM] + [VMEM] * (2 + chunks),
        out_specs=VMEM,
        out_shape=struct((own, CAP, 128), F32),
        compiler_params=params(24),
        name="gate",
    )(place, other, router.T, *arrived)

    bits = bits_of(n_ctx)
    orders = [bits if k % 2 == 0 else bits[::-1] for k in range(chunks)]

    routes = [route_of(order, n_ctx) for order in orders]
    gathered = [None] * chunks
    for k in range(chunks):
        have = {0: arrived[k]}
        if k == 1:
            have[0] = after(arrived[k], *[gathered[0][bit] for bit in bits])
        for bit in orders[k]:
            have.update({rel | bit: swap(a, "ctx", n_ctx, bit) for rel, a in list(have.items())})
        gathered[k] = [have[rel] for rel in range(n_ctx)]
    total, done = None, max(chunks - 2, 0)
    for k in range(done):
        (total,) = project(
            after(place, arrived[-1]),
            [k],
            chunks,
            gathered,
            expert_up,
            expert_down,
            held,
            total,
            None,
        )
    hidden, *far = project(
        after(place, weight),
        list(range(done, chunks)),
        chunks,
        gathered,
        expert_up,
        expert_down,
        held,
        total,
        routes[-1],
    )

    order = list(reversed(range(chunks)))
    open_sums, returned, token = {}, [None] * chunks, hidden
    for i in range(chunks + 3):
        if i < chunks:
            k = order[i]
            if i == chunks - 1 and i and own % 2 == 0:
                paths = [(0, own // 2, bits), (own // 2, own, bits[::-1])]
            else:
                paths = [(0, own, orders[k])]
            results = [far]
            if i:
                results = down_chunk(
                    place,
                    k,
                    chunks,
                    after(hidden, token),
                    expert_down,
                    [(first, last, route_of(path, n_ctx)) for first, last, path in paths],
                )
            open_sums[k] = [
                (first, path, kept, swap(sent, "ctx", n_ctx, path[0]))
                for (first, _, path), (sent, kept) in zip(paths, results)
            ]
            token = results[0][0]
        if 2 <= i < chunks + 2:
            k = order[i - 2]
            sums = []
            for first, path, kept, got in open_sums[k]:
                for bit in path[1:]:
                    kept, sent = halve(kept, after(got, token))
                    got, token = swap(sent, "ctx", n_ctx, bit), sent
                sums.append((first, path, kept, got))
            open_sums[k] = sums
        if i >= 3:
            k = order[i - 3]
            early = [block for m in order[:-2] for block in returned[m]] if i == chunks + 2 else []
            returned[k] = []
            for first, path, kept, got in open_sums[k]:
                token = reply_of(kept, after(got, token, *early), weight, first)
                returned[k].append(swap(token, "exp", n_exp, 2 * k) if k else token)
    returned = [block for blocks in returned for block in blocks]

    mine, theirs = pl.pallas_call(
        combine_kernel,
        in_specs=[VMEM] * (2 + len(returned)),
        out_specs=[VMEM] * 2,
        out_shape=[struct((tokens, features), F32), struct((tokens, features), BF16)],
        compiler_params=params(24),
        name="combine",
    )(normed, placement, *returned)
    out = mine + swap(theirs, "exp", n_exp, 1).astype(F32)
    return out.astype(BF16).reshape(requests, length, features)


def solution(mesh):
    in_specs = (
        P(None, "ctx", "exp"),
        P(None, "ctx", "exp"),
        P(None, "ctx", "exp"),
        P(None, "ctx", "exp"),
        P("exp"),
        P(),
        P("exp", None, "ctx"),
        P("exp", "ctx", None),
        P("ctx", None, None),
    )
    out_specs = P(None, "ctx", "exp")
    run = functools.partial(body, mesh.shape["ctx"], mesh.shape["exp"])
    return jax.shard_map(run, mesh=mesh, in_specs=in_specs, out_specs=out_specs, check_vma=False)
```

```python
import functools

import jax
import jax.numpy as jnp
from jax import lax
from jax.experimental import pallas as pl
from jax.experimental.pallas import tpu as pltpu
from jax.sharding import PartitionSpec as P

CAP = 40
F32 = jnp.float32
BF16 = jnp.bfloat16
VMEM = pl.BlockSpec(memory_space=pltpu.VMEM)
SMEM = pl.BlockSpec(memory_space=pltpu.SMEM)
ANY = pl.BlockSpec(memory_space=pl.ANY)


def params(mib):
    return pltpu.CompilerParams(vmem_limit_bytes=mib << 20)


def bits_of(n):
    return [1 << b for b in range(n.bit_length() - 1)]


def swap(x, axis, n, k, keep=lambda i: True):
    return lax.ppermute(x, axis, [(i, i ^ k) for i in range(n) if keep(i)])


def dot(a, b, ca=1, cb=0, **kw):
    return lax.dot_general(a, b, (((ca,), (cb,)), ((), ())), preferred_element_type=F32, **kw)


def iota(shape, dim):
    return lax.broadcasted_iota(jnp.int32, shape, dim)


def running_sum(log_decay):
    length = log_decay.shape[1]
    tril = (iota((length, length), 0) >= iota((length, length), 1)).astype(F32)
    return dot(tril, log_decay, 1, 1, precision=lax.Precision.HIGHEST)


def running_sum_rows(log_decay):
    length = log_decay.shape[1]
    triu = (iota((length, length), 0) <= iota((length, length), 1)).astype(F32)
    return dot(log_decay, triu, precision=lax.Precision.HIGHEST)


def piece_copies(weights, kind, expert, chunk, owner, buffer, sems):
    copies = []
    for side in range(2):
        rows, cols = buffer.shape[1:]
        tiles = sems.shape[1]
        depth = rows // tiles
        first = (owner ^ (2 * chunk + side)) * (rows if kind == "up" else cols)
        for t in range(tiles):
            if kind == "up":
                source = weights.at[expert, pl.ds(pl.multiple_of(first + t * depth, depth), depth), :]
            else:
                source = weights.at[
                    expert, t * depth : (t + 1) * depth, pl.ds(pl.multiple_of(first, cols), cols)
                ]
            copies.append(
                pltpu.make_async_copy(
                    source, buffer.at[side, t * depth : (t + 1) * depth], sems.at[side, t]
                )
            )
    return copies


def piece_shape(kind, weights, chunks):
    rows, cols = weights.shape[1:]
    return (2, rows // (2 * chunks), cols) if kind == "up" else (2, rows, cols // (2 * chunks))


def with_held(kernel, pieces, place, up, down, *refs):
    sems, refs = refs[-1], refs[:-1]
    outs = refs[len(refs) - len(pieces) :] if pieces else ()
    copies = []
    for i, (kind, chunk) in enumerate(pieces):
        source = up if kind == "up" else down
        copies += piece_copies(source, kind, 0, chunk, place[1], outs[i], sems.at[i])
    for copy in copies:
        copy.start()
    if kernel is not None:
        kernel(place, *refs[: len(refs) - len(pieces)])
    for copy in copies:
        copy.wait()


def call_with_held(kernel, pieces, chunks, place, up, down, args, out_shape, name):
    shapes = [
        jax.ShapeDtypeStruct(piece_shape(kind, up if kind == "up" else down, chunks), BF16)
        for kind, _ in pieces
    ]
    outs = pl.pallas_call(
        functools.partial(with_held, kernel, pieces),
        in_specs=[SMEM, ANY, ANY] + [VMEM] * len(args),
        out_specs=[VMEM] * (len(out_shape) + len(shapes)),
        out_shape=list(out_shape) + shapes,
        scratch_shapes=[pltpu.SemaphoreType.DMA((max(len(pieces), 1), 2, 2))],
        compiler_params=params(24),
        name=name,
    )(place, up, down, *args)
    return outs[: len(out_shape)], dict(zip(pieces, outs[len(out_shape) :]))


def state_kernel(keys, values, log_decay, *refs):
    states, (key_buf, value_buf, sems) = refs[:-3], refs[-3:]
    requests, length, features = keys.shape
    heads = log_decay.shape[0] // requests
    dim = features // heads
    per = requests // len(states)
    copies = []
    for r in range(requests):
        pair = (
            pltpu.make_async_copy(keys.at[r], key_buf.at[r], sems.at[0, r]),
            pltpu.make_async_copy(values.at[r], value_buf.at[r], sems.at[1, r]),
        )
        for copy in pair:
            copy.start()
        copies.append(pair)
    cum = running_sum(log_decay[...])
    fade = jnp.exp(cum[length - 1 : length, :] - cum)
    for r in range(requests):
        for copy in copies[r]:
            copy.wait()
        for h in range(heads):
            lanes = slice(h * dim, (h + 1) * dim)
            at = h * requests + r
            faded = (key_buf[r, :, lanes].astype(F32) * fade[:, at : at + 1]).astype(BF16)
            states[r // per][(r % per) * heads + h] = dot(
                faded, value_buf[r, :, lanes], 0, 0
            ).astype(BF16)


def inside_kernel(place, queries, keys, values, log_decay, ids, inside, placement, other):
    requests, length, features = keys.shape
    heads = log_decay.shape[0] // requests
    dim = features // heads
    causal = iota((length, length), 0) >= iota((length, length), 1)
    cum = running_sum(log_decay[...])
    rows = running_sum_rows(log_decay[...])
    for r in range(requests):
        for h in range(heads):
            lanes = slice(h * dim, (h + 1) * dim)
            at = h * requests + r
            spread = cum[:, at : at + 1] - rows[at : at + 1, :]
            mask = jnp.where(causal, jnp.exp(jnp.minimum(spread, 0.0)), 0.0)
            scores = dot(queries[r, :, lanes], keys[r, :, lanes], 1, 1)
            inside[r, :, lanes] = dot((scores * mask).astype(BF16), values[r, :, lanes])
    slots, tokens = placement.shape
    experts = slots // CAP
    own = other.shape[0] // CAP
    owner = place[1]
    expert_row = iota((experts, tokens), 0)
    relative = sum((expert_row >= own * k).astype(jnp.int32) for k in range(1, experts // own))
    expert = ((2 * relative) ^ owner) * own + (expert_row - relative * own)
    first = jnp.concatenate([ids[r, 0:1, :] for r in range(requests)], axis=1)
    second = jnp.concatenate([ids[r, 1:2, :] for r in range(requests)], axis=1)
    named = (first == expert) | (second == expert)
    row = iota((tokens, tokens), 0)
    col = iota((tokens, tokens), 1)

    def order(i):
        request = sum((i >= length * k).astype(jnp.int32) for k in range(1, requests))
        return (i - request * length) * requests + request

    earlier = (order(row) < order(col)).astype(BF16)
    before = dot(named.astype(BF16), earlier)
    code = jnp.where(named, before, -1.0).astype(BF16)
    slot_row = iota((slots, experts), 0)
    slot_expert = iota((slots, experts), 1)
    spread_rows = (slot_row >= slot_expert * CAP) & (slot_row < slot_expert * CAP + CAP)
    codes = dot(spread_rows.astype(BF16), code)
    row_of = iota((slots, tokens), 0)
    expert_of = ((row_of.astype(F32) + 0.5) * (1.0 / CAP)).astype(jnp.int32)
    taken = codes == (row_of - expert_of * CAP).astype(F32)
    placement[...] = taken.astype(BF16)
    both = (first + second).astype(F32)
    mine = jnp.sum(jnp.where(taken[: own * CAP], both, 0.0), axis=1, keepdims=True)
    me = owner * own + expert_of[: own * CAP, :1]
    other[...] = jnp.broadcast_to(mine.astype(jnp.int32) - me, other.shape)


def output_kernel(place, queries, inside, log_decay, gain, *refs):
    incoming, normed = refs[:-1], refs[-1]
    requests, length, features = queries.shape
    heads = log_decay.shape[0] // requests
    dim = features // heads
    per = requests // len(incoming)
    grow = jnp.exp(running_sum(log_decay[...]))
    for r in range(requests):
        for h in range(heads):
            lanes = slice(h * dim, (h + 1) * dim)
            at = h * requests + r
            carried = dot(queries[r, :, lanes], incoming[r // per][(r % per) * heads + h])
            out = inside[r, :, lanes] + grow[:, at : at + 1] * carried
            square = jnp.mean(out * out, axis=1, keepdims=True) + 1e-05
            normed[r * length : (r + 1) * length, lanes] = (
                out * lax.rsqrt(square) * gain[0:1, lanes]
            ).astype(BF16)


def dispatch_kernel(placement, *refs):
    sides, blocks = refs[:2], refs[2:]
    own, cap, width = blocks[0].shape
    for i, side in enumerate(sides):
        routed = dot(placement[...], side[...])
        lanes = slice(i * width // 2, (i + 1) * width // 2)
        for k, block in enumerate(blocks):
            for j in range(own):
                at = (k * own + j) * cap
                block[j, :, lanes] = routed[at : at + cap].astype(BF16)


def gate_kernel(place, other, router, *refs):
    blocks, weight = refs[:-1], refs[-1]
    own, cap, width = blocks[0].shape
    half = width // 2
    owner = place[1]
    experts = router.shape[0]
    for j in range(own):
        logits = jnp.zeros((cap, experts), F32)
        for k, block in enumerate(blocks):
            for side in range(2):
                at = pl.multiple_of((owner ^ (2 * k + side)) * half, half)
                logits = logits + dot(
                    block[j, :, side * half : (side + 1) * half], router[:, pl.ds(at, half)], 1, 1
                )
        col = iota((cap, experts), 1)
        mine = jnp.sum(jnp.where(col == owner * own + j, logits, 0.0), axis=1, keepdims=True)
        theirs_at = other[j * cap : (j + 1) * cap, :1]
        theirs = jnp.sum(jnp.where(col == theirs_at, logits, 0.0), axis=1, keepdims=True)
        weight[j] = jnp.broadcast_to(1.0 / (1.0 + jnp.exp(theirs - mine)), (cap, 128))


def project_kernel(place, up, down, *refs, chunks, parts, first, last, held, route):
    refs = list(refs)
    blocks = {k: [refs.pop(0) for _ in range(parts)] for k in chunks}
    ready = {piece: refs.pop(0) for piece in held}
    before = None if first else refs.pop(0)
    sems, buffers = refs.pop(), {}
    pieces = [("up", j, k) for j in range(up.shape[0]) for k in chunks]
    if last:
        pieces += [("down", j, chunks[-1]) for j in range(up.shape[0])]
    pieces = [(kind, j, k) for kind, j, k in pieces if j or (kind, k) not in ready]
    for piece in reversed(pieces):
        buffers[piece] = refs.pop()
    out, outs = refs[0], refs[1:]
    copies = {}
    for i, (kind, j, k) in enumerate(pieces):
        copies[kind, j, k] = piece_copies(
            up if kind == "up" else down, kind, j, k, place[1], buffers[kind, j, k], sems.at[i]
        )
        for copy in copies[kind, j, k]:
            copy.start()

    def weights_of(kind, j, k, side):
        if (kind, j, k) not in buffers:
            return ready[kind, k][side]
        mine = copies[kind, j, k]
        for copy in mine[side * len(mine) // 2 : (side + 1) * len(mine) // 2]:
            copy.wait()
        return buffers[kind, j, k][side]

    for j in range(up.shape[0]):
        total = None if first else before[j]
        for k in chunks:
            half = blocks[k][0].shape[2] // 2
            for side in range(2):
                lanes = slice(side * half, (side + 1) * half)
                x = jnp.concatenate([b[j, :, lanes].astype(F32) for b in blocks[k]], axis=0)
                part = dot(x.astype(BF16), weights_of("up", j, k, side))
                total = part if total is None else total + part
        out[j] = (total / (1.0 + jnp.exp(-total))).astype(BF16) if last else total
    if last:
        for j in range(up.shape[0]):
            for side in range(2):
                lanes = slice(side * half, (side + 1) * half)
                result = dot(out[j], weights_of("down", j, chunks[-1], side))
                for ref, members in zip(outs, route):
                    for i, member in enumerate(members):
                        ref[i, j, :, lanes] = result[member * CAP : (member + 1) * CAP].astype(BF16)


def project(place, chunks, count, gathered, up, down, held, total, route):
    own, _, hidden = up.shape
    cap, width = gathered[chunks[0]][0].shape[1:]
    parts = len(gathered[chunks[0]])
    rows = parts * cap
    first, last = total is None, route is not None
    wanted = [("up", k) for k in chunks] + ([("down", chunks[-1])] if last else [])
    ready = [piece for piece in wanted if piece in held]
    loose = [(kind, k) for kind, k in wanted for j in range(own) if j or (kind, k) not in held]
    scratch = [
        pltpu.VMEM(piece_shape(kind, up if kind == "up" else down, count), BF16)
        for kind in ("up", "down")
        for other, _ in loose
        if other == kind
    ]
    struct = jax.ShapeDtypeStruct
    out_shape = [struct((own, rows, hidden), BF16 if last else F32)]
    if last:
        out_shape += [struct((parts // 2, own, cap, width), BF16)] * 2
    work = (len(chunks) + last) * own * width * hidden
    blocks = [block for k in chunks for block in gathered[k]]
    return pl.pallas_call(
        functools.partial(
            project_kernel,
            chunks=chunks,
            parts=parts,
            first=first,
            last=last,
            held=ready,
            route=route,
        ),
        in_specs=[SMEM, ANY, ANY] + [VMEM] * (len(blocks) + len(ready) + (not first)),
        out_specs=[VMEM] * len(out_shape),
        out_shape=out_shape,
        scratch_shapes=scratch + [pltpu.SemaphoreType.DMA((max(len(scratch), 1), 2, 2))],
        compiler_params=params(24),
        cost_estimate=pl.CostEstimate(
            flops=2 * rows * work, bytes_accessed=2 * work, transcendentals=0
        ),
        name=f"project_{chunks[0]}",
    )(
        place,
        up,
        down,
        *blocks,
        *[held[piece] for piece in ready],
        *([] if first else [total]),
    )


def down_kernel(place, weights, hidden, *refs, chunk, shares):
    outs, (buffer, sems) = refs[:-2], refs[-2:]
    own = hidden.shape[0]
    half = buffer.shape[3]
    copies = []
    for j in range(own):
        mine = piece_copies(weights, "down", j, chunk, place[1], buffer.at[j], sems.at[j])
        for copy in mine:
            copy.start()
        copies.append(mine)
    for j in range(own):
        (share,) = [i for i, (first, last, _) in enumerate(shares) if first <= j < last]
        first, _, route = shares[share]
        for side in range(2):
            for copy in copies[j][2 * side : 2 * side + 2]:
                copy.wait()
            result = dot(hidden[j], buffer[j, side])
            lanes = slice(side * half, (side + 1) * half)
            for out, members in zip(outs[2 * share : 2 * share + 2], route):
                for i, member in enumerate(members):
                    out[i, j - first, :, lanes] = result[member * CAP : (member + 1) * CAP].astype(BF16)


def down_chunk(place, chunk, count, hidden, weights, shares):
    own, rows, depth = hidden.shape
    parts = rows // CAP
    shape = piece_shape("down", weights, count)
    width = 2 * shape[2]
    outs = pl.pallas_call(
        functools.partial(down_kernel, chunk=chunk, shares=shares),
        in_specs=[SMEM, ANY, VMEM],
        out_specs=[VMEM] * (2 * len(shares)),
        out_shape=[
            jax.ShapeDtypeStruct((parts // 2, last - first, CAP, width), BF16)
            for first, last, _ in shares
            for _ in range(2)
        ],
        scratch_shapes=[pltpu.VMEM((own, *shape), BF16), pltpu.SemaphoreType.DMA((own, 2, 2))],
        compiler_params=params(24),
        cost_estimate=pl.CostEstimate(
            flops=2 * own * rows * width * depth,
            bytes_accessed=2 * own * width * depth,
            transcendentals=0,
        ),
        name=f"down_{chunk}",
    )(place, weights, hidden)
    return [tuple(outs[2 * i : 2 * i + 2]) for i in range(len(shares))]


def combine_kernel(normed, placement, *refs):
    blocks, (mine, theirs) = refs[:-2], refs[-2:]
    features = normed.shape[1]
    replies = jnp.concatenate(
        [block[j].astype(F32) for block in blocks for j in range(block.shape[0])], axis=0
    ).astype(BF16)
    combined = dot(placement[...], replies, 0, 0)
    mine[...] = normed[...].astype(F32) + combined[:, :features]
    theirs[...] = combined[:, features:].astype(BF16)


def after(x, *others):
    return lax.optimization_barrier((x, *others))[0]


def route_of(bits, n):
    keep = [0]
    for bit in reversed(bits[1:]):
        keep = keep + [m | bit for m in keep]
    return [m | bits[0] for m in keep], keep


def halve_kernel(kept, got, keep, send):
    half = keep.shape[0]
    total = kept[...].astype(F32) + got[...].astype(F32)
    keep[...] = total[:half]
    send[...] = total[half:].astype(BF16)


def halve(kept, got):
    shape = (kept.shape[0] // 2,) + kept.shape[1:]
    return pl.pallas_call(
        halve_kernel,
        in_specs=[VMEM] * 2,
        out_specs=[VMEM] * 2,
        out_shape=[jax.ShapeDtypeStruct(shape, F32), jax.ShapeDtypeStruct(shape, BF16)],
        compiler_params=params(24),
        name="partial_sums",
    )(kept, got)


def reply_kernel(kept, got, weight, out, *, first):
    total = kept[0].astype(F32) + got[0].astype(F32)
    out[...] = (total * weight[first : first + out.shape[0], :, :1]).astype(BF16)


def reply_of(kept, got, weight, first):
    return pl.pallas_call(
        functools.partial(reply_kernel, first=first),
        in_specs=[VMEM] * 3,
        out_specs=VMEM,
        out_shape=jax.ShapeDtypeStruct(kept.shape[1:], BF16),
        compiler_params=params(24),
        name="reply",
    )(kept, got, weight)


def prefix_by_doubling(states, decay, me, n):
    decay_before, steps = jnp.ones_like(decay), []
    bits = bits_of(n)
    for bit in bits:
        upper = (me & bit) != 0
        partner_decay = swap(decay, "ctx", n, bit)
        steps.append((upper, decay_before, decay, partner_decay))
        decay_before = jnp.where(upper, decay_before * partner_decay, decay_before)
        decay = decay * partner_decay
    incoming = []
    for half, total in enumerate(states):
        before = jnp.zeros((), F32)
        for bit, (upper, d_before, d_total, d_partner) in zip(bits, steps):
            last = bit == bits[-1]
            partner = swap(total, "ctx", n, bit, lambda i: not last or not i & bit).astype(F32)
            before = before + jnp.where(upper, d_before[half], 0.0) * partner
            if not last:
                total = (
                    jnp.where(upper, 1.0, d_partner[half]) * total.astype(F32)
                    + jnp.where(upper, d_total[half], 1.0) * partner
                ).astype(BF16)
        incoming.append(before.astype(BF16))
    return incoming


def prefix_of_four(states, decay, me, beside_first, beside_last):
    high, low = (me & 2) != 0, (me & 1) != 0
    near = swap(decay, "ctx", 4, 1)
    far = swap(decay, "ctx", 4, 3)
    one, two = states
    first = beside_first(one)
    got_one = after(swap(one, "ctx", 4, 1, lambda i: i != 3), *first).astype(F32)
    got_two = swap(two, "ctx", 4, 2, lambda i: i < 2).astype(F32)
    sent_one = jnp.where(low, 1.0, near[0]) * one.astype(F32) + jnp.where(low, decay[0], 1.0) * got_one
    sent_two = (
        jnp.where(high & low, 0.0, 1.0) * two.astype(F32)
        + jnp.where(high, jnp.where(low, 1.0, far[1] * decay[1]), 0.0) * got_two
    )
    sent_one, sent_two = sent_one.astype(BF16), sent_two.astype(BF16)
    last = beside_last(sent_two)
    last_one = after(swap(sent_one, "ctx", 4, 2, lambda i: i < 2), *last).astype(F32)
    last_two = swap(sent_two, "ctx", 4, 1, lambda i: i != 1).astype(F32)
    return [
        (jnp.where(low, 1.0, 0.0) * got_one + jnp.where(low, near[0], 1.0) * last_one).astype(BF16),
        (jnp.where(low, near[1], far[1]) * got_two + last_two).astype(BF16),
    ]


def body(n_ctx, n_exp, queries, keys, values, log_decay, norm_gain, router, expert_up, expert_down, expert_ids):
    requests, length, features = queries.shape
    heads = log_decay.shape[2]
    dim = features // heads
    experts = router.shape[1]
    own = expert_up.shape[0]
    tokens = requests * length
    halves = 2 if requests % 2 == 0 else 1
    pairs = requests * heads // halves
    chunks = n_exp // 2
    width = 2 * features
    me = lax.axis_index("ctx")
    place = jnp.stack([me, lax.axis_index("exp")]).astype(jnp.int32)
    struct = jax.ShapeDtypeStruct
    early_pieces = [("up", k) for k in range(max(chunks - 2, 0), chunks)] + [("down", chunks - 1)]
    decay_rows = jnp.transpose(log_decay, (2, 0, 1)).reshape(heads * requests, length)

    states = pl.pallas_call(
        state_kernel,
        in_specs=[ANY] * 2 + [VMEM],
        out_specs=[VMEM] * halves,
        out_shape=[struct((pairs, dim, dim), BF16)] * halves,
        scratch_shapes=[
            pltpu.VMEM(keys.shape, BF16),
            pltpu.VMEM(values.shape, BF16),
            pltpu.SemaphoreType.DMA((2, requests)),
        ],
        compiler_params=params(60),
        name="local_state",
    )(keys, values, decay_rows)
    decay = jnp.exp(jnp.sum(after(log_decay, *states), axis=1)).reshape(halves, pairs, 1, 1)
    part = {}

    def beside_first(token):
        part["inside"], _ = call_with_held(
            inside_kernel,
            [],
            chunks,
            after(place, token),
            expert_up,
            expert_down,
            [queries, keys, values, decay_rows, jnp.transpose(expert_ids, (1, 2, 0))],
            [
                struct((requests, length, features), F32),
                struct((chunks * own * CAP, tokens), BF16),
                struct((own * CAP, 128), jnp.int32),
            ],
            "inside_and_placement",
        )
        return part["inside"][:1]

    def beside_last(token):
        _, part["held"] = call_with_held(
            None, early_pieces, chunks, after(place, token), expert_up, expert_down, [], [], "early_weights"
        )
        return list(part["held"].values())

    if n_ctx == 4 and halves == 2:
        incoming = prefix_of_four(states, decay, me, beside_first, beside_last)
    else:
        incoming = prefix_by_doubling(states, decay, me, n_ctx)
        beside_first(states[0])
        beside_last(states[0])
    inside, placement, other = part["inside"]
    held = part["held"]
    (normed,), _ = call_with_held(
        output_kernel,
        [],
        chunks,
        place,
        expert_up,
        expert_down,
        [queries, inside, decay_rows, norm_gain.reshape(1, features), *incoming],
        [struct((tokens, features), BF16)],
        "normed",
    )

    outgoing = pl.pallas_call(
        dispatch_kernel,
        in_specs=[VMEM] * 3,
        out_specs=[VMEM] * chunks,
        out_shape=[struct((own, CAP, width), BF16)] * chunks,
        compiler_params=params(24),
        name="dispatch",
    )(placement, normed, swap(normed, "exp", n_exp, 1))
    arrived = [outgoing[0]] + [swap(outgoing[k], "exp", n_exp, 2 * k) for k in range(1, chunks)]

    def gate(token):
        return pl.pallas_call(
            gate_kernel,
            in_specs=[SMEM] + [VMEM] * (2 + chunks),
            out_specs=VMEM,
            out_shape=struct((own, CAP, 128), F32),
            compiler_params=params(24),
            name="gate",
        )(after(place, token), other, router.T, *arrived)

    bits = bits_of(n_ctx)
    orders = [bits if k % 2 == 0 else bits[::-1] for k in range(chunks)]

    routes = [route_of(order, n_ctx) for order in orders]
    gathered = [None] * chunks
    for k in range(chunks):
        have = {0: arrived[k]}
        if k == 1:
            have[0] = after(arrived[k], *[gathered[0][bit] for bit in bits])
        for bit in orders[k]:
            have.update({rel | bit: swap(a, "ctx", n_ctx, bit) for rel, a in list(have.items())})
        gathered[k] = [have[rel] for rel in range(n_ctx)]
    total, done = None, max(chunks - 2, 0)
    for k in range(done):
        (total,) = project(
            after(place, arrived[-1]),
            [k],
            chunks,
            gathered,
            expert_up,
            expert_down,
            held,
            total,
            None,
        )
    hidden, *far = project(
        place,
        list(range(done, chunks)),
        chunks,
        gathered,
        expert_up,
        expert_down,
        held,
        total,
        routes[-1],
    )

    order = list(reversed(range(chunks)))
    open_sums, returned, token = {}, [None] * chunks, hidden
    for i in range(chunks + 3):
        if i < chunks:
            k = order[i]
            if i == chunks - 1 and i and own % 2 == 0:
                paths = [(0, own // 2, bits), (own // 2, own, bits[::-1])]
            else:
                paths = [(0, own, orders[k])]
            results = [far]
            if i:
                results = down_chunk(
                    place,
                    k,
                    chunks,
                    after(hidden, token),
                    expert_down,
                    [(first, last, route_of(path, n_ctx)) for first, last, path in paths],
                )
            open_sums[k] = [
                (first, path, kept, swap(sent, "ctx", n_ctx, path[0]))
                for (first, _, path), (sent, kept) in zip(paths, results)
            ]
            token = results[0][0]
            if i == min(3, chunks - 1):
                weight = gate(token)
        if 2 <= i < chunks + 2:
            k = order[i - 2]
            sums = []
            for first, path, kept, got in open_sums[k]:
                for bit in path[1:]:
                    kept, sent = halve(kept, after(got, token))
                    got, token = swap(sent, "ctx", n_ctx, bit), sent
                sums.append((first, path, kept, got))
            open_sums[k] = sums
        if i >= 3:
            k = order[i - 3]
            early = [block for m in order[:-2] for block in returned[m]] if i == chunks + 2 else []
            returned[k] = []
            for first, path, kept, got in open_sums[k]:
                token = reply_of(kept, after(got, token, *early), weight, first)
                returned[k].append(swap(token, "exp", n_exp, 2 * k) if k else token)
    returned = [block for blocks in returned for block in blocks]

    mine, theirs = pl.pallas_call(
        combine_kernel,
        in_specs=[VMEM] * (2 + len(returned)),
        out_specs=[VMEM] * 2,
        out_shape=[struct((tokens, features), F32), struct((tokens, features), BF16)],
        compiler_params=params(24),
        name="combine",
    )(normed, placement, *returned)
    out = mine + swap(theirs, "exp", n_exp, 1).astype(F32)
    return out.astype(BF16).reshape(requests, length, features)


def solution(mesh):
    in_specs = (
        P(None, "ctx", "exp"),
        P(None, "ctx", "exp"),
        P(None, "ctx", "exp"),
        P(None, "ctx", "exp"),
        P("exp"),
        P(),
        P("exp", None, "ctx"),
        P("exp", "ctx", None),
        P("ctx", None, None),
    )
    out_specs = P(None, "ctx", "exp")
    run = functools.partial(body, mesh.shape["ctx"], mesh.shape["exp"])
    return jax.shard_map(run, mesh=mesh, in_specs=in_specs, out_specs=out_specs, check_vma=False)
```
